32 devices in a mesh: gx: 2 (over x), gy: 4 (over z), gz: 4 (over y, core).
Axes of the slice: x: 2, y: 2, z: 4, core: 2. Of those that a mesh axis runs over, the one named last changes fastest.
Arguments:
- positions: float32 [2, 4, 4, 3, 2048], P('gx', 'gy', 'gz'), may hold values from 0 to 1
- charges: float32 [2, 4, 4, 2048], P('gx', 'gy', 'gz'), may hold values from -1.8 to 1.8
- masses: float32 [2, 4, 4, 2048], P('gx', 'gy', 'gz'), may hold values from 1 to 16
- weights: float32 [2, 4, 4, 512], P('gx', 'gy', 'gz'), may hold values from 0 to 1, as said below
- mapping: int32 [2, 4, 4, 2048], P('gx', 'gy', 'gz'), may hold values from 0 to 511, as said below
- atom_lists: int32 [2, 4, 4, 16, 27], P('gx', 'gy', 'gz'), may hold values from 0 to 431, as said below
- bead_lists: int32 [2, 4, 4, 4, 12], P('gx', 'gy', 'gz'), may hold values from 0 to 107, as said below
- leaving: int32 [2, 4, 4, 2, 128], P('gx', 'gy', 'gz'), may hold values from 0 to 511, as said below
Outputs:
- forces: float32 [2, 4, 4, 3, 2048], P('gx', 'gy', 'gz')
- arrivals: float32 [2, 4, 4, 2, 8, 128], P('gx', 'gy', 'gz')
The draws below stay inside these ranges and needn't reach their ends.
Inputs may be any that keep to these rules, and one draw needn't show every extreme that they name: `mapping`: every bead number of a cell names exactly 4 atoms of that cell. `atom_lists`: entry c of every row names a tile of neighbourhood cell c, and within one cell and one column the 16 rows name 16 different tiles. `bead_lists`: the entries of one row are distinct. `leaving`: the 256 entries of a cell are distinct. With s = (i + 0.5) / 2 for a cell at slab index i: all weights are 1 where |s - 0.5| < 0.15 and all are 0 where |s - 0.5| >= 0.35.
All inputs are finite; a program needn't handle non-finite values.
Results may differ from the reference program's by a relative error of at most 0.0003.
Values sent between devices are 32-bit elements; how exact they have to be, the bound alone decides.
No kernel may reach another device: no remote copies, remote signals or barrier semaphores. Data moves between devices by JAX's collectives and lax.ppermute only.
A program may use at most 64 MiB of HBM per device.

```python
import math
import jax
import jax.numpy as jnp
from jax import lax

ATOMS = 2048
MOL_ATOMS = 4
LIST_BEAD = 12
BEADS = 512
ATILES = 16
BTILES = 4
LEAVERS = 128
CELLS_X = 2
CELLS_Y = 4
CELLS_Z = 4


def draw_weights(key, part):
    subkey = jax.random.fold_in(key, 11)
    shape_all = (CELLS_X, CELLS_Y, CELLS_Z, BEADS)
    middle = jax.random.uniform(subkey, shape_all, jnp.float32, 0.05, 0.95)
    slab_pos = (jnp.arange(CELLS_X, dtype=jnp.float32) + 0.5) / CELLS_X
    distance = jnp.abs(slab_pos - 0.5)[:, None, None, None]
    inner_slab = distance < 0.15
    hybrid = distance < 0.35
    return jnp.where(inner_slab, 1.0, jnp.where(hybrid, middle, 0.0)).astype(jnp.float32)


def draw_mapping(key, part):
    key_list = jax.random.split(jax.random.fold_in(key, 23), CELLS_X * CELLS_Y * CELLS_Z)
    shuffled = jax.vmap(lambda subkey: jax.random.permutation(subkey, ATOMS))(key_list)
    return (shuffled // MOL_ATOMS).astype(jnp.int32).reshape(CELLS_X, CELLS_Y, CELLS_Z, ATOMS)


def draw_atom_lists(key, part):
    key_list = jax.random.split(jax.random.fold_in(key, 37), CELLS_X * CELLS_Y * CELLS_Z * 27)
    shuffled = jax.vmap(lambda subkey: jax.random.permutation(subkey, ATILES))(key_list)
    shuffled = shuffled.reshape(CELLS_X, CELLS_Y, CELLS_Z, 27, ATILES)
    column_base = (jnp.arange(27).astype(jnp.int32) * ATILES)[:, None]
    entries = (shuffled.astype(jnp.int32) + column_base).astype(jnp.int32)
    return jnp.swapaxes(entries, 3, 4).astype(jnp.int32)


def draw_bead_lists(key, part):
    key_list = jax.random.split(jax.random.fold_in(key, 41), CELLS_X * CELLS_Y * CELLS_Z * BTILES)
    shuffled = jax.vmap(lambda subkey: jax.random.permutation(subkey, 27 * BTILES))(key_list)
    return shuffled[:, :LIST_BEAD].astype(jnp.int32).reshape(CELLS_X, CELLS_Y, CELLS_Z, BTILES, LIST_BEAD)


def draw_leaving(key, part):
    key_list = jax.random.split(jax.random.fold_in(key, 53), CELLS_X * CELLS_Y * CELLS_Z)
    shuffled = jax.vmap(lambda subkey: jax.random.permutation(subkey, BEADS))(key_list)
    return shuffled[:, :2 * LEAVERS].astype(jnp.int32).reshape(CELLS_X, CELLS_Y, CELLS_Z, 2, LEAVERS)


def block_levels(key, dims, cuts, smallest, largest):
    level = 1.0
    for dim, parts in cuts:
        steps = jax.random.uniform(jax.random.fold_in(jax.random.fold_in(key, 6), dim), (parts,), jnp.float32, smallest / len(cuts), largest / len(cuts))
        level = level * jnp.repeat(jnp.exp(steps), dims[dim] // parts).reshape((-1,) + (1,) * (len(dims) - 1 - dim))
    return level


def noise(key, extent, deviation, bound, cuts=(), kind=jnp.bfloat16):
    values = deviation * jax.random.normal(key, extent, jnp.float32)
    if cuts:
        values = values * block_levels(key, extent, cuts, -0.22, 0.18)
    return jnp.clip(values, -bound, bound).astype(kind)


def setup_inputs(seed: int = 0) -> dict:
    key_of = jax.random.split(jax.random.key(seed), 9)
    return {
        "positions": jnp.clip(1.0 * jax.random.uniform(key_of[0], (CELLS_X, CELLS_Y, CELLS_Z, 3, ATOMS), jnp.float32) ** block_levels(key_of[0], (CELLS_X, CELLS_Y, CELLS_Z, 3, ATOMS), ((0, 2), (1, 4), (2, 4)), -0.2, 0.2), 0.0, 1.0),
        "charges": noise(key_of[1], (CELLS_X, CELLS_Y, CELLS_Z, ATOMS), 0.3, 1.8, ((0, 2), (1, 4), (2, 4)), jnp.float32),
        "masses": jnp.clip(jnp.exp(math.log(16.0) - 2.7725887 * jax.random.uniform(key_of[2], (CELLS_X, CELLS_Y, CELLS_Z, ATOMS), jnp.float32) ** block_levels(key_of[2], (CELLS_X, CELLS_Y, CELLS_Z, ATOMS), ((0, 2), (1, 4), (2, 4)), -0.2, 0.2)), 1.0, 16.0),
        "weights": draw_weights(jax.random.fold_in(key_of[8], 71), 0),
        "mapping": draw_mapping(jax.random.fold_in(key_of[8], 71), 0),
        "atom_lists": draw_atom_lists(jax.random.fold_in(key_of[8], 71), 0),
        "bead_lists": draw_bead_lists(jax.random.fold_in(key_of[8], 71), 0),
        "leaving": draw_leaving(jax.random.fold_in(key_of[8], 71), 0),
    }


soft_core = 0.01
eps_coarse = 2.0
sigma_sq = 0.25

def neighbour_offsets():
    unit_steps = jnp.arange(3, dtype=jnp.float32) - 1.0
    shift_x = jnp.broadcast_to(unit_steps[:, None, None], (3, 3, 3))
    shift_y = jnp.broadcast_to(unit_steps[None, :, None], (3, 3, 3))
    shift_z = jnp.broadcast_to(unit_steps[None, None, :], (3, 3, 3))
    return jnp.stack([shift_x, shift_y, shift_z], axis=3).reshape(27, 3, 1)

def atom_tile(own_rows, listed):
    other = jnp.moveaxis(listed, 1, 0)
    displace = own_rows[:3, :, None, None] - other[:3, None, :, :]
    dist_sq = lax.optimization_barrier(jnp.sum(displace * displace, axis=0))
    inv_root = lax.rsqrt(dist_sq + soft_core)
    strength = (own_rows[3] * own_rows[4])[:, None, None] * (other[3] * other[4])[None, :, :] * (inv_root * inv_root * inv_root)
    return lax.optimization_barrier(jnp.sum(strength[None] * displace, axis=(2, 3)))

def coarse_tile(own_rows, listed):
    other = jnp.moveaxis(listed, 1, 0)
    displace = own_rows[:3, :, None, None] - other[:3, None, :, :]
    dist_sq = lax.optimization_barrier(jnp.sum(displace * displace, axis=0))
    strength = eps_coarse * jnp.exp(-dist_sq / sigma_sq) * (1.0 - own_rows[3][:, None, None] * other[3][None, :, :])
    return lax.optimization_barrier(jnp.sum(strength[None] * displace, axis=(2, 3)))

def listed_forces(near_rows, own_rows, lists, tile_fn):
    width = own_rows.shape[0]
    tile_count = own_rows.shape[1] // 128
    near_tiles = near_rows.reshape(27, width, tile_count, 128)
    own_tiles = jnp.moveaxis(own_rows.reshape(width, tile_count, 128), 1, 0)

    def one_tile(member):
        own_block, listed = member
        picked = near_tiles[listed // tile_count, :, listed % tile_count, :]
        return tile_fn(own_block, picked)
    result = lax.map(one_tile, (own_tiles, lists))
    return jnp.moveaxis(result, 0, 1).reshape(3, -1)

def reference(positions, charges, masses, weights, mapping, atom_lists, bead_lists, leaving):
    cells_x, cells_y, cells_z = (positions.shape[0], positions.shape[1], positions.shape[2])
    atom_count = positions.shape[4]
    bead_count = weights.shape[3]

    def centres_of(coords, mass, label):
        mass_sum = jax.ops.segment_sum(mass, label, num_segments=bead_count)
        centre_pos = jax.ops.segment_sum((mass[None] * coords).T, label, num_segments=bead_count).T / mass_sum
        return (centre_pos, mass_sum)
    centres, mass_sums = jax.vmap(jax.vmap(jax.vmap(centres_of)))(positions, masses, mapping)
    atom_weight = jnp.take_along_axis(weights, mapping, axis=3)
    atom_rows = jnp.concatenate([positions, charges[:, :, :, None], atom_weight[:, :, :, None]], axis=3)
    bead_rows = jnp.concatenate([centres, weights[:, :, :, None]], axis=3)
    offsets = neighbour_offsets()

    def one_cell(flat_cell):
        index_x = flat_cell // (cells_y * cells_z)
        index_y = flat_cell // cells_z % cells_y
        index_z = flat_cell % cells_z
        unit_steps = jnp.arange(3).astype(jnp.int32) - 1
        around_x = (index_x + unit_steps) % cells_x
        around_y = (index_y + unit_steps) % cells_y
        around_z = (index_z + unit_steps) % cells_z
        near_atoms = atom_rows[around_x][:, around_y][:, :, around_z].reshape(27, 5, atom_count)
        near_beads = bead_rows[around_x][:, around_y][:, :, around_z].reshape(27, 4, bead_count)
        near_atoms = near_atoms.at[:, :3].add(offsets)
        near_beads = near_beads.at[:, :3].add(offsets)
        own_atoms = atom_rows[index_x, index_y, index_z]
        own_beads = bead_rows[index_x, index_y, index_z]
        atomic_force = listed_forces(near_atoms, own_atoms, atom_lists[index_x, index_y, index_z], atom_tile)
        coarse_force = listed_forces(near_beads, own_beads, bead_lists[index_x, index_y, index_z], coarse_tile)
        label = mapping[index_x, index_y, index_z]
        fraction = masses[index_x, index_y, index_z] / mass_sums[index_x, index_y, index_z][label]
        return atomic_force + fraction[None] * coarse_force[:, label]
    total_cells = cells_x * cells_y * cells_z
    forces = lax.map(one_cell, jnp.arange(total_cells).astype(jnp.int32))
    forces = forces.reshape(cells_x, cells_y, cells_z, 3, atom_count)

    def payload_of(force, label, centre_pos, weight, mass_sum, leave):
        molecule_force = jax.ops.segment_sum(force.T, label, num_segments=bead_count).T
        record = jnp.concatenate([centre_pos, molecule_force, weight[None], mass_sum[None]], axis=0)
        return (record[:, leave[0]], record[:, leave[1]])
    upward, downward = jax.vmap(jax.vmap(jax.vmap(payload_of)))(forces, mapping, centres, weights, mass_sums, leaving)
    from_lower = jnp.roll(upward, 1, axis=0)
    from_higher = jnp.roll(downward, -1, axis=0)
    from_lower = from_lower.at[:, :, :, 0, :].add(-1.0)
    from_higher = from_higher.at[:, :, :, 0, :].add(1.0)
    arrivals = jnp.stack([from_lower, from_higher], axis=3)
    return (forces, arrivals)
```

```python
import functools

import jax
import jax.numpy as jnp
from jax import lax
from jax.experimental import pallas as pl
from jax.experimental.pallas import tpu as pltpu
from jax.sharding import PartitionSpec as P

SOFT_CORE = 0.01
EPS_COARSE = 2.0
SIGMA_SQ = 0.25
LANES = 128
ROWS = 32
F32, BF16 = jnp.float32, jnp.bfloat16
VMEM = pl.BlockSpec(memory_space=pltpu.VMEM)
SMEM = pl.BlockSpec(memory_space=pltpu.SMEM)
CONTRACT_LANES = (((1,), (1,)), ((), ()))


def split3(v):
    high = v.astype(BF16).astype(F32)
    rest = v - high
    mid = rest.astype(BF16).astype(F32)
    return high, mid, rest - mid


def far_rows(coords, soft):
    rows = []
    for v in coords:
        h, m, l = split3(v)
        rows += [h, h, h, m, m, l]
    norm = coords[0] * coords[0] + coords[1] * coords[1] + (coords[2] * coords[2] + soft)
    one = jnp.ones_like(norm)
    return rows + [one, one, one] + list(split3(norm))


def near_rows(coords, scale):
    rows = []
    for v in coords:
        h, m, l = (-2.0 * scale * part for part in split3(v))
        rows += [h, m, l, h, m, h]
    norm = scale * (coords[0] * coords[0] + coords[1] * coords[1] + coords[2] * coords[2])
    one = jnp.full_like(norm, scale)
    return rows + list(split3(norm)) + [one, one, one]


def store_rows(ref, rows):
    for r, row in enumerate(rows):
        ref[:, r, :] = row
    blank = jnp.zeros_like(rows[0])
    for r in range(len(rows), ROWS):
        ref[:, r, :] = blank


def one_hot(label_ref, out_ref, tiles):
    for t in range(tiles):
        at = slice(t * LANES, (t + 1) * LANES)
        low = lax.rem(label_ref[:, at], LANES)
        ids = lax.broadcasted_iota(jnp.int32, (LANES, LANES), 0)
        out_ref[:, at] = jnp.where(ids == low, 1.0, 0.0).astype(BF16)


def high_mask(label, groups, repeat):
    ids = lax.broadcasted_iota(jnp.int32, (groups, label.shape[1]), 0)
    hit = (ids == label // LANES).astype(F32)
    return jnp.concatenate([hit] * repeat, axis=0)


def stacked3(v):
    return jnp.concatenate(list(split3(v)), axis=0).astype(BF16)


def fold3(v):
    n = v.shape[0] // 3
    return v[:n] + v[n : 2 * n] + v[2 * n :]


def gather_rows(table, label, hot, groups):
    features = table.shape[0] // groups
    picked = fold3(jnp.dot(stacked3(table), hot, preferred_element_type=F32))
    picked = picked * high_mask(label, groups, features)
    return [
        jnp.sum(picked[f * groups : (f + 1) * groups], axis=0, keepdims=True)
        for f in range(features)
    ]


def sum_rows(values, label, hot, groups):
    spread = jnp.concatenate([jnp.broadcast_to(v, (groups, v.shape[1])) for v in values], axis=0)
    spread = spread * high_mask(label, groups, len(values))
    return fold3(
        lax.dot_general(stacked3(spread), hot, CONTRACT_LANES, preferred_element_type=F32)
    )


def prepare_kernel(pos, charge, mass, weight, label_ref, rows_out, mass_out, near_out, hot, near):
    atoms, beads = pos.shape[1], weight.shape[1]
    tiles, groups = atoms // LANES, beads // LANES
    one_hot(label_ref, hot, tiles)
    label = label_ref[...]
    m = mass[...]
    values = [m * pos[k : k + 1, :] for k in range(3)] + [m]
    sums = sum_rows(values, label, hot[...], groups)
    mass_sum = sums[3 * groups :]
    mass_out[...] = mass_sum
    table = jnp.concatenate(
        [weight[:, g * LANES : (g + 1) * LANES] for g in range(groups)], axis=0
    )
    charged = charge[...] * gather_rows(table, label, hot[...], groups)[0]
    for t in range(tiles):
        at = slice(t * LANES, (t + 1) * LANES)
        for k in range(3):
            rows_out[k * tiles + t : k * tiles + t + 1, :] = pos[k : k + 1, at]
        rows_out[3 * tiles + t : 3 * tiles + t + 1, :] = charged[:, at]
    base = 4 * tiles
    for k in range(3):
        rows_out[base + k * groups : base + (k + 1) * groups, :] = (
            sums[k * groups : (k + 1) * groups] / mass_sum
        )
    rows_out[base + 3 * groups : base + 4 * groups, :] = table
    coords = [rows_out[k * tiles : (k + 1) * tiles, :] - 0.5 for k in range(3)]
    store_rows(near, near_rows(coords, 1.0))
    for t in range(tiles):
        near_out[t] = near[t].T.astype(BF16)


def pair_kernel(tiles, groups, entries, sources, first, *refs):
    signs, lists, own, near = refs[:4]
    cells = refs[4 : 4 + sources]
    rest = refs[4 + sources :]
    before = None if first else rest[0]
    out, far, even, odd, total = rest[0 if first else 1 :]
    count = len(entries)
    height = 4 * (tiles + groups)
    columns = []
    for e, (source, cell, steps) in enumerate(entries):
        step = [steps[k] * signs[k] for k in range(3)]
        columns.append(9 * (step[0] + 1) + 3 * (step[1] + 1) + (step[2] + 1))
        base = cell * height
        coords = [
            cells[source][base + k * tiles : base + (k + 1) * tiles, :]
            + (step[k].astype(F32) - 0.5)
            for k in range(3)
        ]
        charged = cells[source][base + 3 * tiles : base + 4 * tiles, :]
        store_rows(far.at[e], far_rows(coords, SOFT_CORE) + coords + [charged])

    def distances(t, into):
        lhs = near[t]
        for e in range(0, count, 2):
            members = range(e, min(e + 2, count))
            rhs = [far[m, lists[t, columns[m]] - tiles * columns[m]].astype(BF16) for m in members]
            rhs = jnp.concatenate(rhs, axis=1) if len(rhs) > 1 else rhs[0]
            into[:, e * LANES : e * LANES + rhs.shape[1]] = jnp.dot(
                lhs, rhs, preferred_element_type=F32
            )

    def strengths(t, dist):
        block = 32
        for i in range(0, LANES, block):
            at = slice(i, i + block)
            acc = [jnp.zeros((block, LANES), F32)] * 4
            for e in range(count):
                k = lists[t, columns[e]] - tiles * columns[e]
                inv = lax.rsqrt(dist[at, e * LANES : (e + 1) * LANES])
                s = inv * inv * inv * far[e, k, 27:28, :]
                acc[3] = acc[3] + s
                for d in range(3):
                    acc[d] = acc[d] + s * far[e, k, 24 + d : 25 + d, :]
            for d in range(4):
                total[d, at, :] = acc[d]
        sums = [jnp.sum(total[d].T, axis=0, keepdims=True) for d in range(4)]
        scale = own[pl.ds(3 * tiles + t, 1), :]
        for d in range(3):
            here = own[pl.ds(d * tiles + t, 1), :] - 0.5
            force = scale * (here * sums[3] - sums[d])
            if before is not None:
                force = force + before[pl.ds(d * tiles + t, 1), :]
            out[pl.ds(d * tiles + t, 1), :] = force

    distances(0, even)

    def two_tiles(step, carry):
        t = 2 * step
        distances(t + 1, odd)
        strengths(t, even)
        distances(jnp.minimum(t + 2, tiles - 1), even)
        strengths(t + 1, odd)
        return carry

    lax.fori_loop(0, tiles // 2, two_tiles, 0)


def final_kernel(tiles, groups, entries, sources, *refs):
    signs, bead_lists, own, mass_sum_ref, atomic, mass, label_ref, leave_ref = refs[:8]
    cells = refs[8 : 8 + sources]
    forces_out, record_out, hot, leave_hot, far, near, nearest, dist, total, coarse = refs[
        8 + sources :
    ]
    listed = bead_lists.shape[1]
    height = 4 * (tiles + groups)
    for source, cell, steps in entries:
        step = [steps[k] * signs[k] for k in range(3)]
        column = 9 * (step[0] + 1) + 3 * (step[1] + 1) + (step[2] + 1)
        base = cell * height + 4 * tiles
        coords = [
            cells[source][base + k * groups : base + (k + 1) * groups, :]
            + (step[k].astype(F32) - 0.5)
            for k in range(3)
        ]
        weight = cells[source][base + 3 * groups : base + 4 * groups, :]
        store_rows(far.at[pl.ds(column * groups, groups)], far_rows(coords, 0.0) + coords + [weight])
    base = 4 * tiles
    coords = [own[base + k * groups : base + (k + 1) * groups, :] - 0.5 for k in range(3)]
    own_weight = own[base + 3 * groups : base + 4 * groups, :]
    store_rows(near, near_rows(coords, -1.0 / SIGMA_SQ) + [own_weight])
    for b in range(groups):
        nearest[b] = near[b].T

    def one_tile(b, carry):
        column = lax.broadcasted_iota(jnp.int32, (LANES, ROWS), 1)
        lhs = jnp.where(column < 24, nearest[b], 0.0).astype(BF16)
        for e in range(listed):
            rhs = far[bead_lists[b, e]].astype(BF16)
            dist[:, e * LANES : (e + 1) * LANES] = jnp.dot(lhs, rhs, preferred_element_type=F32)
        block = 32
        for i in range(0, LANES, block):
            at = slice(i, i + block)
            acc = [jnp.zeros((block, LANES), F32)] * 4
            here = jnp.broadcast_to(nearest[b, at, 24:25], (block, LANES))
            for e in range(listed):
                k = bead_lists[b, e]
                s = jnp.exp(dist[at, e * LANES : (e + 1) * LANES]) * (
                    EPS_COARSE - here * (EPS_COARSE * far[k, 27:28, :])
                )
                acc[3] = acc[3] + s
                for d in range(3):
                    acc[d] = acc[d] + s * far[k, 24 + d : 25 + d, :]
            for d in range(4):
                total[d, at, :] = acc[d]
        sums = [jnp.sum(total[d].T, axis=0, keepdims=True) for d in range(4)]
        for d in range(3):
            centre = own[pl.ds(base + d * groups + b, 1), :] - 0.5
            coarse[pl.ds(d * groups + b, 1), :] = centre * sums[3] - sums[d]
        return carry

    lax.fori_loop(0, groups, one_tile, 0)

    one_hot(label_ref, hot, tiles)
    label = label_ref[...]
    mass_sum = mass_sum_ref[...]
    scaled = coarse[...] / jnp.concatenate([mass_sum] * 3, axis=0)
    spread = gather_rows(scaled, label, hot[...], groups)
    forces = []
    for d in range(3):
        flat = jnp.concatenate(
            [atomic[d * tiles + t : d * tiles + t + 1, :] for t in range(tiles)], axis=1
        )
        forces.append(flat + mass[...] * spread[d])
        forces_out[d : d + 1, :] = forces[d]
    molecule = sum_rows(forces, label, hot[...], groups)
    table = jnp.concatenate(
        [own[base : base + 3 * groups, :], molecule, own_weight, mass_sum], axis=0
    )
    leavers = leave_ref.shape[1] // 2
    one_hot(leave_ref, leave_hot, leave_ref.shape[1] // LANES)
    picked = gather_rows(table, leave_ref[...], leave_hot[...], groups)
    for side, shift in ((0, -1.0), (1, 1.0)):
        for f in range(8):
            row = picked[f][:, side * leavers : (side + 1) * leavers]
            record_out[side, f : f + 1, :] = row + shift if f == 0 else row


def exchange(x, axis):
    n = lax.axis_size(axis)
    if n == 1:
        return [(x, 1), (x, -1)]
    if n == 2:
        other = lax.ppermute(x, axis, [(0, 1), (1, 0)])
        return [(other, 1), (other, -1)]
    if n % 2 == 0:
        inner = [(i, i ^ 1) for i in range(n)]
        outer = [(i, ((i + 1) ^ 1) - 1) for i in range(n)]
        outer = [(i, (j + n) % n) for i, j in outer]
        second = lax.ppermute(x, axis, outer)
        first = lax.ppermute(x, axis, inner)
        return [(first, 1), (second, -1)]
    up = [(i, (i + 1) % n) for i in range(n)]
    down = [(j, i) for i, j in up]
    return [(lax.ppermute(x, axis, down), 1), (lax.ppermute(x, axis, up), -1)]


def sign_of(axis):
    n = lax.axis_size(axis)
    if n > 2 and n % 2 == 0:
        return 1 - 2 * lax.rem(lax.axis_index(axis), 2)
    return jnp.int32(1)


def per_device(positions, charges, masses, weights, mapping, atom_lists, bead_lists, leaving):
    pos = positions[0, 0, 0]
    charge, mass = charges[0, 0], masses[0, 0]
    weight, label = weights[0, 0], mapping[0, 0]
    lists, beads_listed = atom_lists[0, 0, 0], bead_lists[0, 0, 0]
    atoms, beads = pos.shape[1], weight.shape[1]
    tiles, groups = atoms // LANES, beads // LANES
    height = 4 * (tiles + groups)
    limit = pltpu.CompilerParams(vmem_limit_bytes=48 * 2**20)
    signs = jnp.stack([sign_of("gx"), sign_of("gy"), sign_of("gz")]).astype(jnp.int32)

    own, mass_sum, near = pl.pallas_call(
        prepare_kernel,
        out_shape=(
            jax.ShapeDtypeStruct((height, LANES), F32),
            jax.ShapeDtypeStruct((groups, LANES), F32),
            jax.ShapeDtypeStruct((tiles, LANES, ROWS), BF16),
        ),
        in_specs=[VMEM] * 5,
        out_specs=(VMEM,) * 3,
        scratch_shapes=[
            pltpu.VMEM((LANES, atoms), BF16),
            pltpu.VMEM((tiles, ROWS, LANES), F32),
        ],
        compiler_params=limit,
    )(pos, charge, mass, weight, label)

    def pairs(entries, cells, before):
        count = len(entries)
        extra = [] if before is None else [before]
        args = [signs, lists, own, near, *cells, *extra]
        work = tiles * count * LANES * LANES
        return pl.pallas_call(
            functools.partial(pair_kernel, tiles, groups, entries, len(cells), before is None),
            out_shape=jax.ShapeDtypeStruct((3 * tiles, LANES), F32),
            in_specs=[SMEM, SMEM] + [VMEM] * (len(args) - 2),
            out_specs=VMEM,
            scratch_shapes=[
                pltpu.VMEM((count, tiles, ROWS, LANES), F32),
                pltpu.VMEM((LANES, count * LANES), F32),
                pltpu.VMEM((LANES, count * LANES), F32),
                pltpu.VMEM((4, LANES, LANES), F32),
            ],
            compiler_params=limit,
            cost_estimate=pl.CostEstimate(
                flops=60 * work, bytes_accessed=4 * height * LANES, transcendentals=work
            ),
        )(*args)

    with_y = exchange(own, "gy")
    force = pairs([(0, 0, (0, 0, 0))], [own], None)
    column = jnp.concatenate([own] + [block for block, _ in with_y], axis=0)
    y_steps = [0] + [step for _, step in with_y]
    with_x = exchange(column, "gx")
    force = pairs([(0, c, (0, y_steps[c], 0)) for c in (1, 2)], [column], force)
    if lax.axis_size("gx") <= 2:
        plane = jnp.concatenate([column, with_x[0][0]], axis=0)
        plane_cells = [(c, (0, y_steps[c])) for c in range(3)]
        plane_cells += [(3 + c, (x, y_steps[c])) for c in range(3) for x in (1, -1)]
    else:
        plane = jnp.concatenate([column] + [block for block, _ in with_x], axis=0)
        plane_cells = [(c, (0, y_steps[c])) for c in range(3)]
        plane_cells += [
            (3 + 3 * k + c, (with_x[k][1], y_steps[c])) for c in range(3) for k in range(2)
        ]
    with_z = exchange(plane, "gz")
    force = pairs([(0, c, (x, y, 0)) for c, (x, y) in plane_cells[3:]], [plane], force)
    for block, z in with_z:
        force = pairs([(0, c, (x, y, z)) for c, (x, y) in plane_cells], [block], force)

    sources = [plane] + [block for block, _ in with_z]
    z_steps = [0] + [step for _, step in with_z]
    entries = [(s, c, (x, y, z_steps[s])) for s in range(3) for c, (x, y) in plane_cells]
    listed = beads_listed.shape[1]
    leavers = leaving.shape[4]
    forces, record = pl.pallas_call(
        functools.partial(final_kernel, tiles, groups, entries, len(sources)),
        out_shape=(
            jax.ShapeDtypeStruct((3, atoms), F32),
            jax.ShapeDtypeStruct((2, 8, leavers), F32),
        ),
        in_specs=[SMEM, SMEM] + [VMEM] * (6 + len(sources)),
        out_specs=(VMEM, VMEM),
        scratch_shapes=[
            pltpu.VMEM((LANES, atoms), BF16),
            pltpu.VMEM((LANES, 2 * leavers), BF16),
            pltpu.VMEM((27 * groups, ROWS, LANES), F32),
            pltpu.VMEM((groups, ROWS, LANES), F32),
            pltpu.VMEM((groups, LANES, ROWS), F32),
            pltpu.VMEM((LANES, listed * LANES), F32),
            pltpu.VMEM((4, LANES, LANES), F32),
            pltpu.VMEM((3 * groups, LANES), F32),
        ],
        compiler_params=limit,
    )(
        signs, beads_listed, own, mass_sum, force, mass, label,
        leaving[0, 0, 0].reshape(1, 2 * leavers), *sources,
    )
    n = lax.axis_size("gx")
    if n == 2:
        arrivals = lax.ppermute(record, "gx", [(0, 1), (1, 0)])
    else:
        up = [(i, (i + 1) % n) for i in range(n)]
        down = [(j, i) for i, j in up]
        arrivals = jnp.stack(
            [lax.ppermute(record[0], "gx", up), lax.ppermute(record[1], "gx", down)]
        )
    return (forces[None, None, None], arrivals[None, None, None])


def solution(mesh):
    cell = ("gx", "gy", "gz")
    placed = (
        P(*cell, None, None),
        P(*cell, None),
        P(*cell, None),
        P(*cell, None),
        P(*cell, None),
        P(*cell, None, None),
        P(*cell, None, None),
        P(*cell, None, None),
    )
    return jax.shard_map(
        per_device,
        mesh=mesh,
        in_specs=placed,
        out_specs=(P(*cell, None, None), P(*cell, None, None, None)),
        check_vma=False,
    )
```

```python
import functools
import math

import jax
import jax.numpy as jnp
from jax import lax
from jax.experimental import pallas as pl
from jax.experimental.pallas import tpu as pltpu
from jax.sharding import PartitionSpec as P

SOFT_CORE = 0.01
EPS_COARSE = 2.0
SIGMA_SQ = 0.25
LANES = 128
ROWS = 32
PARTS = 4
F32, BF16 = jnp.float32, jnp.bfloat16
VMEM = pl.BlockSpec(memory_space=pltpu.VMEM)
SMEM = pl.BlockSpec(memory_space=pltpu.SMEM)
CONTRACT_LANES = (((1,), (1,)), ((), ()))


def split3(v):
    high = v.astype(BF16).astype(F32)
    rest = v - high
    mid = rest.astype(BF16).astype(F32)
    return high, mid, rest - mid


def far_rows(coords, soft):
    parts = [split3(v) for v in coords]
    norm = coords[0] * coords[0] + coords[1] * coords[1] + (coords[2] * coords[2] + soft)
    nh, nm, nl = split3(norm)
    one = jnp.ones_like(norm)
    rows = [p[0] for p in parts] + [p[1] for p in parts] + [nh, nm]
    return rows + [p[2] for p in parts] + [nl, one, one, one, jnp.zeros_like(one)]


def near_rows(coords, scale):
    parts = [[-2.0 * scale * part for part in split3(v)] for v in coords]
    norm = scale * (coords[0] * coords[0] + coords[1] * coords[1] + coords[2] * coords[2])
    one, zero = jnp.full_like(norm, scale), jnp.zeros_like(norm)
    h, m, l = ([p[k] for p in parts] for k in range(3))
    rows = h + h + [one, one] + m + m + [zero, zero] + l + l + [zero, zero]
    return rows + h + [one] + list(split3(norm)) + [zero]


def picked_rows(far, k, stride):
    first = far[pl.ds(k, 8, stride=stride), :]
    last = far[pl.ds(k + 8 * stride, 8, stride=stride), :]
    return jnp.concatenate([first, first, first, last], axis=0).astype(BF16)


def one_hot(label_ref, out_ref, tiles):
    ids = lax.broadcasted_iota(jnp.int32, (LANES, LANES), 0)
    for t in range(tiles):
        at = slice(t * LANES, (t + 1) * LANES)
        low = lax.rem(label_ref[:, at], LANES)
        out_ref[:, at] = jnp.where(ids == low, 1.0, 0.0).astype(BF16)


def high_mask(label, groups, repeat):
    ids = lax.broadcasted_iota(jnp.int32, (groups, label.shape[1]), 0)
    hit = (ids == label // LANES).astype(F32)
    return jnp.concatenate([hit] * repeat, axis=0)


def stacked3(v):
    return jnp.concatenate(list(split3(v)), axis=0).astype(BF16)


def fold3(v):
    n = v.shape[0] // 3
    return v[:n] + v[n : 2 * n] + v[2 * n :]


def gather_rows(table, label, hot, groups):
    features = table.shape[0] // groups
    picked = fold3(jnp.dot(stacked3(table), hot, preferred_element_type=F32))
    picked = picked * high_mask(label, groups, features)
    return [
        jnp.sum(picked[f * groups : (f + 1) * groups], axis=0, keepdims=True)
        for f in range(features)
    ]


def sum_rows(values, label, hot, groups):
    spread = jnp.concatenate([jnp.broadcast_to(v, (groups, v.shape[1])) for v in values], axis=0)
    spread = spread * high_mask(label, groups, len(values))
    return fold3(
        lax.dot_general(stacked3(spread), hot, CONTRACT_LANES, preferred_element_type=F32)
    )


def flat_row(ref, first, tiles):
    return jnp.concatenate([ref[first + t : first + t + 1, :] for t in range(tiles)], axis=1)


def signs_here():
    return [sign_of(axis) for axis in ("gx", "gy", "gz")]


def column_of(step):
    return 9 * (step[0] + 1) + 3 * (step[1] + 1) + (step[2] + 1)


def as_float(step):
    return float(step) if isinstance(step, int) else step.astype(F32)


def pair_plan(tiles, count):
    held, ahead = (8, 6) if count == 1 else (8, 4) if count == 2 else (2, 1)
    unroll = max(held, 4)
    if tiles % unroll:
        held, unroll, ahead = 2, 2, 1
    return held, unroll, ahead


def prepare_kernel(
    label_ref, mass, pos, weight, charge, rows_out, mass_out, near_out, hot, near
):
    beads = weight.shape[1]
    tiles, groups = pos.shape[1] // LANES, beads // LANES
    one_hot(label_ref, hot, tiles)
    label = label_ref[...]
    m = mass[...]
    values = [m * pos[k : k + 1, :] for k in range(3)] + [m]
    sums = sum_rows(values, label, hot[...], groups)
    mass_sum = sums[3 * groups :]
    mass_out[...] = mass_sum
    table = jnp.concatenate(
        [weight[:, g * LANES : (g + 1) * LANES] for g in range(groups)], axis=0
    )
    charged = charge[...] * gather_rows(table, label, hot[...], groups)[0]
    for t in range(tiles):
        at = slice(t * LANES, (t + 1) * LANES)
        for k in range(3):
            rows_out[k * tiles + t : k * tiles + t + 1, :] = pos[k : k + 1, at]
        rows_out[3 * tiles + t : 3 * tiles + t + 1, :] = charged[:, at]
    base = 4 * tiles
    for k in range(3):
        rows_out[base + k * groups : base + (k + 1) * groups, :] = (
            sums[k * groups : (k + 1) * groups] / mass_sum
        )
    rows_out[base + 3 * groups : base + 4 * groups, :] = table
    coords = [rows_out[k * tiles : (k + 1) * tiles, :] - 0.5 for k in range(3)]
    for r, row in enumerate(near_rows(coords, 1.0)):
        near[r * tiles : (r + 1) * tiles, :] = row
    for t in range(tiles):
        block = near[pl.ds(t, ROWS, stride=tiles), :]
        near_out[t] = block.T.astype(BF16)


def pair_kernel(tiles, groups, entries, sources, first, last, passed, *refs):
    lists, own, near = refs[:3]
    cells = refs[3 : 3 + sources]
    rest = refs[3 + sources :]
    before = None if first else rest[0]
    rest = rest[0 if first else 1 :]
    for p in range(passed):
        rest[passed + 1 + p][...] = rest[p][...]
    rest = rest[passed : passed + 1] + rest[2 * passed + 1 :]
    out, far, held = rest[:3]
    total = rest[-1] if last else None
    count = len(entries)
    height = 4 * (tiles + groups)
    signs = signs_here()
    columns = []
    for e, (source, cell, steps) in enumerate(entries):
        step = [steps[k] * signs[k] if steps[k] else 0 for k in range(3)]
        columns.append(column_of(step))
        base = cell * height
        coords = [
            cells[source][base + k * tiles : base + (k + 1) * tiles, :]
            + (as_float(step[k]) - 0.5)
            for k in range(3)
        ]
        charged = cells[source][base + 3 * tiles : base + 4 * tiles, :]
        for r, row in enumerate(far_rows(coords, SOFT_CORE) + coords + [charged]):
            far[e, r * tiles : (r + 1) * tiles, :] = row

    def number(t, e):
        return lists[t, columns[e]] - tiles * columns[e]

    def distances(t, into, part=None):
        lhs = near[t]
        starts = list(range(0, count, 2))
        if part is not None:
            starts = starts[part::PARTS]
        for e in starts:
            members = range(e, min(e + 2, count))
            rhs = [
                picked_rows(far.at[m], number(t, m), tiles) for m in members
            ]
            rhs = jnp.concatenate(rhs, axis=1) if len(rhs) > 1 else rhs[0]
            inv = lax.rsqrt(jnp.dot(lhs, rhs, preferred_element_type=F32))
            charged = [far[m, pl.ds(19 * tiles + number(t, m), 1), :] for m in members]
            charged = jnp.concatenate(charged, axis=1) if len(charged) > 1 else charged[0]
            into[:, e * LANES : e * LANES + rhs.shape[1]] = inv * inv * inv * charged

    def strengths(t, dist, part):
        block = LANES // PARTS
        at = slice(part * block, (part + 1) * block)
        if True:
            if before is None:
                acc = [jnp.zeros((block, LANES), F32)] * 4
            else:
                acc = [before[t, d, at, :] for d in range(4)]
            for e in range(count):
                k = number(t, e)
                s = dist[at, e * LANES : (e + 1) * LANES]
                acc[3] = acc[3] + s
                for d in range(3):
                    acc[d] = acc[d] + s * far[e, pl.ds((16 + d) * tiles + k, 1), :]
            for d in range(4):
                if last:
                    total[d, at, :] = acc[d]
                else:
                    out[t, d, at, :] = acc[d]
        if not last or part < PARTS - 1:
            return
        sums = [jnp.sum(total[d].T, axis=0, keepdims=True) for d in range(4)]
        scale = own[pl.ds(3 * tiles + t, 1), :]
        for d in range(3):
            here = own[pl.ds(d * tiles + t, 1), :] - 0.5
            out[pl.ds(d * tiles + t, 1), :] = scale * (here * sums[3] - sums[d])

    buffered, unroll, ahead = pair_plan(tiles, count)
    buffers = [held.at[i] for i in range(buffered)]
    for i in range(ahead):
        distances(jnp.int32(i), buffers[i])

    def some_tiles(step, carry):
        for u in range(unroll):
            t = unroll * step + u
            for part in range(PARTS):
                distances(jnp.minimum(t + ahead, tiles - 1), buffers[(u + ahead) % buffered], part)
                strengths(t, buffers[u % buffered], part)

        return carry

    lax.fori_loop(0, tiles // unroll, some_tiles, 0)


def weight_rows(weight):
    h, m, l = split3(weight)
    return [h, h, h, m, m, l], [h, m, l, h, m, h]


def final_kernel(tiles, groups, entries, sources, *refs):
    lists, own, mass_sum_ref, atomic, mass, label_ref, leave_ref, hot = refs[:8]
    cells = refs[8 : 8 + sources]
    rest = refs[8 + sources :]
    forces_out, record_out, leave_hot, raw, far, near, nearest = rest[:7]
    buffers, (total, coarse) = (rest[7:9], rest[9:11]), rest[11:]
    listed = lists.shape[1]
    height = 4 * (tiles + groups)
    signs = signs_here()
    every = len(entries) * groups
    for source, cell, steps in entries:
        step = [steps[k] * signs[k] if steps[k] else 0 for k in range(3)]
        column = column_of(step)
        base = cell * height + 4 * tiles
        for k in range(4):
            block = cells[source][base + k * groups : base + (k + 1) * groups, :]
            if k < 3:
                block = block + (as_float(step[k]) - 0.5)
            raw[k, pl.ds(column * groups, groups), :] = block
    scale = math.sqrt(math.log2(math.e) / SIGMA_SQ)
    coords = [raw[k] for k in range(3)]
    one, zero = jnp.ones_like(coords[0]), jnp.zeros_like(coords[0])
    plain = coords + weight_rows(raw[3])[0] + [one, zero]
    for r, row in enumerate(far_rows([scale * v for v in coords], 0.0) + plain):
        far[r * every : (r + 1) * every, :] = row
    base = 4 * tiles
    coords = [own[base + k * groups : base + (k + 1) * groups, :] - 0.5 for k in range(3)]
    own_weight = own[base + 3 * groups : base + 4 * groups, :]
    zero = jnp.zeros_like(own_weight)
    factors = [-EPS_COARSE * row for row in weight_rows(own_weight)[1]]
    factors += [zero + EPS_COARSE, zero] + [zero] * 8
    for r, row in enumerate(near_rows([scale * v for v in coords], -1.0) + factors):
        near[r * groups : (r + 1) * groups, :] = row
    for b in range(groups):
        nearest[b] = near[pl.ds(b, ROWS + 16, stride=groups), :].T.astype(BF16)

    def products(b, dist, factor):
        lhs = nearest[b]
        for e in range(0, listed, 2):
            members = [lists[b, m] for m in range(e, min(e + 2, listed))]
            at = slice(e * LANES, (e + len(members)) * LANES)
            rhs = jnp.concatenate([picked_rows(far, k, every) for k in members], axis=1)
            dist[:, at] = jnp.dot(lhs[:, :ROWS], rhs, preferred_element_type=F32)
            rhs = [far[pl.ds(k + 19 * every, 8, stride=every), :] for k in members]
            rhs = jnp.concatenate([jnp.concatenate([r, r], axis=0) for r in rhs], axis=1)
            factor[:, at] = jnp.dot(lhs[:, ROWS:], rhs.astype(BF16), preferred_element_type=F32)

    def strengths(b, dist, factor):
        block = 32
        for i in range(0, LANES, block):
            at = slice(i, i + block)
            acc = [jnp.zeros((block, LANES), F32)] * 4
            for e in range(listed):
                k = lists[b, e]
                lanes = slice(e * LANES, (e + 1) * LANES)
                s = jnp.exp2(dist[at, lanes]) * factor[at, lanes]
                acc[3] = acc[3] + s
                for d in range(3):
                    acc[d] = acc[d] + s * far[pl.ds((16 + d) * every + k, 1), :]
            for d in range(4):
                total[d, at, :] = acc[d]
        sums = [jnp.sum(total[d].T, axis=0, keepdims=True) for d in range(4)]
        for d in range(3):
            centre = own[base + d * groups + b : base + d * groups + b + 1, :] - 0.5
            coarse[d * groups + b : d * groups + b + 1, :] = centre * sums[3] - sums[d]

    products(0, *buffers[0])
    for b in range(groups):
        if b + 1 < groups:
            products(b + 1, *buffers[(b + 1) % 2])
        strengths(b, *buffers[b % 2])

    label = label_ref[...]
    mass_sum = mass_sum_ref[...]
    scaled = coarse[...] / jnp.concatenate([mass_sum] * 3, axis=0)
    spread = gather_rows(scaled, label, hot[...], groups)
    forces = []
    for d in range(3):
        forces.append(flat_row(atomic, d * tiles, tiles) + mass[...] * spread[d])
        for t in range(tiles):
            at = slice(t * LANES, (t + 1) * LANES)
            forces_out[d * tiles + t : d * tiles + t + 1, :] = forces[d][:, at]
    molecule = sum_rows(forces, label, hot[...], groups)
    table = jnp.concatenate(
        [own[base : base + 3 * groups, :], molecule, own_weight, mass_sum], axis=0
    )
    leavers = leave_ref.shape[1] // 2
    one_hot(leave_ref, leave_hot, leave_ref.shape[1] // LANES)
    picked = gather_rows(table, leave_ref[...], leave_hot[...], groups)
    for side, shift in ((0, -1.0), (1, 1.0)):
        for f in range(8):
            row = picked[f][:, side * leavers : (side + 1) * leavers]
            record_out[side, f : f + 1, :] = row + shift if f == 0 else row


def exchange(x, axis):
    n = lax.axis_size(axis)
    if n == 1:
        return [(x, 1), (x, -1)]
    if n == 2:
        other = lax.ppermute(x, axis, [(0, 1), (1, 0)])
        return [(other, 1), (other, -1)]
    if n % 2 == 0:
        inner = [(i, i ^ 1) for i in range(n)]
        outer = [(i, ((i + 1) ^ 1) - 1) for i in range(n)]
        outer = [(i, (j + n) % n) for i, j in outer]
        second = lax.ppermute(x, axis, outer)
        first = lax.ppermute(x, axis, inner)
        return [(first, 1), (second, -1)]
    up = [(i, (i + 1) % n) for i in range(n)]
    down = [(j, i) for i, j in up]
    return [(lax.ppermute(x, axis, down), 1), (lax.ppermute(x, axis, up), -1)]


def sign_of(axis):
    n = lax.axis_size(axis)
    if n > 2 and n % 2 == 0:
        return 1 - 2 * lax.rem(lax.axis_index(axis), 2)
    return jnp.int32(1)


def per_device(positions, charges, masses, weights, mapping, atom_lists, bead_lists, leaving):
    atoms, beads = positions.shape[4], weights.shape[3]
    tiles, groups = atoms // LANES, beads // LANES
    pos = positions[0, 0, 0]
    charge, mass = charges[0, 0], masses[0, 0]
    weight, label = weights[0, 0], mapping[0, 0]
    leavers = leaving.shape[4]
    height = 4 * (tiles + groups)
    limit = pltpu.CompilerParams(vmem_limit_bytes=48 * 2**20)
    inputs = [label, mass, pos, weight, charge]
    lists = atom_lists[0, 0, 0]

    def like(x):
        return jax.ShapeDtypeStruct(x.shape, x.dtype)

    own, mass_sum, near, hot = pl.pallas_call(
        prepare_kernel,
        out_shape=(
            jax.ShapeDtypeStruct((height, LANES), F32),
            jax.ShapeDtypeStruct((groups, LANES), F32),
            jax.ShapeDtypeStruct((tiles, LANES, ROWS), BF16),
            jax.ShapeDtypeStruct((LANES, atoms), BF16),
        ),
        in_specs=[VMEM] * 5,
        out_specs=(VMEM,) * 4,
        scratch_shapes=[pltpu.VMEM((ROWS * tiles, LANES), F32)],
        compiler_params=limit,
    )(*inputs)

    def pairs(lists, entries, cells, before, last=False, passed=()):
        count = len(entries)
        args = [lists, own, near, *cells] + ([] if before is None else [before])
        place = len(args) - 1
        args += passed
        shape = (3 * tiles, LANES) if last else (tiles, 4, LANES, LANES)
        work = tiles * count * LANES * LANES
        return pl.pallas_call(
            functools.partial(
                pair_kernel, tiles, groups, entries, len(cells), before is None, last, len(passed)
            ),
            out_shape=(jax.ShapeDtypeStruct(shape, F32), *[like(x) for x in passed]),
            in_specs=[SMEM] + [VMEM] * (len(args) - 1),
            out_specs=(VMEM,) * (1 + len(passed)),
            scratch_shapes=[
                pltpu.VMEM((count, 20 * tiles, LANES), F32),
                pltpu.VMEM((pair_plan(tiles, count)[0], LANES, count * LANES), F32),
            ]
            + ([pltpu.VMEM((4, LANES, LANES), F32)] if last else []),
            input_output_aliases={} if last or before is None else {place: 0},
            compiler_params=limit,
            cost_estimate=pl.CostEstimate(
                flops=60 * work, bytes_accessed=4 * height * LANES, transcendentals=work
            ),
        )(*args)

    with_y = exchange(own, "gy")
    force, lists = pairs(lists, [(0, 0, (0, 0, 0))], [own], None, passed=[lists])
    column = jnp.concatenate([own] + [block for block, _ in with_y], axis=0)
    column, force = lax.optimization_barrier((column, force))
    y_steps = [0] + [step for _, step in with_y]
    with_x = exchange(column, "gx")
    small = [bead_lists[0, 0, 0], leaving.reshape(1, 2 * leavers)]
    entries = [(0, c, (0, y_steps[c], 0)) for c in (1, 2)]
    force, beads_listed, leaving = pairs(lists, entries, [column], force, passed=small)
    plane_cells = [(c, (0, y_steps[c])) for c in range(3)]
    if lax.axis_size("gx") <= 2:
        plane = jnp.concatenate([column, with_x[0][0]], axis=0)
        plane_cells += [(3 + c, (x, y_steps[c])) for c in range(3) for x in (1, -1)]
    else:
        plane = jnp.concatenate([column] + [block for block, _ in with_x], axis=0)
        plane_cells += [
            (3 + 3 * k + c, (with_x[k][1], y_steps[c])) for c in range(3) for k in range(2)
        ]
    plane, force = lax.optimization_barrier((plane, force))
    with_z = exchange(plane, "gz")
    entries = [(0, c, (x, y, 0)) for c, (x, y) in plane_cells[3:]]
    force = pairs(lists, entries, [plane], force)[0]
    for place, (block, z) in enumerate(with_z):
        entries = [(0, c, (x, y, z)) for c, (x, y) in plane_cells]
        force = pairs(lists, entries, [block], force, place == 1)[0]

    sources = [plane] + [block for block, _ in with_z]
    z_steps = [0] + [step for _, step in with_z]
    entries = [(s, c, (x, y, z_steps[s])) for s in range(3) for c, (x, y) in plane_cells]
    every, listed = len(entries) * groups, beads_listed.shape[1]
    forces, record = pl.pallas_call(
        functools.partial(final_kernel, tiles, groups, entries, len(sources)),
        out_shape=(
            jax.ShapeDtypeStruct((3 * tiles, LANES), F32),
            jax.ShapeDtypeStruct((2, 8, leavers), F32),
        ),
        in_specs=[SMEM] + [VMEM] * (7 + len(sources)),
        out_specs=(VMEM, VMEM),
        scratch_shapes=[
            pltpu.VMEM((LANES, 2 * leavers), BF16),
            pltpu.VMEM((4, every, LANES), F32),
            pltpu.VMEM((27 * every, LANES), F32),
            pltpu.VMEM(((ROWS + 16) * groups, LANES), F32),
            pltpu.VMEM((groups, LANES, ROWS + 16), BF16),
            *[pltpu.VMEM((LANES, listed * LANES), F32)] * 4,
            pltpu.VMEM((4, LANES, LANES), F32),
            pltpu.VMEM((3 * groups, LANES), F32),
        ],
        compiler_params=limit,
    )(beads_listed, own, mass_sum, force, mass, label, leaving, hot, *sources)
    n = lax.axis_size("gx")
    if n == 2:
        arrivals = lax.ppermute(record, "gx", [(0, 1), (1, 0)])
    else:
        up = [(i, (i + 1) % n) for i in range(n)]
        down = [(j, i) for i, j in up]
        arrivals = jnp.stack(
            [lax.ppermute(record[0], "gx", up), lax.ppermute(record[1], "gx", down)]
        )
    return (forces.reshape(1, 1, 1, 3, atoms), arrivals[None, None, None])


def solution(mesh):
    cell = ("gx", "gy", "gz")
    placed = (
        P(*cell, None, None),
        P(*cell, None),
        P(*cell, None),
        P(*cell, None),
        P(*cell, None),
        P(*cell, None, None),
        P(*cell, None, None),
        P(*cell, None, None),
    )
    return jax.shard_map(
        per_device,
        mesh=mesh,
        in_specs=placed,
        out_specs=(P(*cell, None, None), P(*cell, None, None, None)),
        check_vma=False,
    )
```

```python
import functools
import itertools
import math

import jax
import jax.numpy as jnp
from jax import lax
from jax.experimental import pallas as pl
from jax.experimental.pallas import tpu as pltpu
from jax.sharding import PartitionSpec as P

SOFT_CORE = 0.01
EPS_COARSE = 2.0
SIGMA_SQ = 0.25
LANES = 128
ROWS = 32
PARTS = 4
F32, BF16 = jnp.float32, jnp.bfloat16
VMEM = pl.BlockSpec(memory_space=pltpu.VMEM)
HBM = pl.BlockSpec(memory_space=pltpu.HBM)
CONTRACT_LANES = (((1,), (1,)), ((), ()))


def split3(v):
    high = v.astype(BF16).astype(F32)
    rest = v - high
    mid = rest.astype(BF16).astype(F32)
    return high, mid, rest - mid


def far_rows(coords, soft):
    parts = [split3(v) for v in coords]
    norm = coords[0] * coords[0] + coords[1] * coords[1] + (coords[2] * coords[2] + soft)
    nh, nm, nl = split3(norm)
    one = jnp.ones_like(norm)
    rows = [p[0] for p in parts] + [p[1] for p in parts] + [nh, nm]
    return rows + [p[2] for p in parts] + [nl, one, one, one, jnp.zeros_like(one)]


def near_rows(coords, scale):
    parts = [[-2.0 * scale * part for part in split3(v)] for v in coords]
    norm = scale * (coords[0] * coords[0] + coords[1] * coords[1] + coords[2] * coords[2])
    one, zero = jnp.full_like(norm, scale), jnp.zeros_like(norm)
    h, m, l = ([p[k] for p in parts] for k in range(3))
    rows = h + h + [one, one] + m + m + [zero, zero] + l + l + [zero, zero]
    return rows + h + [one] + list(split3(norm)) + [zero]


def picked_rows(far, k, stride):
    first = far[pl.ds(k, 8, stride=stride), :]
    last = far[pl.ds(k + 8 * stride, 8, stride=stride), :]
    return jnp.concatenate([first, first, first, last], axis=0).astype(BF16)


def one_hot(label_ref, out_ref, tiles):
    ids = lax.broadcasted_iota(jnp.int32, (LANES, LANES), 0)
    for t in range(tiles):
        at = slice(t * LANES, (t + 1) * LANES)
        low = lax.rem(label_ref[:, at], LANES)
        out_ref[:, at] = jnp.where(ids == low, 1.0, 0.0).astype(BF16)


def high_mask(label, groups, repeat):
    ids = lax.broadcasted_iota(jnp.int32, (groups, label.shape[1]), 0)
    hit = (ids == label // LANES).astype(F32)
    return jnp.concatenate([hit] * repeat, axis=0)


def stacked3(v):
    return jnp.concatenate(list(split3(v)), axis=0).astype(BF16)


def fold3(v):
    n = v.shape[0] // 3
    return v[:n] + v[n : 2 * n] + v[2 * n :]


def gather_rows(table, label, hot, groups):
    features = table.shape[0] // groups
    picked = fold3(jnp.dot(stacked3(table), hot, preferred_element_type=F32))
    picked = picked * high_mask(label, groups, features)
    return [
        jnp.sum(picked[f * groups : (f + 1) * groups], axis=0, keepdims=True)
        for f in range(features)
    ]


def sum_rows(values, label, hot, groups):
    spread = jnp.concatenate([jnp.broadcast_to(v, (groups, v.shape[1])) for v in values], axis=0)
    spread = spread * high_mask(label, groups, len(values))
    return fold3(
        lax.dot_general(stacked3(spread), hot, CONTRACT_LANES, preferred_element_type=F32)
    )


def flat_row(ref, first, tiles):
    return jnp.concatenate([ref[first + t : first + t + 1, :] for t in range(tiles)], axis=1)


def signs_here():
    return [sign_of(axis) for axis in ("gx", "gy", "gz")]


def column_of(step):
    return 9 * (step[0] + 1) + 3 * (step[1] + 1) + (step[2] + 1)


def number_plan(tiles):
    bits = max((tiles - 1).bit_length(), 1)
    return bits, min(31 // bits, 9)


def place_of(step, tiles):
    bits, share = number_plan(tiles)
    order = 3 * (step[0] + 1) + (step[1] + 1)
    return -(-9 // share) * (step[2] + 1) + order // share, bits * (order % share)


def packed_numbers(lists, tiles):
    numbers = lists - tiles * lax.broadcasted_iota(jnp.int32, lists.shape, 1)
    for sign, width in zip(signs_here(), (9, 3, 1)):
        pieces = []
        for start in range(0, 27, 3 * width):
            for k in (2, 1, 0):
                pieces.append(numbers[:, start + k * width : start + (k + 1) * width])
        numbers = jnp.where(sign < 0, jnp.concatenate(pieces, axis=1), numbers)
    words = {}
    for x, y, z in itertools.product((-1, 0, 1), repeat=3):
        word, shift = place_of((x, y, z), tiles)
        column = column_of((x, y, z))
        piece = lax.shift_left(numbers[:, column : column + 1], jnp.int32(shift))
        words[word] = words[word] + piece if word in words else piece
    return jnp.concatenate([words[word] for word in sorted(words)], axis=1)


def as_float(step):
    return float(step) if isinstance(step, int) else step.astype(F32)


def pair_plan(tiles, count):
    held, ahead = (8, 6) if count == 1 else (8, 4) if count == 2 else (2, 1)
    unroll = max(held, 4)
    if tiles % unroll:
        held, unroll, ahead = 2, 2, 1
    return held, unroll, ahead


def prepare_kernel(
    label_in, mass_in, pos_in, weight_in, charge_in, lists_in, bead_lists_in, leaving_in,
    rows_out, mass_out, near_out, hot, label_ref, mass, lists_out, bead_lists_out, leaving_out,
    pos, weight, charge, near, sem,
):
    moves = [
        (label_in, label_ref), (mass_in, mass), (pos_in, pos), (weight_in, weight),
        (charge_in, charge), (lists_in, lists_out), (bead_lists_in, bead_lists_out),
        (leaving_in, leaving_out),
    ]
    copies = [pltpu.make_async_copy(a, b, sem.at[i]) for i, (a, b) in enumerate(moves)]
    for copy in copies:
        copy.start()
    beads = weight.shape[1]
    tiles, groups = pos.shape[0] // 3, beads // LANES
    copies[0].wait()
    one_hot(label_ref, hot, tiles)
    label = label_ref[...]
    copies[1].wait()
    copies[2].wait()
    m = mass[...]
    values = [m * flat_row(pos, k * tiles, tiles) for k in range(3)] + [m]
    sums = sum_rows(values, label, hot[...], groups)
    mass_sum = sums[3 * groups :]
    mass_out[...] = mass_sum
    for copy in copies[3:]:
        copy.wait()
    table = jnp.concatenate(
        [weight[:, g * LANES : (g + 1) * LANES] for g in range(groups)], axis=0
    )
    charged = charge[...] * gather_rows(table, label, hot[...], groups)[0]
    rows_out[: 3 * tiles, :] = pos[...]
    for t in range(tiles):
        at = slice(t * LANES, (t + 1) * LANES)
        rows_out[3 * tiles + t : 3 * tiles + t + 1, :] = charged[:, at]
    base = 4 * tiles
    for k in range(3):
        rows_out[base + k * groups : base + (k + 1) * groups, :] = (
            sums[k * groups : (k + 1) * groups] / mass_sum
        )
    rows_out[base + 3 * groups : base + 4 * groups, :] = table
    coords = [rows_out[k * tiles : (k + 1) * tiles, :] - 0.5 for k in range(3)]
    for r, row in enumerate(near_rows(coords, 1.0)):
        near[r * tiles : (r + 1) * tiles, :] = row
    for t in range(tiles):
        block = near[pl.ds(t, ROWS, stride=tiles), :]
        near_out[t] = block.T.astype(BF16)


def pair_kernel(tiles, groups, entries, sources, first, last, passed, *refs):
    numbers, own, near = refs[:3]
    cells = refs[3 : 3 + sources]
    rest = refs[3 + sources :]
    before = None if first else rest[0]
    rest = rest[0 if first else 1 :]
    for p in range(passed):
        rest[passed + 1 + p][...] = rest[p][...]
    rest = rest[passed : passed + 1] + rest[2 * passed + 1 :]
    if first:
        rest[1][...] = packed_numbers(numbers[...], tiles)
        numbers, rest = rest[1], rest[:1] + rest[2:]
    out, far, held = rest[:3]
    total = rest[-1] if last else None
    count = len(entries)
    height = 4 * (tiles + groups)
    signs = signs_here()
    places = []
    for e, (source, cell, steps) in enumerate(entries):
        step = [steps[k] * signs[k] if steps[k] else 0 for k in range(3)]
        places.append(place_of(steps, tiles))
        base = cell * height
        coords = [
            cells[source][base + k * tiles : base + (k + 1) * tiles, :]
            + (as_float(step[k]) - 0.5)
            for k in range(3)
        ]
        charged = cells[source][base + 3 * tiles : base + 4 * tiles, :]
        for r, row in enumerate(far_rows(coords, SOFT_CORE) + coords + [charged]):
            far[e, r * tiles : (r + 1) * tiles, :] = row

    bits = number_plan(tiles)[0]

    used = sorted({word for word, _ in places})

    def words_of(t):
        row = numbers[pl.ds(t, 1), :]
        return tuple(row[0, word] for word in used)

    def numbers_of(words):
        words = dict(zip(used, words))
        return [
            lax.bitwise_and(
                lax.shift_right_logical(words[word], jnp.int32(shift)), jnp.int32((1 << bits) - 1)
            )
            for word, shift in places
        ]

    def distances(t, into, ks, part=None):
        lhs = near[t]
        starts = list(range(0, count, 2))
        if part is not None:
            starts = starts[part::PARTS]
        for e in starts:
            members = range(e, min(e + 2, count))
            rhs = [
                picked_rows(far.at[m], ks[m], tiles) for m in members
            ]
            rhs = jnp.concatenate(rhs, axis=1) if len(rhs) > 1 else rhs[0]
            inv = lax.rsqrt(jnp.dot(lhs, rhs, preferred_element_type=F32))
            charged = [far[m, pl.ds(19 * tiles + ks[m], 1), :] for m in members]
            charged = jnp.concatenate(charged, axis=1) if len(charged) > 1 else charged[0]
            into[:, e * LANES : e * LANES + rhs.shape[1]] = inv * inv * inv * charged

    def strengths(t, dist, ks, part):
        block = LANES // PARTS
        at = slice(part * block, (part + 1) * block)
        if True:
            if before is None:
                acc = [jnp.zeros((block, LANES), F32)] * 4
            else:
                acc = [before[t, d, at, :] for d in range(4)]
            for e in range(count):
                k = ks[e]
                s = dist[at, e * LANES : (e + 1) * LANES]
                acc[3] = acc[3] + s
                for d in range(3):
                    acc[d] = acc[d] + s * far[e, pl.ds((16 + d) * tiles + k, 1), :]
            for d in range(4):
                if last:
                    total[d, at, :] = acc[d]
                else:
                    out[t, d, at, :] = acc[d]
        if not last or part < PARTS - 1:
            return
        sums = [jnp.sum(total[d].T, axis=0, keepdims=True) for d in range(4)]
        scale = own[pl.ds(3 * tiles + t, 1), :]
        for d in range(3):
            here = own[pl.ds(d * tiles + t, 1), :] - 0.5
            out[pl.ds(d * tiles + t, 1), :] = scale * (here * sums[3] - sums[d])

    buffered, unroll, ahead = pair_plan(tiles, count)
    buffers = [held.at[i] for i in range(buffered)]
    words = [words_of(min(i, tiles - 1)) for i in range(unroll + ahead)]
    for i in range(ahead):
        distances(i, buffers[i], numbers_of(words[i]))

    def some_tiles(step, words):
        following = [
            words_of(jnp.minimum(unroll * (step + 1) + ahead + u, tiles - 1)) for u in range(unroll)
        ]
        for u in range(unroll):
            t = unroll * step + u
            later = jnp.minimum(t + ahead, tiles - 1)
            ks, ks_later = numbers_of(words[u]), numbers_of(words[u + ahead])
            for part in range(PARTS):
                distances(later, buffers[(u + ahead) % buffered], ks_later, part)
                strengths(t, buffers[u % buffered], ks, part)
        return tuple(words[unroll:]) + tuple(following)

    lax.fori_loop(0, tiles // unroll, some_tiles, tuple(words))


def weight_rows(weight):
    h, m, l = split3(weight)
    return [h, h, h, m, m, l], [h, m, l, h, m, h]


def final_kernel(tiles, groups, entries, sources, *refs):
    lists_ref, own, mass_sum_ref, atomic, mass, label_ref, leave_ref, hot = refs[:8]
    cells = refs[8 : 8 + sources]
    rest = refs[8 + sources :]
    forces_out, record_out, leave_hot, raw, far, near, nearest = rest[:7]
    buffers, (total, coarse) = (rest[7:9], rest[9:11]), rest[11:]
    lists, listed = lists_ref[...], lists_ref.shape[1]
    height = 4 * (tiles + groups)
    signs = signs_here()
    every = len(entries) * groups
    for source, cell, steps in entries:
        step = [steps[k] * signs[k] if steps[k] else 0 for k in range(3)]
        column = column_of(step)
        base = cell * height + 4 * tiles
        for k in range(4):
            block = cells[source][base + k * groups : base + (k + 1) * groups, :]
            if k < 3:
                block = block + (as_float(step[k]) - 0.5)
            raw[k, pl.ds(column * groups, groups), :] = block
    scale = math.sqrt(math.log2(math.e) / SIGMA_SQ)
    coords = [raw[k] for k in range(3)]
    one, zero = jnp.ones_like(coords[0]), jnp.zeros_like(coords[0])
    plain = coords + weight_rows(raw[3])[0] + [one, zero]
    for r, row in enumerate(far_rows([scale * v for v in coords], 0.0) + plain):
        far[r * every : (r + 1) * every, :] = row
    base = 4 * tiles
    coords = [own[base + k * groups : base + (k + 1) * groups, :] - 0.5 for k in range(3)]
    own_weight = own[base + 3 * groups : base + 4 * groups, :]
    zero = jnp.zeros_like(own_weight)
    factors = [-EPS_COARSE * row for row in weight_rows(own_weight)[1]]
    factors += [zero + EPS_COARSE, zero] + [zero] * 8
    for r, row in enumerate(near_rows([scale * v for v in coords], -1.0) + factors):
        near[r * groups : (r + 1) * groups, :] = row
    for b in range(groups):
        nearest[b] = near[pl.ds(b, ROWS + 16, stride=groups), :].T.astype(BF16)

    def products(b, dist, factor):
        lhs = nearest[b]
        for e in range(0, listed, 2):
            members = [lists[b, m] for m in range(e, min(e + 2, listed))]
            at = slice(e * LANES, (e + len(members)) * LANES)
            rhs = jnp.concatenate([picked_rows(far, k, every) for k in members], axis=1)
            dist[:, at] = jnp.dot(lhs[:, :ROWS], rhs, preferred_element_type=F32)
            rhs = [far[pl.ds(k + 19 * every, 8, stride=every), :] for k in members]
            rhs = jnp.concatenate([jnp.concatenate([r, r], axis=0) for r in rhs], axis=1)
            factor[:, at] = jnp.dot(lhs[:, ROWS:], rhs.astype(BF16), preferred_element_type=F32)

    def strengths(b, dist, factor):
        block = 32
        for i in range(0, LANES, block):
            at = slice(i, i + block)
            acc = [jnp.zeros((block, LANES), F32)] * 4
            for e in range(listed):
                k = lists[b, e]
                lanes = slice(e * LANES, (e + 1) * LANES)
                s = jnp.exp2(dist[at, lanes]) * factor[at, lanes]
                acc[3] = acc[3] + s
                for d in range(3):
                    acc[d] = acc[d] + s * far[pl.ds((16 + d) * every + k, 1), :]
            for d in range(4):
                total[d, at, :] = acc[d]
        sums = [jnp.sum(total[d].T, axis=0, keepdims=True) for d in range(4)]
        for d in range(3):
            centre = own[base + d * groups + b : base + d * groups + b + 1, :] - 0.5
            coarse[d * groups + b : d * groups + b + 1, :] = centre * sums[3] - sums[d]

    products(0, *buffers[0])
    for b in range(groups):
        if b + 1 < groups:
            products(b + 1, *buffers[(b + 1) % 2])
        strengths(b, *buffers[b % 2])

    label = label_ref[...]
    mass_sum = mass_sum_ref[...]
    scaled = coarse[...] / jnp.concatenate([mass_sum] * 3, axis=0)
    spread = gather_rows(scaled, label, hot[...], groups)
    forces = []
    for d in range(3):
        forces.append(flat_row(atomic, d * tiles, tiles) + mass[...] * spread[d])
        for t in range(tiles):
            at = slice(t * LANES, (t + 1) * LANES)
            forces_out[d * tiles + t : d * tiles + t + 1, :] = forces[d][:, at]
    molecule = sum_rows(forces, label, hot[...], groups)
    table = jnp.concatenate(
        [own[base : base + 3 * groups, :], molecule, own_weight, mass_sum], axis=0
    )
    leavers = leave_ref.shape[1] // 2
    one_hot(leave_ref, leave_hot, leave_ref.shape[1] // LANES)
    picked = gather_rows(table, leave_ref[...], leave_hot[...], groups)
    for side, shift in ((0, -1.0), (1, 1.0)):
        for f in range(8):
            row = picked[f][:, side * leavers : (side + 1) * leavers]
            record_out[side, f : f + 1, :] = row + shift if f == 0 else row


def exchange(x, axis):
    n = lax.axis_size(axis)
    if n == 1:
        return [(x, 1), (x, -1)]
    if n == 2:
        other = lax.ppermute(x, axis, [(0, 1), (1, 0)])
        return [(other, 1), (other, -1)]
    if n % 2 == 0:
        inner = [(i, i ^ 1) for i in range(n)]
        outer = [(i, ((i + 1) ^ 1) - 1) for i in range(n)]
        outer = [(i, (j + n) % n) for i, j in outer]
        second = lax.ppermute(x, axis, outer)
        first = lax.ppermute(x, axis, inner)
        return [(first, 1), (second, -1)]
    up = [(i, (i + 1) % n) for i in range(n)]
    down = [(j, i) for i, j in up]
    return [(lax.ppermute(x, axis, down), 1), (lax.ppermute(x, axis, up), -1)]


def sign_of(axis):
    n = lax.axis_size(axis)
    if n > 2 and n % 2 == 0:
        return 1 - 2 * lax.rem(lax.axis_index(axis), 2)
    return jnp.int32(1)


def per_device(positions, charges, masses, weights, mapping, atom_lists, bead_lists, leaving):
    atoms, beads = positions.shape[4], weights.shape[3]
    tiles, groups = atoms // LANES, beads // LANES
    pos = positions.reshape(3 * tiles, LANES)
    charge, mass = charges[0, 0], masses[0, 0]
    weight, label = weights[0, 0], mapping[0, 0]
    leavers = leaving.shape[4]
    height = 4 * (tiles + groups)
    limit = pltpu.CompilerParams(vmem_limit_bytes=48 * 2**20)
    inputs = [
        label, mass, pos, weight, charge,
        atom_lists[0, 0, 0], bead_lists[0, 0, 0], leaving.reshape(1, 2 * leavers),
    ]

    def like(x):
        return jax.ShapeDtypeStruct(x.shape, x.dtype)

    own, mass_sum, near, hot, label, mass, lists, *small = pl.pallas_call(
        prepare_kernel,
        out_shape=(
            jax.ShapeDtypeStruct((height, LANES), F32),
            jax.ShapeDtypeStruct((groups, LANES), F32),
            jax.ShapeDtypeStruct((tiles, LANES, ROWS), BF16),
            jax.ShapeDtypeStruct((LANES, atoms), BF16),
            like(label),
            like(mass),
            *[like(x) for x in inputs[5:]],
        ),
        in_specs=[HBM] * 8,
        out_specs=(VMEM,) * 9,
        scratch_shapes=[
            *[pltpu.VMEM(x.shape, x.dtype) for x in inputs[2:5]],
            pltpu.VMEM((ROWS * tiles, LANES), F32),
            pltpu.SemaphoreType.DMA((8,)),
        ],
        compiler_params=pltpu.CompilerParams(vmem_limit_bytes=48 * 2**20),
    )(*[pltpu.with_memory_space_constraint(x, pltpu.HBM) for x in inputs])

    def pairs(lists, entries, cells, before, last=False, passed=()):
        count = len(entries)
        args = [lists, own, near, *cells] + ([] if before is None else [before])
        place = len(args) - 1
        args += passed
        words = jax.ShapeDtypeStruct((tiles, 3 * -(-9 // number_plan(tiles)[1])), jnp.int32)
        extra = [*passed, words] if before is None else passed
        shape = (3 * tiles, LANES) if last else (tiles, 4, LANES, LANES)
        work = tiles * count * LANES * LANES
        return pl.pallas_call(
            functools.partial(
                pair_kernel, tiles, groups, entries, len(cells), before is None, last, len(passed)
            ),
            out_shape=(jax.ShapeDtypeStruct(shape, F32), *[like(x) for x in extra]),
            in_specs=[VMEM] * len(args),
            out_specs=(VMEM,) * (1 + len(extra)),
            scratch_shapes=[
                pltpu.VMEM((count, 20 * tiles, LANES), F32),
                pltpu.VMEM((pair_plan(tiles, count)[0], LANES, count * LANES), F32),
            ]
            + ([pltpu.VMEM((4, LANES, LANES), F32)] if last else []),
            input_output_aliases={} if last or before is None else {place: 0},
            compiler_params=limit,
            cost_estimate=pl.CostEstimate(
                flops=60 * work, bytes_accessed=4 * height * LANES, transcendentals=work
            ),
        )(*args)

    with_y = exchange(own, "gy")
    force, lists = pairs(lists, [(0, 0, (0, 0, 0))], [own], None)
    column = jnp.concatenate([own] + [block for block, _ in with_y], axis=0)
    column, force = lax.optimization_barrier((column, force))
    y_steps = [0] + [step for _, step in with_y]
    with_x = exchange(column, "gx")
    entries = [(0, c, (0, y_steps[c], 0)) for c in (1, 2)]
    force, beads_listed, leaving = pairs(lists, entries, [column], force, passed=small)
    plane_cells = [(c, (0, y_steps[c])) for c in range(3)]
    if lax.axis_size("gx") <= 2:
        plane = jnp.concatenate([column, with_x[0][0]], axis=0)
        plane_cells += [(3 + c, (x, y_steps[c])) for c in range(3) for x in (1, -1)]
    else:
        plane = jnp.concatenate([column] + [block for block, _ in with_x], axis=0)
        plane_cells += [
            (3 + 3 * k + c, (with_x[k][1], y_steps[c])) for c in range(3) for k in range(2)
        ]
    plane, force = lax.optimization_barrier((plane, force))
    with_z = exchange(plane, "gz")
    entries = [(0, c, (x, y, 0)) for c, (x, y) in plane_cells[3:]]
    force = pairs(lists, entries, [plane], force)[0]
    for place, (block, z) in enumerate(with_z):
        entries = [(0, c, (x, y, z)) for c, (x, y) in plane_cells]
        force = pairs(lists, entries, [block], force, place == 1)[0]

    sources = [plane] + [block for block, _ in with_z]
    z_steps = [0] + [step for _, step in with_z]
    entries = [(s, c, (x, y, z_steps[s])) for s in range(3) for c, (x, y) in plane_cells]
    every, listed = len(entries) * groups, beads_listed.shape[1]
    forces, record = pl.pallas_call(
        functools.partial(final_kernel, tiles, groups, entries, len(sources)),
        out_shape=(
            jax.ShapeDtypeStruct((3 * tiles, LANES), F32),
            jax.ShapeDtypeStruct((2, 8, leavers), F32),
        ),
        in_specs=[VMEM] * (8 + len(sources)),
        out_specs=(VMEM, VMEM),
        scratch_shapes=[
            pltpu.VMEM((LANES, 2 * leavers), BF16),
            pltpu.VMEM((4, every, LANES), F32),
            pltpu.VMEM((27 * every, LANES), F32),
            pltpu.VMEM(((ROWS + 16) * groups, LANES), F32),
            pltpu.VMEM((groups, LANES, ROWS + 16), BF16),
            *[pltpu.VMEM((LANES, listed * LANES), F32)] * 4,
            pltpu.VMEM((4, LANES, LANES), F32),
            pltpu.VMEM((3 * groups, LANES), F32),
        ],
        compiler_params=limit,
    )(beads_listed, own, mass_sum, force, mass, label, leaving, hot, *sources)
    n = lax.axis_size("gx")
    if n == 2:
        arrivals = lax.ppermute(record, "gx", [(0, 1), (1, 0)])
    else:
        up = [(i, (i + 1) % n) for i in range(n)]
        down = [(j, i) for i, j in up]
        arrivals = jnp.stack(
            [lax.ppermute(record[0], "gx", up), lax.ppermute(record[1], "gx", down)]
        )
    return (forces.reshape(1, 1, 1, 3, atoms), arrivals[None, None, None])


def solution(mesh):
    cell = ("gx", "gy", "gz")
    placed = (
        P(*cell, None, None),
        P(*cell, None),
        P(*cell, None),
        P(*cell, None),
        P(*cell, None),
        P(*cell, None, None),
        P(*cell, None, None),
        P(*cell, None, None),
    )
    return jax.shard_map(
        per_device,
        mesh=mesh,
        in_specs=placed,
        out_specs=(P(*cell, None, None), P(*cell, None, None, None)),
        check_vma=False,
    )
```

```python
import functools
import itertools
import math

import jax
import jax.numpy as jnp
from jax import lax
from jax.experimental import pallas as pl
from jax.experimental.pallas import tpu as pltpu
from jax.sharding import PartitionSpec as P

SOFT_CORE = 0.01
EPS_COARSE = 2.0
SIGMA_SQ = 0.25
LANES = 128
ROWS = 32
PARTS = 4
F32, BF16 = jnp.float32, jnp.bfloat16
VMEM = pl.BlockSpec(memory_space=pltpu.VMEM)
HBM = pl.BlockSpec(memory_space=pltpu.HBM)
CONTRACT_LANES = (((1,), (1,)), ((), ()))


def split3(v):
    high = v.astype(BF16).astype(F32)
    rest = v - high
    mid = rest.astype(BF16).astype(F32)
    return high, mid, rest - mid


def far_rows(coords, soft):
    parts = [split3(v) for v in coords]
    norm = coords[0] * coords[0] + coords[1] * coords[1] + (coords[2] * coords[2] + soft)
    nh, nm, nl = split3(norm)
    one = jnp.ones_like(norm)
    rows = [p[0] for p in parts] + [p[1] for p in parts] + [nh, nm]
    return rows + [p[2] for p in parts] + [nl, one, one, one, jnp.zeros_like(one)]


def near_rows(coords, scale):
    parts = [[-2.0 * scale * part for part in split3(v)] for v in coords]
    norm = scale * (coords[0] * coords[0] + coords[1] * coords[1] + coords[2] * coords[2])
    one, zero = jnp.full_like(norm, scale), jnp.zeros_like(norm)
    h, m, l = ([p[k] for p in parts] for k in range(3))
    rows = h + h + [one, one] + m + m + [zero, zero] + l + l + [zero, zero]
    return rows + h + [one] + list(split3(norm)) + [zero]


def picked_rows(far, k, stride):
    first = far[pl.ds(k, 8, stride=stride), :]
    last = far[pl.ds(k + 8 * stride, 8, stride=stride), :]
    return jnp.concatenate([first, first, first, last], axis=0).astype(BF16)


def one_hot(label_ref, out_ref, tiles):
    ids = lax.broadcasted_iota(jnp.int32, (LANES, LANES), 0)
    for t in range(tiles):
        at = slice(t * LANES, (t + 1) * LANES)
        low = lax.rem(label_ref[:, at], LANES)
        out_ref[:, at] = jnp.where(ids == low, 1.0, 0.0).astype(BF16)


def high_mask(label, groups, repeat):
    ids = lax.broadcasted_iota(jnp.int32, (groups, label.shape[1]), 0)
    hit = (ids == label // LANES).astype(F32)
    return jnp.concatenate([hit] * repeat, axis=0)


def stacked3(v):
    return jnp.concatenate(list(split3(v)), axis=0).astype(BF16)


def fold3(v):
    n = v.shape[0] // 3
    return v[:n] + v[n : 2 * n] + v[2 * n :]


def gather_rows(table, label, hot, groups):
    features = table.shape[0] // groups
    picked = fold3(jnp.dot(stacked3(table), hot, preferred_element_type=F32))
    picked = picked * high_mask(label, groups, features)
    return [
        jnp.sum(picked[f * groups : (f + 1) * groups], axis=0, keepdims=True)
        for f in range(features)
    ]


def sum_rows(values, label, hot, groups):
    spread = jnp.concatenate([jnp.broadcast_to(v, (groups, v.shape[1])) for v in values], axis=0)
    spread = spread * high_mask(label, groups, len(values))
    return fold3(
        lax.dot_general(stacked3(spread), hot, CONTRACT_LANES, preferred_element_type=F32)
    )


def flat_row(ref, first, tiles):
    return jnp.concatenate([ref[first + t : first + t + 1, :] for t in range(tiles)], axis=1)


def signs_here():
    return [sign_of(axis) for axis in ("gx", "gy", "gz")]


def column_of(step):
    return 9 * (step[0] + 1) + 3 * (step[1] + 1) + (step[2] + 1)


def number_plan(tiles):
    bits = max((tiles - 1).bit_length(), 1)
    return bits, min(31 // bits, 9)


def place_of(step, tiles):
    bits, share = number_plan(tiles)
    order = 3 * (step[0] + 1) + (step[1] + 1)
    return -(-9 // share) * (step[2] + 1) + order // share, bits * (order % share)


def packed_numbers(lists, tiles):
    numbers = lists - tiles * lax.broadcasted_iota(jnp.int32, lists.shape, 1)
    for sign, width in zip(signs_here(), (9, 3, 1)):
        pieces = []
        for start in range(0, 27, 3 * width):
            for k in (2, 1, 0):
                pieces.append(numbers[:, start + k * width : start + (k + 1) * width])
        numbers = jnp.where(sign < 0, jnp.concatenate(pieces, axis=1), numbers)
    words = {}
    for x, y, z in itertools.product((-1, 0, 1), repeat=3):
        word, shift = place_of((x, y, z), tiles)
        column = column_of((x, y, z))
        piece = lax.shift_left(numbers[:, column : column + 1], jnp.int32(shift))
        words[word] = words[word] + piece if word in words else piece
    return jnp.concatenate([words[word] for word in sorted(words)], axis=1)


def as_float(step):
    return float(step) if isinstance(step, int) else step.astype(F32)


def pair_plan(tiles, count):
    held, ahead = (8, 6) if count == 1 else (8, 4) if count == 2 else (2, 1)
    unroll = max(held, 4)
    if tiles % unroll:
        held, unroll, ahead = 2, 2, 1
    return held, unroll, ahead


def prepare_kernel(
    label_in, mass_in, pos_in, weight_in, charge_in, lists_in, bead_lists_in, leaving_in,
    rows_out, mass_out, hot, label_ref, mass, lists_out, bead_lists_out, leaving_out,
    pos, weight, charge, sem,
):
    moves = [
        (label_in, label_ref), (mass_in, mass), (pos_in, pos), (weight_in, weight),
        (charge_in, charge), (lists_in, lists_out), (bead_lists_in, bead_lists_out),
        (leaving_in, leaving_out),
    ]
    copies = [pltpu.make_async_copy(a, b, sem.at[i]) for i, (a, b) in enumerate(moves)]
    for copy in copies:
        copy.start()
    beads = weight.shape[1]
    tiles, groups = pos.shape[0] // 3, beads // LANES
    copies[0].wait()
    one_hot(label_ref, hot, tiles)
    label = label_ref[...]
    copies[1].wait()
    copies[2].wait()
    m = mass[...]
    values = [m * flat_row(pos, k * tiles, tiles) for k in range(3)] + [m]
    sums = sum_rows(values, label, hot[...], groups)
    mass_sum = sums[3 * groups :]
    mass_out[...] = mass_sum
    for copy in copies[3:]:
        copy.wait()
    table = jnp.concatenate(
        [weight[:, g * LANES : (g + 1) * LANES] for g in range(groups)], axis=0
    )
    charged = charge[...] * gather_rows(table, label, hot[...], groups)[0]
    rows_out[: 3 * tiles, :] = pos[...]
    for t in range(tiles):
        at = slice(t * LANES, (t + 1) * LANES)
        rows_out[3 * tiles + t : 3 * tiles + t + 1, :] = charged[:, at]
    base = 4 * tiles
    for k in range(3):
        rows_out[base + k * groups : base + (k + 1) * groups, :] = (
            sums[k * groups : (k + 1) * groups] / mass_sum
        )
    rows_out[base + 3 * groups : base + 4 * groups, :] = table


def pair_kernel(tiles, groups, entries, sources, first, last, *refs):
    numbers, own = refs[:2]
    near = None if first else refs[2]
    refs = refs[2 if first else 3 :]
    cells = refs[:sources]
    rest = refs[sources:]
    before = None if first else rest[0]
    rest = rest[0 if first else 1 :]
    if first:
        rest[1][...] = packed_numbers(numbers[...], tiles)
        numbers, near, rest = rest[1], rest[2], rest[:1] + rest[3:]
        coords = [own[k * tiles : (k + 1) * tiles, :] - 0.5 for k in range(3)]
        for r, row in enumerate(near_rows(coords, 1.0)):
            rest[-1][r * tiles : (r + 1) * tiles, :] = row
        for t in range(tiles):
            near[t] = rest[-1][pl.ds(t, ROWS, stride=tiles), :].T.astype(BF16)
    out, far, held = rest[:3]
    total = rest[-1] if last else None
    count = len(entries)
    height = 4 * (tiles + groups)
    signs = signs_here()
    places = []
    for e, (source, cell, steps) in enumerate(entries):
        step = [steps[k] * signs[k] if steps[k] else 0 for k in range(3)]
        places.append(place_of(steps, tiles))
        base = cell * height
        coords = [
            cells[source][base + k * tiles : base + (k + 1) * tiles, :]
            + (as_float(step[k]) - 0.5)
            for k in range(3)
        ]
        charged = cells[source][base + 3 * tiles : base + 4 * tiles, :]
        for r, row in enumerate(far_rows(coords, SOFT_CORE) + coords + [charged]):
            far[e, r * tiles : (r + 1) * tiles, :] = row

    bits = number_plan(tiles)[0]

    used = sorted({word for word, _ in places})

    def words_of(t):
        row = numbers[pl.ds(t, 1), :]
        return tuple(row[0, word] for word in used)

    def numbers_of(words):
        words = dict(zip(used, words))
        return [
            lax.bitwise_and(
                lax.shift_right_logical(words[word], jnp.int32(shift)), jnp.int32((1 << bits) - 1)
            )
            for word, shift in places
        ]

    def distances(t, into, ks, part=None):
        lhs = near[t]
        starts = list(range(0, count, 2))
        if part is not None:
            starts = starts[part::PARTS]
        for e in starts:
            members = range(e, min(e + 2, count))
            rhs = [
                picked_rows(far.at[m], ks[m], tiles) for m in members
            ]
            rhs = jnp.concatenate(rhs, axis=1) if len(rhs) > 1 else rhs[0]
            inv = lax.rsqrt(jnp.dot(lhs, rhs, preferred_element_type=F32))
            charged = [far[m, pl.ds(19 * tiles + ks[m], 1), :] for m in members]
            charged = jnp.concatenate(charged, axis=1) if len(charged) > 1 else charged[0]
            into[:, e * LANES : e * LANES + rhs.shape[1]] = inv * inv * inv * charged

    def strengths(t, dist, ks, part):
        block = LANES // PARTS
        at = slice(part * block, (part + 1) * block)
        if True:
            if before is None:
                acc = [jnp.zeros((block, LANES), F32)] * 4
            else:
                acc = [before[t, d, at, :] for d in range(4)]
            for e in range(count):
                k = ks[e]
                s = dist[at, e * LANES : (e + 1) * LANES]
                acc[3] = acc[3] + s
                for d in range(3):
                    acc[d] = acc[d] + s * far[e, pl.ds((16 + d) * tiles + k, 1), :]
            for d in range(4):
                if last:
                    total[d, at, :] = acc[d]
                else:
                    out[t, d, at, :] = acc[d]
        if not last or part < PARTS - 1:
            return
        sums = [jnp.sum(total[d].T, axis=0, keepdims=True) for d in range(4)]
        scale = own[pl.ds(3 * tiles + t, 1), :]
        for d in range(3):
            here = own[pl.ds(d * tiles + t, 1), :] - 0.5
            out[pl.ds(d * tiles + t, 1), :] = scale * (here * sums[3] - sums[d])

    buffered, unroll, ahead = pair_plan(tiles, count)
    buffers = [held.at[i] for i in range(buffered)]
    words = [words_of(min(i, tiles - 1)) for i in range(unroll + ahead)]
    for i in range(ahead):
        distances(i, buffers[i], numbers_of(words[i]))

    def some_tiles(step, words):
        following = [
            words_of(jnp.minimum(unroll * (step + 1) + ahead + u, tiles - 1)) for u in range(unroll)
        ]
        for u in range(unroll):
            t = unroll * step + u
            later = jnp.minimum(t + ahead, tiles - 1)
            ks, ks_later = numbers_of(words[u]), numbers_of(words[u + ahead])
            for part in range(PARTS):
                distances(later, buffers[(u + ahead) % buffered], ks_later, part)
                strengths(t, buffers[u % buffered], ks, part)
        return tuple(words[unroll:]) + tuple(following)

    lax.fori_loop(0, tiles // unroll, some_tiles, tuple(words))


def weight_rows(weight):
    h, m, l = split3(weight)
    return [h, h, h, m, m, l], [h, m, l, h, m, h]


def final_kernel(tiles, groups, entries, sources, *refs):
    lists_ref, own, mass_sum_ref, atomic, mass, label_ref, leave_ref, hot = refs[:8]
    cells = refs[8 : 8 + sources]
    rest = refs[8 + sources :]
    forces_out, record_out, leave_hot, raw, far, near, nearest = rest[:7]
    buffers, (total, coarse) = rest[7:9], rest[9:]
    lists, listed = lists_ref[...], lists_ref.shape[1]
    height = 4 * (tiles + groups)
    signs = signs_here()
    every = len(entries) * groups
    for source, cell, steps in entries:
        step = [steps[k] * signs[k] if steps[k] else 0 for k in range(3)]
        column = column_of(step)
        base = cell * height + 4 * tiles
        for k in range(4):
            block = cells[source][base + k * groups : base + (k + 1) * groups, :]
            if k < 3:
                block = block + (as_float(step[k]) - 0.5)
            raw[k, pl.ds(column * groups, groups), :] = block
    scale = math.sqrt(math.log2(math.e) / SIGMA_SQ)
    coords = [raw[k] for k in range(3)]
    one, zero = jnp.ones_like(coords[0]), jnp.zeros_like(coords[0])
    plain = coords + weight_rows(raw[3])[0] + [one, zero]
    for r, row in enumerate(far_rows([scale * v for v in coords], 0.0) + plain):
        far[r * every : (r + 1) * every, :] = row
    base = 4 * tiles
    coords = [own[base + k * groups : base + (k + 1) * groups, :] - 0.5 for k in range(3)]
    own_weight = own[base + 3 * groups : base + 4 * groups, :]
    zero = jnp.zeros_like(own_weight)
    factors = [-EPS_COARSE * row for row in weight_rows(own_weight)[1]]
    factors += [zero + EPS_COARSE, zero] + [zero] * 8
    for r, row in enumerate(near_rows([scale * v for v in coords], -1.0) + factors):
        near[r * groups : (r + 1) * groups, :] = row
    for b in range(groups):
        nearest[b] = near[pl.ds(b, ROWS + 16, stride=groups), :].T.astype(BF16)

    def products(b, into):
        lhs = nearest[b]
        for e in range(0, listed, 2):
            members = [lists[b, m] for m in range(e, min(e + 2, listed))]
            rhs = jnp.concatenate([picked_rows(far, k, every) for k in members], axis=1)
            dist = jnp.dot(lhs[:, :ROWS], rhs, preferred_element_type=F32)
            rhs = [far[pl.ds(k + 19 * every, 8, stride=every), :] for k in members]
            rhs = jnp.concatenate([jnp.concatenate([r, r], axis=0) for r in rhs], axis=1)
            factor = jnp.dot(lhs[:, ROWS:], rhs.astype(BF16), preferred_element_type=F32)
            into[:, e * LANES : (e + len(members)) * LANES] = jnp.exp2(dist) * factor

    def strengths(b, held):
        block = LANES // PARTS
        for part in range(PARTS):
            at = slice(part * block, (part + 1) * block)
            acc = [jnp.zeros((block, LANES), F32)] * 4
            for e in range(listed):
                k = lists[b, e]
                s = held[at, e * LANES : (e + 1) * LANES]
                acc[3] = acc[3] + s
                for d in range(3):
                    acc[d] = acc[d] + s * far[pl.ds((16 + d) * every + k, 1), :]
            for d in range(4):
                total[d, at, :] = acc[d]
        sums = [jnp.sum(total[d].T, axis=0, keepdims=True) for d in range(4)]
        for d in range(3):
            centre = own[base + d * groups + b : base + d * groups + b + 1, :] - 0.5
            coarse[d * groups + b : d * groups + b + 1, :] = centre * sums[3] - sums[d]

    products(0, buffers[0])
    for b in range(groups):
        if b + 1 < groups:
            products(b + 1, buffers[(b + 1) % 2])
        strengths(b, buffers[b % 2])

    label = label_ref[...]
    mass_sum = mass_sum_ref[...]
    scaled = coarse[...] / jnp.concatenate([mass_sum] * 3, axis=0)
    spread = gather_rows(scaled, label, hot[...], groups)
    forces = []
    for d in range(3):
        forces.append(flat_row(atomic, d * tiles, tiles) + mass[...] * spread[d])
        for t in range(tiles):
            at = slice(t * LANES, (t + 1) * LANES)
            forces_out[d * tiles + t : d * tiles + t + 1, :] = forces[d][:, at]
    molecule = sum_rows(forces, label, hot[...], groups)
    table = jnp.concatenate(
        [own[base : base + 3 * groups, :], molecule, own_weight, mass_sum], axis=0
    )
    leavers = leave_ref.shape[1] // 2
    one_hot(leave_ref, leave_hot, leave_ref.shape[1] // LANES)
    picked = gather_rows(table, leave_ref[...], leave_hot[...], groups)
    for side, shift in ((0, -1.0), (1, 1.0)):
        for f in range(8):
            row = picked[f][:, side * leavers : (side + 1) * leavers]
            record_out[side, f : f + 1, :] = row + shift if f == 0 else row


def moves(axis):
    n = lax.axis_size(axis)
    if n <= 2:
        return [([n - 1 - i for i in range(n)], (1, -1))]
    if n % 2 == 0:
        inner = [i ^ 1 for i in range(n)]
        return [([(((i + 1) ^ 1) - 1) % n for i in range(n)], (-1,)), (inner, (1,))]
    return [([(i + 1) % n for i in range(n)], (-1,)), ([(i - 1) % n for i in range(n)], (1,))]


def exchange(x, axis):
    return [
        (lax.ppermute(x, axis, list(enumerate(receivers))), steps)
        for receivers, steps in moves(axis)
    ]


def exchange_plane(x, first, second):
    sizes = lax.axis_size(first), lax.axis_size(second)
    still = [(list(range(n)), (0,)) for n in sizes]
    blocks = []
    for to_b, steps_b in moves(second) + [still[1]]:
        for to_a, steps_a in [still[0]] + moves(first):
            steps = [(p, q) for p in steps_a for q in steps_b]
            if steps == [(0, 0)]:
                continue
            pairs = [
                (a * sizes[1] + b, to_a[a] * sizes[1] + to_b[b])
                for a in range(sizes[0])
                for b in range(sizes[1])
            ]
            blocks.append((lax.ppermute(x, (first, second), pairs), steps))
    return blocks


def sign_of(axis):
    n = lax.axis_size(axis)
    if n > 2 and n % 2 == 0:
        return 1 - 2 * lax.rem(lax.axis_index(axis), 2)
    return jnp.int32(1)


def per_device(positions, charges, masses, weights, mapping, atom_lists, bead_lists, leaving):
    atoms, beads = positions.shape[4], weights.shape[3]
    tiles, groups = atoms // LANES, beads // LANES
    pos = positions.reshape(3 * tiles, LANES)
    charge, mass = charges[0, 0], masses[0, 0]
    weight, label = weights[0, 0], mapping[0, 0]
    leavers = leaving.shape[4]
    height = 4 * (tiles + groups)
    limit = pltpu.CompilerParams(vmem_limit_bytes=48 * 2**20)
    inputs = [
        label, mass, pos, weight, charge,
        atom_lists[0, 0, 0], bead_lists[0, 0, 0], leaving.reshape(1, 2 * leavers),
    ]

    def like(x):
        return jax.ShapeDtypeStruct(x.shape, x.dtype)

    own, mass_sum, hot, label, mass, lists, *small = pl.pallas_call(
        prepare_kernel,
        out_shape=(
            jax.ShapeDtypeStruct((height, LANES), F32),
            jax.ShapeDtypeStruct((groups, LANES), F32),
            jax.ShapeDtypeStruct((LANES, atoms), BF16),
            like(label),
            like(mass),
            *[like(x) for x in inputs[5:]],
        ),
        in_specs=[HBM] * 8,
        out_specs=(VMEM,) * 8,
        scratch_shapes=[
            *[pltpu.VMEM(x.shape, x.dtype) for x in inputs[2:5]],
            pltpu.SemaphoreType.DMA((8,)),
        ],
        compiler_params=pltpu.CompilerParams(vmem_limit_bytes=48 * 2**20),
    )(*[pltpu.with_memory_space_constraint(x, pltpu.HBM) for x in inputs])

    def pairs(lists, near, entries, cells, before, last=False):
        count = len(entries)
        first = before is None
        args = [lists, own, *cells] if first else [lists, own, near, *cells, before]
        place = len(args) - 1
        words = jax.ShapeDtypeStruct((tiles, 3 * -(-9 // number_plan(tiles)[1])), jnp.int32)
        points = jax.ShapeDtypeStruct((tiles, LANES, ROWS), BF16)
        extra = [words, points] if first else []
        shape = (3 * tiles, LANES) if last else (tiles, 4, LANES, LANES)
        work = tiles * count * LANES * LANES
        return pl.pallas_call(
            functools.partial(
                pair_kernel, tiles, groups, entries, len(cells), before is None, last
            ),
            out_shape=(jax.ShapeDtypeStruct(shape, F32), *extra),
            in_specs=[VMEM] * len(args),
            out_specs=(VMEM,) * (1 + len(extra)),
            scratch_shapes=[
                pltpu.VMEM((count, 20 * tiles, LANES), F32),
                pltpu.VMEM((pair_plan(tiles, count)[0], LANES, count * LANES), F32),
            ]
            + ([pltpu.VMEM((4, LANES, LANES), F32)] if last else [])
            + ([pltpu.VMEM((ROWS * tiles, LANES), F32)] if first else []),
            input_output_aliases={} if last or before is None else {place: 0},
            compiler_params=limit,
            cost_estimate=pl.CostEstimate(
                flops=60 * work, bytes_accessed=4 * height * LANES, transcendentals=work
            ),
        )(*args)

    with_x = exchange(own, "gx")
    force, lists, near = pairs(lists, None, [(0, 0, (0, 0, 0))], [own], None)
    column = jnp.concatenate([own] + [block for block, _ in with_x], axis=0)
    column, force = lax.optimization_barrier((column, force))
    cells = [(0, 0)] + [(c + 1, x) for c, (_, steps) in enumerate(with_x) for x in steps]
    with_y = exchange(column, "gy")[::-1]
    entries = [(0, c, (x, 0, 0)) for c, x in cells[1:]]
    force = pairs(lists, near, entries, [column], force)[0]
    near_y, far_y = with_y[:1], with_y[1:]
    if far_y:
        entries = [(0, c, (x, y, 0)) for y in near_y[0][1] for c, x in cells]
        force = pairs(lists, near, entries, [near_y[0][0]], force)[0]
    plane = jnp.concatenate([column] + [block for block, _ in with_y], axis=0)
    plane, force = lax.optimization_barrier((plane, force))
    held = 1 + len(with_x)
    plane_cells = [(c, (x, 0)) for c, x in cells]
    plane_cells += [
        (held * (k + 1) + c, (x, y))
        for k, (_, steps) in enumerate(with_y)
        for y in steps
        for c, x in cells
    ]
    with_z = [(block, z) for block, steps in exchange(plane, "gz") for z in steps][::-1]
    left = far_y[0][1] if far_y else near_y[0][1]
    entries = [(0, c, (x, y, 0)) for c, (x, y) in plane_cells if y in left]
    force = pairs(lists, near, entries, [plane], force)[0]
    for place, (block, z) in enumerate(with_z):
        entries = [(0, c, (x, y, z)) for c, (x, y) in plane_cells]
        force = pairs(lists, near, entries, [block], force, place == 1)[0]

    sources = [plane] + [block for block, _ in with_z]
    z_steps = [0] + [step for _, step in with_z]
    entries = [(s, c, (x, y, z_steps[s])) for s in range(3) for c, (x, y) in plane_cells]
    every, listed = len(entries) * groups, small[0].shape[1]
    forces, record = pl.pallas_call(
        functools.partial(final_kernel, tiles, groups, entries, len(sources)),
        out_shape=(
            jax.ShapeDtypeStruct((3 * tiles, LANES), F32),
            jax.ShapeDtypeStruct((2, 8, leavers), F32),
        ),
        in_specs=[VMEM] * (8 + len(sources)),
        out_specs=(VMEM, VMEM),
        scratch_shapes=[
            pltpu.VMEM((LANES, 2 * leavers), BF16),
            pltpu.VMEM((4, every, LANES), F32),
            pltpu.VMEM((27 * every, LANES), F32),
            pltpu.VMEM(((ROWS + 16) * groups, LANES), F32),
            pltpu.VMEM((groups, LANES, ROWS + 16), BF16),
            *[pltpu.VMEM((LANES, listed * LANES), F32)] * 2,
            pltpu.VMEM((4, LANES, LANES), F32),
            pltpu.VMEM((3 * groups, LANES), F32),
        ],
        compiler_params=limit,
    )(small[0], own, mass_sum, force, mass, label, small[1], hot, *sources)
    n = lax.axis_size("gx")
    if n == 2:
        arrivals = lax.ppermute(record, "gx", [(0, 1), (1, 0)])
    else:
        up = [(i, (i + 1) % n) for i in range(n)]
        down = [(j, i) for i, j in up]
        arrivals = jnp.stack(
            [lax.ppermute(record[0], "gx", up), lax.ppermute(record[1], "gx", down)]
        )
    return (forces.reshape(1, 1, 1, 3, atoms), arrivals[None, None, None])


def solution(mesh):
    cell = ("gx", "gy", "gz")
    placed = (
        P(*cell, None, None),
        P(*cell, None),
        P(*cell, None),
        P(*cell, None),
        P(*cell, None),
        P(*cell, None, None),
        P(*cell, None, None),
        P(*cell, None, None),
    )
    return jax.shard_map(
        per_device,
        mesh=mesh,
        in_specs=placed,
        out_specs=(P(*cell, None, None), P(*cell, None, None, None)),
        check_vma=False,
    )
```

```python
import functools
import itertools
import math

import jax
import jax.numpy as jnp
from jax import lax
from jax.experimental import pallas as pl
from jax.experimental.pallas import tpu as pltpu
from jax.sharding import PartitionSpec as P

SOFT_CORE = 0.01
EPS_COARSE = 2.0
SIGMA_SQ = 0.25
LANES = 128
ROWS = 32
PARTS = 4
F32, BF16 = jnp.float32, jnp.bfloat16
VMEM = pl.BlockSpec(memory_space=pltpu.VMEM)
HBM = pl.BlockSpec(memory_space=pltpu.HBM)
CONTRACT_LANES = (((1,), (1,)), ((), ()))


def split3(v):
    high = v.astype(BF16).astype(F32)
    rest = v - high
    mid = rest.astype(BF16).astype(F32)
    return high, mid, rest - mid


def far_rows(coords, soft):
    parts = [split3(v) for v in coords]
    norm = coords[0] * coords[0] + coords[1] * coords[1] + (coords[2] * coords[2] + soft)
    nh, nm, nl = split3(norm)
    one = jnp.ones_like(norm)
    rows = [p[0] for p in parts] + [p[1] for p in parts] + [nh, nm]
    return rows + [p[2] for p in parts] + [nl, one, one, one, jnp.zeros_like(one)]


def near_rows(coords, scale):
    parts = [[-2.0 * scale * part for part in split3(v)] for v in coords]
    norm = scale * (coords[0] * coords[0] + coords[1] * coords[1] + coords[2] * coords[2])
    one, zero = jnp.full_like(norm, scale), jnp.zeros_like(norm)
    h, m, l = ([p[k] for p in parts] for k in range(3))
    rows = h + h + [one, one] + m + m + [zero, zero] + l + l + [zero, zero]
    return rows + h + [one] + list(split3(norm)) + [zero]


def picked_rows(far, k, stride):
    first = far[pl.ds(k, 8, stride=stride), :]
    last = far[pl.ds(k + 8 * stride, 8, stride=stride), :]
    return jnp.concatenate([first, first, first, last], axis=0).astype(BF16)


def one_hot(label_ref, out_ref, tiles):
    ids = lax.broadcasted_iota(jnp.int32, (LANES, LANES), 0)
    for t in range(tiles):
        at = slice(t * LANES, (t + 1) * LANES)
        low = lax.rem(label_ref[:, at], LANES)
        out_ref[:, at] = jnp.where(ids == low, 1.0, 0.0).astype(BF16)


def high_mask(label, groups, repeat):
    ids = lax.broadcasted_iota(jnp.int32, (groups, label.shape[1]), 0)
    hit = (ids == label // LANES).astype(F32)
    return jnp.concatenate([hit] * repeat, axis=0)


def stacked3(v):
    return jnp.concatenate(list(split3(v)), axis=0).astype(BF16)


def fold3(v):
    n = v.shape[0] // 3
    return v[:n] + v[n : 2 * n] + v[2 * n :]


def gather_rows(table, label, hot, groups):
    features = table.shape[0] // groups
    picked = fold3(jnp.dot(stacked3(table), hot, preferred_element_type=F32))
    picked = picked * high_mask(label, groups, features)
    return [
        jnp.sum(picked[f * groups : (f + 1) * groups], axis=0, keepdims=True)
        for f in range(features)
    ]


def sum_rows(values, label, hot, groups):
    spread = jnp.concatenate([jnp.broadcast_to(v, (groups, v.shape[1])) for v in values], axis=0)
    spread = spread * high_mask(label, groups, len(values))
    return fold3(
        lax.dot_general(stacked3(spread), hot, CONTRACT_LANES, preferred_element_type=F32)
    )


def flat_row(ref, first, tiles):
    return jnp.concatenate([ref[first + t : first + t + 1, :] for t in range(tiles)], axis=1)


def signs_here():
    return [sign_of(axis) for axis in ("gx", "gy", "gz")]


def column_of(step):
    return 9 * (step[0] + 1) + 3 * (step[1] + 1) + (step[2] + 1)


def number_plan(tiles):
    bits = max((tiles - 1).bit_length(), 1)
    return bits, min(31 // bits, 9)


def place_of(step, tiles):
    bits, share = number_plan(tiles)
    order = 3 * (step[0] + 1) + (step[1] + 1)
    return -(-9 // share) * (step[2] + 1) + order // share, bits * (order % share)


def packed_numbers(lists, tiles):
    numbers = lists - tiles * lax.broadcasted_iota(jnp.int32, lists.shape, 1)
    for sign, width in zip(signs_here(), (9, 3, 1)):
        pieces = []
        for start in range(0, 27, 3 * width):
            for k in (2, 1, 0):
                pieces.append(numbers[:, start + k * width : start + (k + 1) * width])
        numbers = jnp.where(sign < 0, jnp.concatenate(pieces, axis=1), numbers)
    words = {}
    for x, y, z in itertools.product((-1, 0, 1), repeat=3):
        word, shift = place_of((x, y, z), tiles)
        column = column_of((x, y, z))
        piece = lax.shift_left(numbers[:, column : column + 1], jnp.int32(shift))
        words[word] = words[word] + piece if word in words else piece
    return jnp.concatenate([words[word] for word in sorted(words)], axis=1)


def as_float(step):
    return float(step) if isinstance(step, int) else step.astype(F32)


def pair_plan(tiles, count):
    held, ahead = (8, 6) if count == 1 else (8, 4) if count == 2 else (2, 1)
    unroll = 8 if count < 6 else 4
    if tiles % unroll:
        held, unroll, ahead = 2, 2, 1
    return held, unroll, ahead


def prepare_kernel(
    label_in, mass_in, pos_in, weight_in, charge_in, lists_in, bead_lists_in, leaving_in,
    rows_out, mass_out, hot, label_ref, mass, lists_out, bead_lists_out, leaving_out,
    pos, weight, charge, sem,
):
    moves = [
        (label_in, label_ref), (mass_in, mass), (pos_in, pos), (weight_in, weight),
        (charge_in, charge), (lists_in, lists_out), (bead_lists_in, bead_lists_out),
        (leaving_in, leaving_out),
    ]
    copies = [pltpu.make_async_copy(a, b, sem.at[i]) for i, (a, b) in enumerate(moves)]
    for copy in copies:
        copy.start()
    beads = weight.shape[1]
    tiles, groups = pos.shape[0] // 3, beads // LANES
    copies[0].wait()
    one_hot(label_ref, hot, tiles)
    label = label_ref[...]
    copies[1].wait()
    copies[2].wait()
    m = mass[...]
    values = [m * flat_row(pos, k * tiles, tiles) for k in range(3)] + [m]
    sums = sum_rows(values, label, hot[...], groups)
    mass_sum = sums[3 * groups :]
    mass_out[...] = mass_sum
    for copy in copies[3:]:
        copy.wait()
    table = jnp.concatenate(
        [weight[:, g * LANES : (g + 1) * LANES] for g in range(groups)], axis=0
    )
    charged = charge[...] * gather_rows(table, label, hot[...], groups)[0]
    rows_out[: 3 * tiles, :] = pos[...]
    for t in range(tiles):
        at = slice(t * LANES, (t + 1) * LANES)
        rows_out[3 * tiles + t : 3 * tiles + t + 1, :] = charged[:, at]
    base = 4 * tiles
    for k in range(3):
        rows_out[base + k * groups : base + (k + 1) * groups, :] = (
            sums[k * groups : (k + 1) * groups] / mass_sum
        )
    rows_out[base + 3 * groups : base + 4 * groups, :] = table


def pair_kernel(tiles, groups, entries, sources, first, last, *refs):
    numbers, own = refs[:2]
    near = None if first else refs[2]
    refs = refs[2 if first else 3 :]
    cells = refs[:sources]
    rest = refs[sources:]
    before = None if first else rest[0]
    rest = rest[0 if first else 1 :]
    if first:
        rest[1][...] = packed_numbers(numbers[...], tiles)
        numbers, near, rest = rest[1], rest[2], rest[:1] + rest[3:]
        coords = [own[k * tiles : (k + 1) * tiles, :] - 0.5 for k in range(3)]
        for r, row in enumerate(near_rows(coords, 1.0)):
            rest[-1][r * tiles : (r + 1) * tiles, :] = row
        for t in range(tiles):
            near[t] = rest[-1][pl.ds(t, ROWS, stride=tiles), :].T.astype(BF16)
    out, far, held = rest[:3]
    total = rest[-1] if last else None
    count = len(entries)
    height = 4 * (tiles + groups)
    signs = signs_here()
    places = []
    for e, (source, cell, steps) in enumerate(entries):
        step = [steps[k] * signs[k] if steps[k] else 0 for k in range(3)]
        places.append(place_of(steps, tiles))
        base = cell * height
        coords = [
            cells[source][base + k * tiles : base + (k + 1) * tiles, :]
            + (as_float(step[k]) - 0.5)
            for k in range(3)
        ]
        charged = cells[source][base + 3 * tiles : base + 4 * tiles, :]
        for r, row in enumerate(far_rows(coords, SOFT_CORE) + coords + [charged]):
            far[e, r * tiles : (r + 1) * tiles, :] = row

    bits = number_plan(tiles)[0]

    used = sorted({word for word, _ in places})

    def words_of(t):
        row = numbers[pl.ds(t, 1), :]
        return tuple(row[0, word] for word in used)

    def numbers_of(words):
        words = dict(zip(used, words))
        return [
            lax.bitwise_and(
                lax.shift_right_logical(words[word], jnp.int32(shift)), jnp.int32((1 << bits) - 1)
            )
            for word, shift in places
        ]

    def distances(t, into, ks, part=None):
        lhs = near[t]
        starts = list(range(0, count, 2))
        if part is not None:
            starts = starts[part::PARTS]
        for e in starts:
            members = range(e, min(e + 2, count))
            rhs = [
                picked_rows(far.at[m], ks[m], tiles) for m in members
            ]
            rhs = jnp.concatenate(rhs, axis=1) if len(rhs) > 1 else rhs[0]
            inv = lax.rsqrt(jnp.dot(lhs, rhs, preferred_element_type=F32))
            charged = [far[m, pl.ds(19 * tiles + ks[m], 1), :] for m in members]
            charged = jnp.concatenate(charged, axis=1) if len(charged) > 1 else charged[0]
            into[:, e * LANES : e * LANES + rhs.shape[1]] = inv * inv * inv * charged

    def strengths(t, dist, ks, part):
        block = LANES // PARTS
        at = slice(part * block, (part + 1) * block)
        if True:
            if before is None:
                acc = [jnp.zeros((block, LANES), F32)] * 4
            else:
                acc = [before[t, d, at, :] for d in range(4)]
            for e in range(count):
                k = ks[e]
                s = dist[at, e * LANES : (e + 1) * LANES]
                acc[3] = acc[3] + s
                for d in range(3):
                    acc[d] = acc[d] + s * far[e, pl.ds((16 + d) * tiles + k, 1), :]
            for d in range(4):
                if last:
                    total[d, at, :] = acc[d]
                else:
                    out[t, d, at, :] = acc[d]
        if not last or part < PARTS - 1:
            return
        sums = [jnp.sum(total[d].T, axis=0, keepdims=True) for d in range(4)]
        scale = own[pl.ds(3 * tiles + t, 1), :]
        for d in range(3):
            here = own[pl.ds(d * tiles + t, 1), :] - 0.5
            out[pl.ds(d * tiles + t, 1), :] = scale * (here * sums[3] - sums[d])

    buffered, unroll, ahead = pair_plan(tiles, count)
    buffers = [held.at[i] for i in range(buffered)]
    words = [words_of(min(i, tiles - 1)) for i in range(unroll + ahead)]
    for i in range(ahead):
        distances(i, buffers[i], numbers_of(words[i]))

    def some_tiles(step, words):
        following = [
            words_of(jnp.minimum(unroll * (step + 1) + ahead + u, tiles - 1)) for u in range(unroll)
        ]
        for u in range(unroll):
            t = unroll * step + u
            later = jnp.minimum(t + ahead, tiles - 1)
            ks, ks_later = numbers_of(words[u]), numbers_of(words[u + ahead])
            for part in range(PARTS):
                distances(later, buffers[(u + ahead) % buffered], ks_later, part)
                strengths(t, buffers[u % buffered], ks, part)
        return tuple(words[unroll:]) + tuple(following)

    lax.fori_loop(0, tiles // unroll, some_tiles, tuple(words))


def weight_rows(weight):
    h, m, l = split3(weight)
    return [h, h, h, m, m, l], [h, m, l, h, m, h]


def final_kernel(tiles, groups, entries, sources, *refs):
    lists_ref, own, mass_sum_ref, atomic, mass, label_ref, leave_ref, hot = refs[:8]
    cells = refs[8 : 8 + sources]
    rest = refs[8 + sources :]
    forces_out, record_out, leave_hot, raw, far, near, nearest = rest[:7]
    buffers, (total, coarse) = rest[7:9], rest[9:]
    lists, listed = lists_ref[...], lists_ref.shape[1]
    height = 4 * (tiles + groups)
    signs = signs_here()
    every = len(entries) * groups
    for source, cell, steps in entries:
        step = [steps[k] * signs[k] if steps[k] else 0 for k in range(3)]
        column = column_of(step)
        base = cell * height + 4 * tiles
        for k in range(4):
            block = cells[source][base + k * groups : base + (k + 1) * groups, :]
            if k < 3:
                block = block + (as_float(step[k]) - 0.5)
            raw[k, pl.ds(column * groups, groups), :] = block
    scale = math.sqrt(math.log2(math.e) / SIGMA_SQ)
    coords = [raw[k] for k in range(3)]
    one, zero = jnp.ones_like(coords[0]), jnp.zeros_like(coords[0])
    plain = coords + weight_rows(raw[3])[0] + [one, zero]
    for r, row in enumerate(far_rows([scale * v for v in coords], 0.0) + plain):
        far[r * every : (r + 1) * every, :] = row
    base = 4 * tiles
    coords = [own[base + k * groups : base + (k + 1) * groups, :] - 0.5 for k in range(3)]
    own_weight = own[base + 3 * groups : base + 4 * groups, :]
    zero = jnp.zeros_like(own_weight)
    factors = [-EPS_COARSE * row for row in weight_rows(own_weight)[1]]
    factors += [zero + EPS_COARSE, zero] + [zero] * 8
    for r, row in enumerate(near_rows([scale * v for v in coords], -1.0) + factors):
        near[r * groups : (r + 1) * groups, :] = row
    for b in range(groups):
        nearest[b] = near[pl.ds(b, ROWS + 16, stride=groups), :].T.astype(BF16)

    def products(b, into):
        lhs = nearest[b]
        for e in range(0, listed, 2):
            members = [lists[b, m] for m in range(e, min(e + 2, listed))]
            rhs = jnp.concatenate([picked_rows(far, k, every) for k in members], axis=1)
            dist = jnp.dot(lhs[:, :ROWS], rhs, preferred_element_type=F32)
            rhs = [far[pl.ds(k + 19 * every, 8, stride=every), :] for k in members]
            rhs = jnp.concatenate([jnp.concatenate([r, r], axis=0) for r in rhs], axis=1)
            factor = jnp.dot(lhs[:, ROWS:], rhs.astype(BF16), preferred_element_type=F32)
            into[:, e * LANES : (e + len(members)) * LANES] = jnp.exp2(dist) * factor

    def strengths(b, held):
        block = LANES // PARTS
        for part in range(PARTS):
            at = slice(part * block, (part + 1) * block)
            acc = [jnp.zeros((block, LANES), F32)] * 4
            for e in range(listed):
                k = lists[b, e]
                s = held[at, e * LANES : (e + 1) * LANES]
                acc[3] = acc[3] + s
                for d in range(3):
                    acc[d] = acc[d] + s * far[pl.ds((16 + d) * every + k, 1), :]
            for d in range(4):
                total[d, at, :] = acc[d]
        sums = [jnp.sum(total[d].T, axis=0, keepdims=True) for d in range(4)]
        for d in range(3):
            centre = own[base + d * groups + b : base + d * groups + b + 1, :] - 0.5
            coarse[d * groups + b : d * groups + b + 1, :] = centre * sums[3] - sums[d]

    products(0, buffers[0])
    for b in range(groups):
        if b + 1 < groups:
            products(b + 1, buffers[(b + 1) % 2])
        strengths(b, buffers[b % 2])

    label = label_ref[...]
    mass_sum = mass_sum_ref[...]
    scaled = coarse[...] / jnp.concatenate([mass_sum] * 3, axis=0)
    spread = gather_rows(scaled, label, hot[...], groups)
    forces = []
    for d in range(3):
        forces.append(flat_row(atomic, d * tiles, tiles) + mass[...] * spread[d])
        for t in range(tiles):
            at = slice(t * LANES, (t + 1) * LANES)
            forces_out[d * tiles + t : d * tiles + t + 1, :] = forces[d][:, at]
    molecule = sum_rows(forces, label, hot[...], groups)
    table = jnp.concatenate(
        [own[base : base + 3 * groups, :], molecule, own_weight, mass_sum], axis=0
    )
    leavers = leave_ref.shape[1] // 2
    one_hot(leave_ref, leave_hot, leave_ref.shape[1] // LANES)
    picked = gather_rows(table, leave_ref[...], leave_hot[...], groups)
    for side, shift in ((0, -1.0), (1, 1.0)):
        for f in range(8):
            row = picked[f][:, side * leavers : (side + 1) * leavers]
            record_out[side, f : f + 1, :] = row + shift if f == 0 else row


def moves(axis):
    n = lax.axis_size(axis)
    if n <= 2:
        return [([n - 1 - i for i in range(n)], (1, -1))]
    if n % 2 == 0:
        inner = [i ^ 1 for i in range(n)]
        return [([(((i + 1) ^ 1) - 1) % n for i in range(n)], (-1,)), (inner, (1,))]
    return [([(i + 1) % n for i in range(n)], (-1,)), ([(i - 1) % n for i in range(n)], (1,))]


def exchange(x, axis):
    return [
        (lax.ppermute(x, axis, list(enumerate(receivers))), steps)
        for receivers, steps in moves(axis)
    ]


def exchange_plane(x, first, second):
    sizes = lax.axis_size(first), lax.axis_size(second)
    still = [(list(range(n)), (0,)) for n in sizes]
    blocks = []
    for to_b, steps_b in moves(second) + [still[1]]:
        for to_a, steps_a in [still[0]] + moves(first):
            steps = [(p, q) for p in steps_a for q in steps_b]
            if steps == [(0, 0)]:
                continue
            pairs = [
                (a * sizes[1] + b, to_a[a] * sizes[1] + to_b[b])
                for a in range(sizes[0])
                for b in range(sizes[1])
            ]
            blocks.append((lax.ppermute(x, (first, second), pairs), steps))
    return blocks


def sign_of(axis):
    n = lax.axis_size(axis)
    if n > 2 and n % 2 == 0:
        return 1 - 2 * lax.rem(lax.axis_index(axis), 2)
    return jnp.int32(1)


def per_device(positions, charges, masses, weights, mapping, atom_lists, bead_lists, leaving):
    atoms, beads = positions.shape[4], weights.shape[3]
    tiles, groups = atoms // LANES, beads // LANES
    pos = positions.reshape(3 * tiles, LANES)
    charge, mass = charges[0, 0], masses[0, 0]
    weight, label = weights[0, 0], mapping[0, 0]
    leavers = leaving.shape[4]
    height = 4 * (tiles + groups)
    limit = pltpu.CompilerParams(vmem_limit_bytes=48 * 2**20)
    inputs = [
        label, mass, pos, weight, charge,
        atom_lists[0, 0, 0], bead_lists[0, 0, 0], leaving.reshape(1, 2 * leavers),
    ]

    def like(x):
        return jax.ShapeDtypeStruct(x.shape, x.dtype)

    own, mass_sum, hot, label, mass, lists, *small = pl.pallas_call(
        prepare_kernel,
        out_shape=(
            jax.ShapeDtypeStruct((height, LANES), F32),
            jax.ShapeDtypeStruct((groups, LANES), F32),
            jax.ShapeDtypeStruct((LANES, atoms), BF16),
            like(label),
            like(mass),
            *[like(x) for x in inputs[5:]],
        ),
        in_specs=[HBM] * 8,
        out_specs=(VMEM,) * 8,
        scratch_shapes=[
            *[pltpu.VMEM(x.shape, x.dtype) for x in inputs[2:5]],
            pltpu.SemaphoreType.DMA((8,)),
        ],
        compiler_params=pltpu.CompilerParams(vmem_limit_bytes=48 * 2**20),
    )(*[pltpu.with_memory_space_constraint(x, pltpu.HBM) for x in inputs])

    def pairs(lists, near, entries, cells, before, last=False):
        count = len(entries)
        first = before is None
        args = [lists, own, *cells] if first else [lists, own, near, *cells, before]
        place = len(args) - 1
        words = jax.ShapeDtypeStruct((tiles, 3 * -(-9 // number_plan(tiles)[1])), jnp.int32)
        points = jax.ShapeDtypeStruct((tiles, LANES, ROWS), BF16)
        extra = [words, points] if first else []
        shape = (3 * tiles, LANES) if last else (tiles, 4, LANES, LANES)
        work = tiles * count * LANES * LANES
        return pl.pallas_call(
            functools.partial(
                pair_kernel, tiles, groups, entries, len(cells), before is None, last
            ),
            out_shape=(jax.ShapeDtypeStruct(shape, F32), *extra),
            in_specs=[VMEM] * len(args),
            out_specs=(VMEM,) * (1 + len(extra)),
            scratch_shapes=[
                pltpu.VMEM((count, 20 * tiles, LANES), F32),
                pltpu.VMEM((pair_plan(tiles, count)[0], LANES, count * LANES), F32),
            ]
            + ([pltpu.VMEM((4, LANES, LANES), F32)] if last else [])
            + ([pltpu.VMEM((ROWS * tiles, LANES), F32)] if first else []),
            input_output_aliases={} if last or before is None else {place: 0},
            compiler_params=limit,
            cost_estimate=pl.CostEstimate(
                flops=60 * work, bytes_accessed=4 * height * LANES, transcendentals=work
            ),
        )(*args)

    with_x = exchange(own, "gx")
    force, lists, near = pairs(lists, None, [(0, 0, (0, 0, 0))], [own], None)
    column = jnp.concatenate([own] + [block for block, _ in with_x], axis=0)
    column, force = lax.optimization_barrier((column, force))
    cells = [(0, 0)] + [(c + 1, x) for c, (_, steps) in enumerate(with_x) for x in steps]
    with_y = exchange(column, "gy")[::-1]
    entries = [(0, c, (x, 0, 0)) for c, x in cells[1:]]
    force = pairs(lists, near, entries, [column], force)[0]
    near_y, far_y = with_y[:1], with_y[1:]
    if far_y:
        entries = [(0, c, (x, y, 0)) for y in near_y[0][1] for c, x in cells]
        force = pairs(lists, near, entries, [near_y[0][0]], force)[0]
    plane = jnp.concatenate([column] + [block for block, _ in with_y], axis=0)
    plane, force = lax.optimization_barrier((plane, force))
    held = 1 + len(with_x)
    plane_cells = [(c, (x, 0)) for c, x in cells]
    plane_cells += [
        (held * (k + 1) + c, (x, y))
        for k, (_, steps) in enumerate(with_y)
        for y in steps
        for c, x in cells
    ]
    with_z = [(block, z) for block, steps in exchange(plane, "gz") for z in steps][::-1]
    left = far_y[0][1] if far_y else near_y[0][1]
    entries = [(0, c, (x, y, 0)) for c, (x, y) in plane_cells if y in left]
    force = pairs(lists, near, entries, [plane], force)[0]
    for place, (block, z) in enumerate(with_z):
        entries = [(0, c, (x, y, z)) for c, (x, y) in plane_cells]
        force = pairs(lists, near, entries, [block], force, place == 1)[0]

    sources = [plane] + [block for block, _ in with_z]
    z_steps = [0] + [step for _, step in with_z]
    entries = [(s, c, (x, y, z_steps[s])) for s in range(3) for c, (x, y) in plane_cells]
    every, listed = len(entries) * groups, small[0].shape[1]
    forces, record = pl.pallas_call(
        functools.partial(final_kernel, tiles, groups, entries, len(sources)),
        out_shape=(
            pltpu.VMEM((3 * tiles, LANES), F32),
            jax.ShapeDtypeStruct((2, 8, leavers), F32),
        ),
        in_specs=[VMEM] * (8 + len(sources)),
        out_specs=(VMEM, VMEM),
        scratch_shapes=[
            pltpu.VMEM((LANES, 2 * leavers), BF16),
            pltpu.VMEM((4, every, LANES), F32),
            pltpu.VMEM((27 * every, LANES), F32),
            pltpu.VMEM(((ROWS + 16) * groups, LANES), F32),
            pltpu.VMEM((groups, LANES, ROWS + 16), BF16),
            *[pltpu.VMEM((LANES, listed * LANES), F32)] * 2,
            pltpu.VMEM((4, LANES, LANES), F32),
            pltpu.VMEM((3 * groups, LANES), F32),
        ],
        compiler_params=limit,
    )(small[0], own, mass_sum, force, mass, label, small[1], hot, *sources)
    n = lax.axis_size("gx")
    if n == 2:
        arrivals = lax.ppermute(record, "gx", [(0, 1), (1, 0)])
    else:
        up = [(i, (i + 1) % n) for i in range(n)]
        down = [(j, i) for i, j in up]
        arrivals = jnp.stack(
            [lax.ppermute(record[0], "gx", up), lax.ppermute(record[1], "gx", down)]
        )
    return (forces.reshape(1, 1, 1, 3, atoms), arrivals[None, None, None])


def solution(mesh):
    cell = ("gx", "gy", "gz")
    placed = (
        P(*cell, None, None),
        P(*cell, None),
        P(*cell, None),
        P(*cell, None),
        P(*cell, None),
        P(*cell, None, None),
        P(*cell, None, None),
        P(*cell, None, None),
    )
    return jax.shard_map(
        per_device,
        mesh=mesh,
        in_specs=placed,
        out_specs=(P(*cell, None, None), P(*cell, None, None, None)),
        check_vma=False,
    )
```

```python
import functools
import itertools
import math

import jax
import jax.numpy as jnp
from jax import lax
from jax.experimental import pallas as pl
from jax.experimental.pallas import tpu as pltpu
from jax.sharding import PartitionSpec as P

SOFT_CORE = 0.01
EPS_COARSE = 2.0
SIGMA_SQ = 0.25
LANES = 128
ROWS = 32
PARTS = 4
F32, BF16 = jnp.float32, jnp.bfloat16
VMEM = pl.BlockSpec(memory_space=pltpu.VMEM)
HBM = pl.BlockSpec(memory_space=pltpu.HBM)
CONTRACT_LANES = (((1,), (1,)), ((), ()))


def split3(v):
    high = v.astype(BF16).astype(F32)
    rest = v - high
    mid = rest.astype(BF16).astype(F32)
    return high, mid, rest - mid


def far_rows(coords, soft):
    parts = [split3(v) for v in coords]
    norm = coords[0] * coords[0] + coords[1] * coords[1] + (coords[2] * coords[2] + soft)
    nh, nm, nl = split3(norm)
    one = jnp.ones_like(norm)
    rows = [p[0] for p in parts] + [p[1] for p in parts] + [nh, nm]
    return rows + [p[2] for p in parts] + [nl, one, one, one, jnp.zeros_like(one)]


def near_rows(coords, scale):
    parts = [[-2.0 * scale * part for part in split3(v)] for v in coords]
    norm = scale * (coords[0] * coords[0] + coords[1] * coords[1] + coords[2] * coords[2])
    one, zero = jnp.full_like(norm, scale), jnp.zeros_like(norm)
    h, m, l = ([p[k] for p in parts] for k in range(3))
    rows = h + h + [one, one] + m + m + [zero, zero] + l + l + [zero, zero]
    return rows + h + [one] + list(split3(norm)) + [zero]


def picked_rows(far, k, stride):
    first = far[pl.ds(k, 8, stride=stride), :]
    last = far[pl.ds(k + 8 * stride, 8, stride=stride), :]
    return jnp.concatenate([first, first, first, last], axis=0).astype(BF16)


def one_hot(label_ref, out_ref, tiles):
    ids = lax.broadcasted_iota(jnp.int32, (LANES, LANES), 0)
    for t in range(tiles):
        at = slice(t * LANES, (t + 1) * LANES)
        low = lax.rem(label_ref[:, at], LANES)
        out_ref[:, at] = jnp.where(ids == low, 1.0, 0.0).astype(BF16)


def high_mask(label, groups, repeat):
    ids = lax.broadcasted_iota(jnp.int32, (groups, label.shape[1]), 0)
    hit = (ids == label // LANES).astype(F32)
    return jnp.concatenate([hit] * repeat, axis=0)


def stacked3(v):
    return jnp.concatenate(list(split3(v)), axis=0).astype(BF16)


def fold3(v):
    n = v.shape[0] // 3
    return v[:n] + v[n : 2 * n] + v[2 * n :]


def gather_rows(table, label, hot, groups):
    features = table.shape[0] // groups
    picked = fold3(jnp.dot(stacked3(table), hot, preferred_element_type=F32))
    picked = picked * high_mask(label, groups, features)
    return [
        jnp.sum(picked[f * groups : (f + 1) * groups], axis=0, keepdims=True)
        for f in range(features)
    ]


def sum_rows(values, label, hot, groups):
    spread = jnp.concatenate([jnp.broadcast_to(v, (groups, v.shape[1])) for v in values], axis=0)
    spread = spread * high_mask(label, groups, len(values))
    return fold3(
        lax.dot_general(stacked3(spread), hot, CONTRACT_LANES, preferred_element_type=F32)
    )


def flat_row(ref, first, tiles):
    return jnp.concatenate([ref[first + t : first + t + 1, :] for t in range(tiles)], axis=1)


def signs_here():
    return [sign_of(axis) for axis in ("gx", "gy", "gz")]


def column_of(step):
    return 9 * (step[0] + 1) + 3 * (step[1] + 1) + (step[2] + 1)


def number_plan(tiles):
    bits = max((tiles - 1).bit_length(), 1)
    return bits, min(31 // bits, 9)


def place_of(step, tiles):
    bits, share = number_plan(tiles)
    order = 3 * (step[0] + 1) + (step[1] + 1)
    return -(-9 // share) * (step[2] + 1) + order // share, bits * (order % share)


def packed_numbers(lists, tiles):
    numbers = lists - tiles * lax.broadcasted_iota(jnp.int32, lists.shape, 1)
    for sign, width in zip(signs_here(), (9, 3, 1)):
        pieces = []
        for start in range(0, 27, 3 * width):
            for k in (2, 1, 0):
                pieces.append(numbers[:, start + k * width : start + (k + 1) * width])
        numbers = jnp.where(sign < 0, jnp.concatenate(pieces, axis=1), numbers)
    words = {}
    for x, y, z in itertools.product((-1, 0, 1), repeat=3):
        word, shift = place_of((x, y, z), tiles)
        column = column_of((x, y, z))
        piece = lax.shift_left(numbers[:, column : column + 1], jnp.int32(shift))
        words[word] = words[word] + piece if word in words else piece
    return jnp.concatenate([words[word] for word in sorted(words)], axis=1)


def as_float(step):
    return float(step) if isinstance(step, int) else step.astype(F32)


def pair_plan(tiles, count):
    held, ahead = (8, 6) if count == 1 else (8, 4) if count == 2 else (2, 1)
    unroll = 8 if count < 6 else 4
    if tiles % unroll:
        held, unroll, ahead = 2, 2, 1
    return held, unroll, ahead


def prepare_kernel(
    label_in, mass_in, pos_in, weight_in, charge_in, lists_in, bead_lists_in, leaving_in,
    rows_out, mass_out, hot, label_ref, mass, lists_out, bead_lists_out, leaving_out,
    pos, weight, charge, sem,
):
    moves = [
        (label_in, label_ref), (mass_in, mass), (pos_in, pos), (weight_in, weight),
        (charge_in, charge), (lists_in, lists_out), (bead_lists_in, bead_lists_out),
        (leaving_in, leaving_out),
    ]
    copies = [pltpu.make_async_copy(a, b, sem.at[i]) for i, (a, b) in enumerate(moves)]
    for copy in copies:
        copy.start()
    beads = weight.shape[1]
    tiles, groups = pos.shape[0] // 3, beads // LANES
    copies[0].wait()
    one_hot(label_ref, hot, tiles)
    label = label_ref[...]
    copies[1].wait()
    copies[2].wait()
    m = mass[...]
    values = [m * flat_row(pos, k * tiles, tiles) for k in range(3)] + [m]
    sums = sum_rows(values, label, hot[...], groups)
    mass_sum = sums[3 * groups :]
    mass_out[...] = mass_sum
    for copy in copies[3:]:
        copy.wait()
    table = jnp.concatenate(
        [weight[:, g * LANES : (g + 1) * LANES] for g in range(groups)], axis=0
    )
    charged = charge[...] * gather_rows(table, label, hot[...], groups)[0]
    rows_out[: 3 * tiles, :] = pos[...]
    for t in range(tiles):
        at = slice(t * LANES, (t + 1) * LANES)
        rows_out[3 * tiles + t : 3 * tiles + t + 1, :] = charged[:, at]
    base = 4 * tiles
    for k in range(3):
        rows_out[base + k * groups : base + (k + 1) * groups, :] = (
            sums[k * groups : (k + 1) * groups] / mass_sum
        )
    rows_out[base + 3 * groups : base + 4 * groups, :] = table


def pair_kernel(tiles, groups, entries, sources, first, last, *refs):
    numbers, own = refs[:2]
    near = None if first else refs[2]
    refs = refs[2 if first else 3 :]
    cells = refs[:sources]
    rest = refs[sources:]
    before = None if first else rest[0]
    rest = rest[0 if first else 1 :]
    if first:
        rest[1][...] = packed_numbers(numbers[...], tiles)
        numbers, near, rest = rest[1], rest[2], rest[:1] + rest[3:]
        coords = [own[k * tiles : (k + 1) * tiles, :] - 0.5 for k in range(3)]
        for r, row in enumerate(near_rows(coords, 1.0)):
            rest[-1][r * tiles : (r + 1) * tiles, :] = row
        for t in range(tiles):
            near[t] = rest[-1][pl.ds(t, ROWS, stride=tiles), :].T.astype(BF16)
    out, far, held = rest[:3]
    total = rest[-1] if last else None
    count = len(entries)
    height = 4 * (tiles + groups)
    signs = signs_here()
    places = []
    for e, (source, cell, steps) in enumerate(entries):
        step = [steps[k] * signs[k] if steps[k] else 0 for k in range(3)]
        places.append(place_of(steps, tiles))
        base = cell * height
        coords = [
            cells[source][base + k * tiles : base + (k + 1) * tiles, :]
            + (as_float(step[k]) - 0.5)
            for k in range(3)
        ]
        charged = cells[source][base + 3 * tiles : base + 4 * tiles, :]
        for r, row in enumerate(far_rows(coords, SOFT_CORE) + coords + [charged]):
            far[e, r * tiles : (r + 1) * tiles, :] = row

    bits = number_plan(tiles)[0]

    used = sorted({word for word, _ in places})

    def words_of(t):
        row = numbers[pl.ds(t, 1), :]
        return tuple(row[0, word] for word in used)

    def numbers_of(words):
        words = dict(zip(used, words))
        return [
            lax.bitwise_and(
                lax.shift_right_logical(words[word], jnp.int32(shift)), jnp.int32((1 << bits) - 1)
            )
            for word, shift in places
        ]

    def distances(t, into, ks, part=None):
        lhs = near[t]
        starts = list(range(0, count, 2))
        if part is not None:
            starts = starts[part::PARTS]
        for e in starts:
            members = range(e, min(e + 2, count))
            rhs = [
                picked_rows(far.at[m], ks[m], tiles) for m in members
            ]
            rhs = jnp.concatenate(rhs, axis=1) if len(rhs) > 1 else rhs[0]
            inv = lax.rsqrt(jnp.dot(lhs, rhs, preferred_element_type=F32))
            charged = [far[m, pl.ds(19 * tiles + ks[m], 1), :] for m in members]
            charged = jnp.concatenate(charged, axis=1) if len(charged) > 1 else charged[0]
            into[:, e * LANES : e * LANES + rhs.shape[1]] = inv * inv * inv * charged

    def strengths(t, dist, ks, part):
        block = LANES // PARTS
        at = slice(part * block, (part + 1) * block)
        if True:
            if before is None:
                acc = [jnp.zeros((block, LANES), F32)] * 4
            else:
                acc = [before[t, d, at, :] for d in range(4)]
            for e in range(count):
                k = ks[e]
                s = dist[at, e * LANES : (e + 1) * LANES]
                acc[3] = acc[3] + s
                for d in range(3):
                    acc[d] = acc[d] + s * far[e, pl.ds((16 + d) * tiles + k, 1), :]
            for d in range(4):
                if last:
                    total[d, at, :] = acc[d]
                else:
                    out[t, d, at, :] = acc[d]
        if not last or part < PARTS - 1:
            return
        sums = [jnp.sum(total[d].T, axis=0, keepdims=True) for d in range(4)]
        scale = own[pl.ds(3 * tiles + t, 1), :]
        for d in range(3):
            here = own[pl.ds(d * tiles + t, 1), :] - 0.5
            out[pl.ds(d * tiles + t, 1), :] = scale * (here * sums[3] - sums[d])

    buffered, unroll, ahead = pair_plan(tiles, count)
    buffers = [held.at[i] for i in range(buffered)]
    words = [words_of(min(i, tiles - 1)) for i in range(unroll + ahead)]
    for i in range(ahead):
        distances(i, buffers[i], numbers_of(words[i]))

    def some_tiles(step, words):
        following = [
            words_of(jnp.minimum(unroll * (step + 1) + ahead + u, tiles - 1)) for u in range(unroll)
        ]
        for u in range(unroll):
            t = unroll * step + u
            later = jnp.minimum(t + ahead, tiles - 1)
            ks, ks_later = numbers_of(words[u]), numbers_of(words[u + ahead])
            for part in range(PARTS):
                distances(later, buffers[(u + ahead) % buffered], ks_later, part)
                strengths(t, buffers[u % buffered], ks, part)
        return tuple(words[unroll:]) + tuple(following)

    lax.fori_loop(0, tiles // unroll, some_tiles, tuple(words))


def weight_rows(weight):
    h, m, l = split3(weight)
    return [h, h, h, m, m, l], [h, m, l, h, m, h]


def force_kernel(tiles, groups, scaled, atomic, mass, label_ref, hot, forces_out):
    spread = gather_rows(scaled[...], label_ref[...], hot[...], groups)
    for d in range(3):
        added = mass[...] * spread[d]
        for t in range(tiles):
            row = slice(d * tiles + t, d * tiles + t + 1)
            forces_out[row, :] = atomic[row, :] + added[:, t * LANES : (t + 1) * LANES]


def record_kernel(tiles, groups, entries, sources, *refs):
    lists_ref, own, mass_sum_ref, atomic, label_ref, leave_ref, hot = refs[:7]
    cells = refs[7 : 7 + sources]
    rest = refs[7 + sources :]
    scaled_out, record_out, leave_hot, raw, far, near, nearest = rest[:7]
    buffers, (total, coarse) = rest[7:9], rest[9:]
    lists, listed = lists_ref[...], lists_ref.shape[1]
    height = 4 * (tiles + groups)
    signs = signs_here()
    every = len(entries) * groups
    for source, cell, steps in entries:
        step = [steps[k] * signs[k] if steps[k] else 0 for k in range(3)]
        column = column_of(step)
        base = cell * height + 4 * tiles
        for k in range(4):
            block = cells[source][base + k * groups : base + (k + 1) * groups, :]
            if k < 3:
                block = block + (as_float(step[k]) - 0.5)
            raw[k, pl.ds(column * groups, groups), :] = block
    scale = math.sqrt(math.log2(math.e) / SIGMA_SQ)
    coords = [raw[k] for k in range(3)]
    one, zero = jnp.ones_like(coords[0]), jnp.zeros_like(coords[0])
    plain = coords + weight_rows(raw[3])[0] + [one, zero]
    for r, row in enumerate(far_rows([scale * v for v in coords], 0.0) + plain):
        far[r * every : (r + 1) * every, :] = row
    base = 4 * tiles
    coords = [own[base + k * groups : base + (k + 1) * groups, :] - 0.5 for k in range(3)]
    own_weight = own[base + 3 * groups : base + 4 * groups, :]
    zero = jnp.zeros_like(own_weight)
    factors = [-EPS_COARSE * row for row in weight_rows(own_weight)[1]]
    factors += [zero + EPS_COARSE, zero] + [zero] * 8
    for r, row in enumerate(near_rows([scale * v for v in coords], -1.0) + factors):
        near[r * groups : (r + 1) * groups, :] = row
    for b in range(groups):
        nearest[b] = near[pl.ds(b, ROWS + 16, stride=groups), :].T.astype(BF16)

    def products(b, into):
        lhs = nearest[b]
        for e in range(0, listed, 2):
            members = [lists[b, m] for m in range(e, min(e + 2, listed))]
            rhs = jnp.concatenate([picked_rows(far, k, every) for k in members], axis=1)
            dist = jnp.dot(lhs[:, :ROWS], rhs, preferred_element_type=F32)
            rhs = [far[pl.ds(k + 19 * every, 8, stride=every), :] for k in members]
            rhs = jnp.concatenate([jnp.concatenate([r, r], axis=0) for r in rhs], axis=1)
            factor = jnp.dot(lhs[:, ROWS:], rhs.astype(BF16), preferred_element_type=F32)
            into[:, e * LANES : (e + len(members)) * LANES] = jnp.exp2(dist) * factor

    def strengths(b, held):
        block = LANES // PARTS
        for part in range(PARTS):
            at = slice(part * block, (part + 1) * block)
            acc = [jnp.zeros((block, LANES), F32)] * 4
            for e in range(listed):
                k = lists[b, e]
                s = held[at, e * LANES : (e + 1) * LANES]
                acc[3] = acc[3] + s
                for d in range(3):
                    acc[d] = acc[d] + s * far[pl.ds((16 + d) * every + k, 1), :]
            for d in range(4):
                total[d, at, :] = acc[d]
        sums = [jnp.sum(total[d].T, axis=0, keepdims=True) for d in range(4)]
        for d in range(3):
            centre = own[base + d * groups + b : base + d * groups + b + 1, :] - 0.5
            coarse[d * groups + b : d * groups + b + 1, :] = centre * sums[3] - sums[d]

    products(0, buffers[0])
    for b in range(groups):
        if b + 1 < groups:
            products(b + 1, buffers[(b + 1) % 2])
        strengths(b, buffers[b % 2])

    mass_sum = mass_sum_ref[...]
    flat = [flat_row(atomic, d * tiles, tiles) for d in range(3)]
    summed = sum_rows(flat, label_ref[...], hot[...], groups)
    scaled_out[...] = coarse[...] / jnp.concatenate([mass_sum] * 3, axis=0)
    molecule = summed + coarse[...]
    table = jnp.concatenate(
        [own[base : base + 3 * groups, :], molecule, own_weight, mass_sum], axis=0
    )
    leavers = leave_ref.shape[1] // 2
    one_hot(leave_ref, leave_hot, leave_ref.shape[1] // LANES)
    picked = gather_rows(table, leave_ref[...], leave_hot[...], groups)
    for side, shift in ((0, -1.0), (1, 1.0)):
        for f in range(8):
            row = picked[f][:, side * leavers : (side + 1) * leavers]
            record_out[side, f : f + 1, :] = row + shift if f == 0 else row


def moves(axis):
    n = lax.axis_size(axis)
    if n <= 2:
        return [([n - 1 - i for i in range(n)], (1, -1))]
    if n % 2 == 0:
        inner = [i ^ 1 for i in range(n)]
        return [([(((i + 1) ^ 1) - 1) % n for i in range(n)], (-1,)), (inner, (1,))]
    return [([(i + 1) % n for i in range(n)], (-1,)), ([(i - 1) % n for i in range(n)], (1,))]


def exchange(x, axis):
    return [
        (lax.ppermute(x, axis, list(enumerate(receivers))), steps)
        for receivers, steps in moves(axis)
    ]


def exchange_plane(x, first, second):
    sizes = lax.axis_size(first), lax.axis_size(second)
    still = [(list(range(n)), (0,)) for n in sizes]
    blocks = []
    for to_b, steps_b in moves(second) + [still[1]]:
        for to_a, steps_a in [still[0]] + moves(first):
            steps = [(p, q) for p in steps_a for q in steps_b]
            if steps == [(0, 0)]:
                continue
            pairs = [
                (a * sizes[1] + b, to_a[a] * sizes[1] + to_b[b])
                for a in range(sizes[0])
                for b in range(sizes[1])
            ]
            blocks.append((lax.ppermute(x, (first, second), pairs), steps))
    return blocks


def sign_of(axis):
    n = lax.axis_size(axis)
    if n > 2 and n % 2 == 0:
        return 1 - 2 * lax.rem(lax.axis_index(axis), 2)
    return jnp.int32(1)


def per_device(positions, charges, masses, weights, mapping, atom_lists, bead_lists, leaving):
    atoms, beads = positions.shape[4], weights.shape[3]
    tiles, groups = atoms // LANES, beads // LANES
    pos = positions.reshape(3 * tiles, LANES)
    charge, mass = charges[0, 0], masses[0, 0]
    weight, label = weights[0, 0], mapping[0, 0]
    leavers = leaving.shape[4]
    height = 4 * (tiles + groups)
    limit = pltpu.CompilerParams(vmem_limit_bytes=48 * 2**20)
    inputs = [
        label, mass, pos, weight, charge,
        atom_lists[0, 0, 0], bead_lists[0, 0, 0], leaving.reshape(1, 2 * leavers),
    ]

    def like(x):
        return jax.ShapeDtypeStruct(x.shape, x.dtype)

    own, mass_sum, hot, label, mass, lists, *small = pl.pallas_call(
        prepare_kernel,
        out_shape=(
            jax.ShapeDtypeStruct((height, LANES), F32),
            jax.ShapeDtypeStruct((groups, LANES), F32),
            jax.ShapeDtypeStruct((LANES, atoms), BF16),
            like(label),
            like(mass),
            *[like(x) for x in inputs[5:]],
        ),
        in_specs=[HBM] * 8,
        out_specs=(VMEM,) * 8,
        scratch_shapes=[
            *[pltpu.VMEM(x.shape, x.dtype) for x in inputs[2:5]],
            pltpu.SemaphoreType.DMA((8,)),
        ],
        compiler_params=pltpu.CompilerParams(vmem_limit_bytes=48 * 2**20),
    )(*[pltpu.with_memory_space_constraint(x, pltpu.HBM) for x in inputs])

    def pairs(lists, near, entries, cells, before, last=False):
        count = len(entries)
        first = before is None
        args = [lists, own, *cells] if first else [lists, own, near, *cells, before]
        place = len(args) - 1
        words = jax.ShapeDtypeStruct((tiles, 3 * -(-9 // number_plan(tiles)[1])), jnp.int32)
        points = jax.ShapeDtypeStruct((tiles, LANES, ROWS), BF16)
        extra = [words, points] if first else []
        shape = (3 * tiles, LANES) if last else (tiles, 4, LANES, LANES)
        work = tiles * count * LANES * LANES
        return pl.pallas_call(
            functools.partial(
                pair_kernel, tiles, groups, entries, len(cells), before is None, last
            ),
            out_shape=(jax.ShapeDtypeStruct(shape, F32), *extra),
            in_specs=[VMEM] * len(args),
            out_specs=(VMEM,) * (1 + len(extra)),
            scratch_shapes=[
                pltpu.VMEM((count, 20 * tiles, LANES), F32),
                pltpu.VMEM((pair_plan(tiles, count)[0], LANES, count * LANES), F32),
            ]
            + ([pltpu.VMEM((4, LANES, LANES), F32)] if last else [])
            + ([pltpu.VMEM((ROWS * tiles, LANES), F32)] if first else []),
            input_output_aliases={} if last or before is None else {place: 0},
            compiler_params=limit,
            cost_estimate=pl.CostEstimate(
                flops=60 * work, bytes_accessed=4 * height * LANES, transcendentals=work
            ),
        )(*args)

    with_x = exchange(own, "gx")
    force, lists, near = pairs(lists, None, [(0, 0, (0, 0, 0))], [own], None)
    column = jnp.concatenate([own] + [block for block, _ in with_x], axis=0)
    column, force = lax.optimization_barrier((column, force))
    cells = [(0, 0)] + [(c + 1, x) for c, (_, steps) in enumerate(with_x) for x in steps]
    with_y = exchange(column, "gy")[::-1]
    entries = [(0, c, (x, 0, 0)) for c, x in cells[1:]]
    force = pairs(lists, near, entries, [column], force)[0]
    near_y, far_y = with_y[:1], with_y[1:]
    if far_y:
        entries = [(0, c, (x, y, 0)) for y in near_y[0][1] for c, x in cells]
        force = pairs(lists, near, entries, [near_y[0][0]], force)[0]
    plane = jnp.concatenate([column] + [block for block, _ in with_y], axis=0)
    plane, force = lax.optimization_barrier((plane, force))
    held = 1 + len(with_x)
    plane_cells = [(c, (x, 0)) for c, x in cells]
    plane_cells += [
        (held * (k + 1) + c, (x, y))
        for k, (_, steps) in enumerate(with_y)
        for y in steps
        for c, x in cells
    ]
    with_z = [(block, z) for block, steps in exchange(plane, "gz") for z in steps][::-1]
    left = far_y[0][1] if far_y else near_y[0][1]
    entries = [(0, c, (x, y, 0)) for c, (x, y) in plane_cells if y in left]
    force = pairs(lists, near, entries, [plane], force)[0]
    for place, (block, z) in enumerate(with_z):
        entries = [(0, c, (x, y, z)) for c, (x, y) in plane_cells]
        force = pairs(lists, near, entries, [block], force, place == 1)[0]

    sources = [plane] + [block for block, _ in with_z]
    z_steps = [0] + [step for _, step in with_z]
    entries = [(s, c, (x, y, z_steps[s])) for s in range(3) for c, (x, y) in plane_cells]
    every, listed = len(entries) * groups, small[0].shape[1]
    scaled, record = pl.pallas_call(
        functools.partial(record_kernel, tiles, groups, entries, len(sources)),
        out_shape=(
            jax.ShapeDtypeStruct((3 * groups, LANES), F32),
            jax.ShapeDtypeStruct((2, 8, leavers), F32),
        ),
        in_specs=[VMEM] * (7 + len(sources)),
        out_specs=(VMEM, VMEM),
        scratch_shapes=[
            pltpu.VMEM((LANES, 2 * leavers), BF16),
            pltpu.VMEM((4, every, LANES), F32),
            pltpu.VMEM((27 * every, LANES), F32),
            pltpu.VMEM(((ROWS + 16) * groups, LANES), F32),
            pltpu.VMEM((groups, LANES, ROWS + 16), BF16),
            *[pltpu.VMEM((LANES, listed * LANES), F32)] * 2,
            pltpu.VMEM((4, LANES, LANES), F32),
            pltpu.VMEM((3 * groups, LANES), F32),
        ],
        compiler_params=limit,
    )(small[0], own, mass_sum, force, label, small[1], hot, *sources)
    forces = pl.pallas_call(
        functools.partial(force_kernel, tiles, groups),
        out_shape=jax.ShapeDtypeStruct((3 * tiles, LANES), F32),
        in_specs=[VMEM] * 5,
        out_specs=VMEM,
        compiler_params=limit,
    )(scaled, force, mass, label, hot)
    n = lax.axis_size("gx")
    if n == 2:
        arrivals = lax.ppermute(record, "gx", [(0, 1), (1, 0)])
    else:
        up = [(i, (i + 1) % n) for i in range(n)]
        down = [(j, i) for i, j in up]
        arrivals = jnp.stack(
            [lax.ppermute(record[0], "gx", up), lax.ppermute(record[1], "gx", down)]
        )
    return (forces.reshape(1, 1, 1, 3, atoms), arrivals[None, None, None])


def solution(mesh):
    cell = ("gx", "gy", "gz")
    placed = (
        P(*cell, None, None),
        P(*cell, None),
        P(*cell, None),
        P(*cell, None),
        P(*cell, None),
        P(*cell, None, None),
        P(*cell, None, None),
        P(*cell, None, None),
    )
    return jax.shard_map(
        per_device,
        mesh=mesh,
        in_specs=placed,
        out_specs=(P(*cell, None, None), P(*cell, None, None, None)),
        check_vma=False,
    )
```

```python
import functools
import itertools
import math

import jax
import jax.numpy as jnp
from jax import lax
from jax.experimental import pallas as pl
from jax.experimental.pallas import tpu as pltpu
from jax.sharding import PartitionSpec as P

SOFT_CORE = 0.01
EPS_COARSE = 2.0
SIGMA_SQ = 0.25
LANES = 128
ROWS = 32
PARTS = 2
F32, BF16 = jnp.float32, jnp.bfloat16
VMEM = pl.BlockSpec(memory_space=pltpu.VMEM)
HBM = pl.BlockSpec(memory_space=pltpu.HBM)
CONTRACT_LANES = (((1,), (1,)), ((), ()))


def split3(v):
    high = v.astype(BF16).astype(F32)
    rest = v - high
    mid = rest.astype(BF16).astype(F32)
    return high, mid, rest - mid


def far_rows(coords, soft):
    parts = [split3(v) for v in coords]
    norm = coords[0] * coords[0] + coords[1] * coords[1] + (coords[2] * coords[2] + soft)
    nh, nm, nl = split3(norm)
    one = jnp.ones_like(norm)
    rows = [p[0] for p in parts] + [p[1] for p in parts] + [nh, nm]
    return rows + [p[2] for p in parts] + [nl, one, one, one, jnp.zeros_like(one)]


def near_rows(coords, scale):
    parts = [[-2.0 * scale * part for part in split3(v)] for v in coords]
    norm = scale * (coords[0] * coords[0] + coords[1] * coords[1] + coords[2] * coords[2])
    one, zero = jnp.full_like(norm, scale), jnp.zeros_like(norm)
    h, m, l = ([p[k] for p in parts] for k in range(3))
    rows = h + h + [one, one] + m + m + [zero, zero] + l + l + [zero, zero]
    return rows + h + [one] + list(split3(norm)) + [zero]


def picked_rows(far, k, stride):
    first = far[pl.ds(k, 8, stride=stride), :]
    last = far[pl.ds(k + 8 * stride, 8, stride=stride), :]
    return jnp.concatenate([first, first, first, last], axis=0).astype(BF16)


def one_hot(label_ref, out_ref, tiles):
    ids = lax.broadcasted_iota(jnp.int32, (LANES, LANES), 0)
    for t in range(tiles):
        at = slice(t * LANES, (t + 1) * LANES)
        low = lax.rem(label_ref[:, at], LANES)
        out_ref[:, at] = jnp.where(ids == low, 1.0, 0.0).astype(BF16)


def high_mask(label, groups, repeat):
    ids = lax.broadcasted_iota(jnp.int32, (groups, label.shape[1]), 0)
    hit = (ids == label // LANES).astype(F32)
    return jnp.concatenate([hit] * repeat, axis=0)


def stacked3(v):
    return jnp.concatenate(list(split3(v)), axis=0).astype(BF16)


def fold3(v):
    n = v.shape[0] // 3
    return v[:n] + v[n : 2 * n] + v[2 * n :]


def gather_rows(table, label, hot, groups):
    features = table.shape[0] // groups
    picked = fold3(jnp.dot(stacked3(table), hot, preferred_element_type=F32))
    picked = picked * high_mask(label, groups, features)
    return [
        jnp.sum(picked[f * groups : (f + 1) * groups], axis=0, keepdims=True)
        for f in range(features)
    ]


def sum_rows(values, label, hot, groups):
    spread = jnp.concatenate([jnp.broadcast_to(v, (groups, v.shape[1])) for v in values], axis=0)
    spread = spread * high_mask(label, groups, len(values))
    return fold3(
        lax.dot_general(stacked3(spread), hot, CONTRACT_LANES, preferred_element_type=F32)
    )


def flat_row(ref, first, tiles):
    return jnp.concatenate([ref[first + t : first + t + 1, :] for t in range(tiles)], axis=1)


def signs_here():
    return [sign_of(axis) for axis in ("gx", "gy", "gz")]


def column_of(step):
    return 9 * (step[0] + 1) + 3 * (step[1] + 1) + (step[2] + 1)


def number_plan(tiles):
    bits = max((tiles - 1).bit_length(), 1)
    return bits, min(31 // bits, 9)


def place_of(step, tiles):
    bits, share = number_plan(tiles)
    order = 3 * (step[0] + 1) + (step[1] + 1)
    return -(-9 // share) * (step[2] + 1) + order // share, bits * (order % share)


def packed_numbers(lists, tiles):
    numbers = lists - tiles * lax.broadcasted_iota(jnp.int32, lists.shape, 1)
    for sign, width in zip(signs_here(), (9, 3, 1)):
        pieces = []
        for start in range(0, 27, 3 * width):
            for k in (2, 1, 0):
                pieces.append(numbers[:, start + k * width : start + (k + 1) * width])
        numbers = jnp.where(sign < 0, jnp.concatenate(pieces, axis=1), numbers)
    words = {}
    for x, y, z in itertools.product((-1, 0, 1), repeat=3):
        word, shift = place_of((x, y, z), tiles)
        column = column_of((x, y, z))
        piece = lax.shift_left(numbers[:, column : column + 1], jnp.int32(shift))
        words[word] = words[word] + piece if word in words else piece
    return jnp.concatenate([words[word] for word in sorted(words)], axis=1)


def as_float(step):
    return float(step) if isinstance(step, int) else step.astype(F32)


def pair_plan(tiles, count):
    held, ahead = (8, 6) if count == 1 else (8, 4) if count == 2 else (2, 1)
    unroll = 8 if count < 6 else 4
    if tiles % unroll:
        held, unroll, ahead = 2, 2, 1
    return held, unroll, ahead


def prepare_kernel(
    label_in, mass_in, pos_in, weight_in, charge_in, lists_in, bead_lists_in, leaving_in,
    rows_out, mass_out, hot, label_ref, mass, lists_out, bead_lists_out, leaving_out,
    pos, weight, charge, sem,
):
    moves = [
        (label_in, label_ref), (mass_in, mass), (pos_in, pos), (weight_in, weight),
        (charge_in, charge), (lists_in, lists_out), (bead_lists_in, bead_lists_out),
        (leaving_in, leaving_out),
    ]
    copies = [pltpu.make_async_copy(a, b, sem.at[i]) for i, (a, b) in enumerate(moves)]
    for copy in copies:
        copy.start()
    beads = weight.shape[1]
    tiles, groups = pos.shape[0] // 3, beads // LANES
    copies[0].wait()
    one_hot(label_ref, hot, tiles)
    label = label_ref[...]
    copies[1].wait()
    copies[2].wait()
    m = mass[...]
    values = [m * flat_row(pos, k * tiles, tiles) for k in range(3)] + [m]
    sums = sum_rows(values, label, hot[...], groups)
    mass_sum = sums[3 * groups :]
    mass_out[...] = mass_sum
    for copy in copies[3:]:
        copy.wait()
    table = jnp.concatenate(
        [weight[:, g * LANES : (g + 1) * LANES] for g in range(groups)], axis=0
    )
    charged = charge[...] * gather_rows(table, label, hot[...], groups)[0]
    rows_out[: 3 * tiles, :] = pos[...]
    for t in range(tiles):
        at = slice(t * LANES, (t + 1) * LANES)
        rows_out[3 * tiles + t : 3 * tiles + t + 1, :] = charged[:, at]
    base = 4 * tiles
    for k in range(3):
        rows_out[base + k * groups : base + (k + 1) * groups, :] = (
            sums[k * groups : (k + 1) * groups] / mass_sum
        )
    rows_out[base + 3 * groups : base + 4 * groups, :] = table


def pair_kernel(tiles, groups, entries, sources, first, last, *refs):
    numbers, own = refs[:2]
    near = None if first else refs[2]
    refs = refs[2 if first else 3 :]
    cells = refs[:sources]
    rest = refs[sources:]
    before = None if first else rest[0]
    rest = rest[0 if first else 1 :]
    if first:
        rest[1][...] = packed_numbers(numbers[...], tiles)
        numbers, near, rest = rest[1], rest[2], rest[:1] + rest[3:]
        coords = [own[k * tiles : (k + 1) * tiles, :] - 0.5 for k in range(3)]
        for r, row in enumerate(near_rows(coords, 1.0)):
            rest[-1][r * tiles : (r + 1) * tiles, :] = row
        for t in range(tiles):
            near[t] = rest[-1][pl.ds(t, ROWS, stride=tiles), :].T.astype(BF16)
    out, far, held = rest[:3]
    total = rest[-1] if last else None
    count = len(entries)
    height = 4 * (tiles + groups)
    signs = signs_here()
    places = []
    for e, (source, cell, steps) in enumerate(entries):
        step = [steps[k] * signs[k] if steps[k] else 0 for k in range(3)]
        places.append(place_of(steps, tiles))
        base = cell * height
        coords = [
            cells[source][base + k * tiles : base + (k + 1) * tiles, :]
            + (as_float(step[k]) - 0.5)
            for k in range(3)
        ]
        charged = cells[source][base + 3 * tiles : base + 4 * tiles, :]
        for r, row in enumerate(far_rows(coords, SOFT_CORE) + coords + [charged]):
            far[e, r * tiles : (r + 1) * tiles, :] = row

    bits = number_plan(tiles)[0]

    used = sorted({word for word, _ in places})

    def words_of(t):
        row = numbers[pl.ds(t, 1), :]
        return tuple(row[0, word] for word in used)

    def numbers_of(words):
        words = dict(zip(used, words))
        return [
            lax.bitwise_and(
                lax.shift_right_logical(words[word], jnp.int32(shift)), jnp.int32((1 << bits) - 1)
            )
            for word, shift in places
        ]

    def distances(t, into, ks, part=None):
        lhs = near[t]
        starts = list(range(0, count, 2))
        if part is not None:
            starts = starts[part::PARTS]
        for e in starts:
            members = range(e, min(e + 2, count))
            rhs = [
                picked_rows(far.at[m], ks[m], tiles) for m in members
            ]
            rhs = jnp.concatenate(rhs, axis=1) if len(rhs) > 1 else rhs[0]
            inv = lax.rsqrt(jnp.dot(lhs, rhs, preferred_element_type=F32))
            charged = [far[m, pl.ds(19 * tiles + ks[m], 1), :] for m in members]
            charged = jnp.concatenate(charged, axis=1) if len(charged) > 1 else charged[0]
            into[:, e * LANES : e * LANES + rhs.shape[1]] = inv * inv * inv * charged

    def strengths(t, dist, ks, part):
        block = LANES // PARTS
        at = slice(part * block, (part + 1) * block)
        if True:
            if before is None:
                acc = [jnp.zeros((block, LANES), F32)] * 4
            else:
                acc = [before[t, d, at, :] for d in range(4)]
            for e in range(count):
                k = ks[e]
                s = dist[at, e * LANES : (e + 1) * LANES]
                acc[3] = acc[3] + s
                for d in range(3):
                    acc[d] = acc[d] + s * far[e, pl.ds((16 + d) * tiles + k, 1), :]
            for d in range(4):
                if last:
                    total[d, at, :] = acc[d]
                else:
                    out[t, d, at, :] = acc[d]
        if not last or part < PARTS - 1:
            return
        sums = [jnp.sum(total[d].T, axis=0, keepdims=True) for d in range(4)]
        scale = own[pl.ds(3 * tiles + t, 1), :]
        for d in range(3):
            here = own[pl.ds(d * tiles + t, 1), :] - 0.5
            out[pl.ds(d * tiles + t, 1), :] = scale * (here * sums[3] - sums[d])

    buffered, unroll, ahead = pair_plan(tiles, count)
    buffers = [held.at[i] for i in range(buffered)]
    words = [words_of(min(i, tiles - 1)) for i in range(unroll + ahead)]
    for i in range(ahead):
        distances(i, buffers[i], numbers_of(words[i]))

    def some_tiles(step, words):
        following = [
            words_of(jnp.minimum(unroll * (step + 1) + ahead + u, tiles - 1)) for u in range(unroll)
        ]
        for u in range(unroll):
            t = unroll * step + u
            later = jnp.minimum(t + ahead, tiles - 1)
            ks, ks_later = numbers_of(words[u]), numbers_of(words[u + ahead])
            for part in range(PARTS):
                distances(later, buffers[(u + ahead) % buffered], ks_later, part)
                strengths(t, buffers[u % buffered], ks, part)
        return tuple(words[unroll:]) + tuple(following)

    lax.fori_loop(0, tiles // unroll, some_tiles, tuple(words))


def weight_rows(weight):
    h, m, l = split3(weight)
    return [h, h, h, m, m, l], [h, m, l, h, m, h]


def force_kernel(tiles, groups, scaled, atomic, mass, label_ref, hot, forces_out):
    spread = gather_rows(scaled[...], label_ref[...], hot[...], groups)
    for d in range(3):
        added = mass[...] * spread[d]
        for t in range(tiles):
            row = slice(d * tiles + t, d * tiles + t + 1)
            forces_out[row, :] = atomic[row, :] + added[:, t * LANES : (t + 1) * LANES]


def record_kernel(tiles, groups, entries, sources, *refs):
    lists_ref, own, mass_sum_ref, atomic, label_ref, leave_ref, hot = refs[:7]
    cells = refs[7 : 7 + sources]
    rest = refs[7 + sources :]
    scaled_out, record_out, leave_hot, raw, far, near, nearest = rest[:7]
    buffers, (total, coarse) = rest[7:9], rest[9:]
    lists, listed = lists_ref[...], lists_ref.shape[1]
    height = 4 * (tiles + groups)
    signs = signs_here()
    every = len(entries) * groups
    for source, cell, steps in entries:
        step = [steps[k] * signs[k] if steps[k] else 0 for k in range(3)]
        column = column_of(step)
        base = cell * height + 4 * tiles
        for k in range(4):
            block = cells[source][base + k * groups : base + (k + 1) * groups, :]
            if k < 3:
                block = block + (as_float(step[k]) - 0.5)
            raw[k, pl.ds(column * groups, groups), :] = block
    scale = math.sqrt(math.log2(math.e) / SIGMA_SQ)
    coords = [raw[k] for k in range(3)]
    one, zero = jnp.ones_like(coords[0]), jnp.zeros_like(coords[0])
    plain = coords + weight_rows(raw[3])[0] + [one, zero]
    for r, row in enumerate(far_rows([scale * v for v in coords], 0.0) + plain):
        far[r * every : (r + 1) * every, :] = row
    base = 4 * tiles
    coords = [own[base + k * groups : base + (k + 1) * groups, :] - 0.5 for k in range(3)]
    own_weight = own[base + 3 * groups : base + 4 * groups, :]
    zero = jnp.zeros_like(own_weight)
    factors = [-EPS_COARSE * row for row in weight_rows(own_weight)[1]]
    factors += [zero + EPS_COARSE, zero] + [zero] * 8
    for r, row in enumerate(near_rows([scale * v for v in coords], -1.0) + factors):
        near[r * groups : (r + 1) * groups, :] = row
    for b in range(groups):
        nearest[b] = near[pl.ds(b, ROWS + 16, stride=groups), :].T.astype(BF16)

    def products(b, into):
        lhs = nearest[b]
        for e in range(0, listed, 2):
            members = [lists[b, m] for m in range(e, min(e + 2, listed))]
            rhs = jnp.concatenate([picked_rows(far, k, every) for k in members], axis=1)
            dist = jnp.dot(lhs[:, :ROWS], rhs, preferred_element_type=F32)
            rhs = [far[pl.ds(k + 19 * every, 8, stride=every), :] for k in members]
            rhs = jnp.concatenate([jnp.concatenate([r, r], axis=0) for r in rhs], axis=1)
            factor = jnp.dot(lhs[:, ROWS:], rhs.astype(BF16), preferred_element_type=F32)
            into[:, e * LANES : (e + len(members)) * LANES] = jnp.exp2(dist) * factor

    def strengths(b, held):
        block = LANES // PARTS
        for part in range(PARTS):
            at = slice(part * block, (part + 1) * block)
            acc = [jnp.zeros((block, LANES), F32)] * 4
            for e in range(listed):
                k = lists[b, e]
                s = held[at, e * LANES : (e + 1) * LANES]
                acc[3] = acc[3] + s
                for d in range(3):
                    acc[d] = acc[d] + s * far[pl.ds((16 + d) * every + k, 1), :]
            for d in range(4):
                total[d, at, :] = acc[d]
        sums = [jnp.sum(total[d].T, axis=0, keepdims=True) for d in range(4)]
        for d in range(3):
            centre = own[base + d * groups + b : base + d * groups + b + 1, :] - 0.5
            coarse[d * groups + b : d * groups + b + 1, :] = centre * sums[3] - sums[d]

    products(0, buffers[0])
    for b in range(groups):
        if b + 1 < groups:
            products(b + 1, buffers[(b + 1) % 2])
        strengths(b, buffers[b % 2])

    mass_sum = mass_sum_ref[...]
    flat = [flat_row(atomic, d * tiles, tiles) for d in range(3)]
    summed = sum_rows(flat, label_ref[...], hot[...], groups)
    scaled_out[...] = coarse[...] / jnp.concatenate([mass_sum] * 3, axis=0)
    molecule = summed + coarse[...]
    table = jnp.concatenate(
        [own[base : base + 3 * groups, :], molecule, own_weight, mass_sum], axis=0
    )
    leavers = leave_ref.shape[1] // 2
    one_hot(leave_ref, leave_hot, leave_ref.shape[1] // LANES)
    picked = gather_rows(table, leave_ref[...], leave_hot[...], groups)
    for side, shift in ((0, -1.0), (1, 1.0)):
        for f in range(8):
            row = picked[f][:, side * leavers : (side + 1) * leavers]
            record_out[side, f : f + 1, :] = row + shift if f == 0 else row


def moves(axis):
    n = lax.axis_size(axis)
    if n <= 2:
        return [([n - 1 - i for i in range(n)], (1, -1))]
    if n % 2 == 0:
        inner = [i ^ 1 for i in range(n)]
        return [([(((i + 1) ^ 1) - 1) % n for i in range(n)], (-1,)), (inner, (1,))]
    return [([(i + 1) % n for i in range(n)], (-1,)), ([(i - 1) % n for i in range(n)], (1,))]


def exchange(x, axis):
    return [
        (lax.ppermute(x, axis, list(enumerate(receivers))), steps)
        for receivers, steps in moves(axis)
    ]


def exchange_plane(x, first, second):
    sizes = lax.axis_size(first), lax.axis_size(second)
    still = [(list(range(n)), (0,)) for n in sizes]
    blocks = []
    for to_b, steps_b in moves(second) + [still[1]]:
        for to_a, steps_a in [still[0]] + moves(first):
            steps = [(p, q) for p in steps_a for q in steps_b]
            if steps == [(0, 0)]:
                continue
            pairs = [
                (a * sizes[1] + b, to_a[a] * sizes[1] + to_b[b])
                for a in range(sizes[0])
                for b in range(sizes[1])
            ]
            blocks.append((lax.ppermute(x, (first, second), pairs), steps))
    return blocks


def sign_of(axis):
    n = lax.axis_size(axis)
    if n > 2 and n % 2 == 0:
        return 1 - 2 * lax.rem(lax.axis_index(axis), 2)
    return jnp.int32(1)


def per_device(positions, charges, masses, weights, mapping, atom_lists, bead_lists, leaving):
    atoms, beads = positions.shape[4], weights.shape[3]
    tiles, groups = atoms // LANES, beads // LANES
    pos = positions.reshape(3 * tiles, LANES)
    charge, mass = charges[0, 0], masses[0, 0]
    weight, label = weights[0, 0], mapping[0, 0]
    leavers = leaving.shape[4]
    height = 4 * (tiles + groups)
    limit = pltpu.CompilerParams(vmem_limit_bytes=48 * 2**20)
    inputs = [
        label, mass, pos, weight, charge,
        atom_lists[0, 0, 0], bead_lists[0, 0, 0], leaving.reshape(1, 2 * leavers),
    ]

    def like(x):
        return jax.ShapeDtypeStruct(x.shape, x.dtype)

    own, mass_sum, hot, label, mass, lists, *small = pl.pallas_call(
        prepare_kernel,
        out_shape=(
            jax.ShapeDtypeStruct((height, LANES), F32),
            jax.ShapeDtypeStruct((groups, LANES), F32),
            jax.ShapeDtypeStruct((LANES, atoms), BF16),
            like(label),
            like(mass),
            *[like(x) for x in inputs[5:]],
        ),
        in_specs=[HBM] * 8,
        out_specs=(VMEM,) * 8,
        scratch_shapes=[
            *[pltpu.VMEM(x.shape, x.dtype) for x in inputs[2:5]],
            pltpu.SemaphoreType.DMA((8,)),
        ],
        compiler_params=pltpu.CompilerParams(vmem_limit_bytes=48 * 2**20),
    )(*[pltpu.with_memory_space_constraint(x, pltpu.HBM) for x in inputs])

    def pairs(lists, near, entries, cells, before, last=False):
        count = len(entries)
        first = before is None
        args = [lists, own, *cells] if first else [lists, own, near, *cells, before]
        place = len(args) - 1
        words = jax.ShapeDtypeStruct((tiles, 3 * -(-9 // number_plan(tiles)[1])), jnp.int32)
        points = jax.ShapeDtypeStruct((tiles, LANES, ROWS), BF16)
        extra = [words, points] if first else []
        shape = (3 * tiles, LANES) if last else (tiles, 4, LANES, LANES)
        work = tiles * count * LANES * LANES
        return pl.pallas_call(
            functools.partial(
                pair_kernel, tiles, groups, entries, len(cells), before is None, last
            ),
            out_shape=(jax.ShapeDtypeStruct(shape, F32), *extra),
            in_specs=[VMEM] * len(args),
            out_specs=(VMEM,) * (1 + len(extra)),
            scratch_shapes=[
                pltpu.VMEM((count, 20 * tiles, LANES), F32),
                pltpu.VMEM((pair_plan(tiles, count)[0], LANES, count * LANES), F32),
            ]
            + ([pltpu.VMEM((4, LANES, LANES), F32)] if last else [])
            + ([pltpu.VMEM((ROWS * tiles, LANES), F32)] if first else []),
            input_output_aliases={} if last or before is None else {place: 0},
            compiler_params=limit,
            cost_estimate=pl.CostEstimate(
                flops=60 * work, bytes_accessed=4 * height * LANES, transcendentals=work
            ),
        )(*args)

    with_x = exchange(own, "gx")
    force, lists, near = pairs(lists, None, [(0, 0, (0, 0, 0))], [own], None)
    column = jnp.concatenate([own] + [block for block, _ in with_x], axis=0)
    column, force = lax.optimization_barrier((column, force))
    cells = [(0, 0)] + [(c + 1, x) for c, (_, steps) in enumerate(with_x) for x in steps]
    with_y = exchange(column, "gy")[::-1]
    entries = [(0, c, (x, 0, 0)) for c, x in cells[1:]]
    force = pairs(lists, near, entries, [column], force)[0]
    near_y, far_y = with_y[:1], with_y[1:]
    if far_y:
        entries = [(0, c, (x, y, 0)) for y in near_y[0][1] for c, x in cells]
        force = pairs(lists, near, entries, [near_y[0][0]], force)[0]
    plane = jnp.concatenate([column] + [block for block, _ in with_y], axis=0)
    plane, force = lax.optimization_barrier((plane, force))
    held = 1 + len(with_x)
    plane_cells = [(c, (x, 0)) for c, x in cells]
    plane_cells += [
        (held * (k + 1) + c, (x, y))
        for k, (_, steps) in enumerate(with_y)
        for y in steps
        for c, x in cells
    ]
    with_z = [(block, z) for block, steps in exchange(plane, "gz") for z in steps][::-1]
    left = far_y[0][1] if far_y else near_y[0][1]
    entries = [(0, c, (x, y, 0)) for c, (x, y) in plane_cells if y in left]
    force = pairs(lists, near, entries, [plane], force)[0]
    for place, (block, z) in enumerate(with_z):
        entries = [(0, c, (x, y, z)) for c, (x, y) in plane_cells]
        force = pairs(lists, near, entries, [block], force, place == 1)[0]

    sources = [plane] + [block for block, _ in with_z]
    z_steps = [0] + [step for _, step in with_z]
    entries = [(s, c, (x, y, z_steps[s])) for s in range(3) for c, (x, y) in plane_cells]
    every, listed = len(entries) * groups, small[0].shape[1]
    scaled, record = pl.pallas_call(
        functools.partial(record_kernel, tiles, groups, entries, len(sources)),
        out_shape=(
            jax.ShapeDtypeStruct((3 * groups, LANES), F32),
            jax.ShapeDtypeStruct((2, 8, leavers), F32),
        ),
        in_specs=[VMEM] * (7 + len(sources)),
        out_specs=(VMEM, VMEM),
        scratch_shapes=[
            pltpu.VMEM((LANES, 2 * leavers), BF16),
            pltpu.VMEM((4, every, LANES), F32),
            pltpu.VMEM((27 * every, LANES), F32),
            pltpu.VMEM(((ROWS + 16) * groups, LANES), F32),
            pltpu.VMEM((groups, LANES, ROWS + 16), BF16),
            *[pltpu.VMEM((LANES, listed * LANES), F32)] * 2,
            pltpu.VMEM((4, LANES, LANES), F32),
            pltpu.VMEM((3 * groups, LANES), F32),
        ],
        compiler_params=limit,
    )(small[0], own, mass_sum, force, label, small[1], hot, *sources)
    forces = pl.pallas_call(
        functools.partial(force_kernel, tiles, groups),
        out_shape=jax.ShapeDtypeStruct((3 * tiles, LANES), F32),
        in_specs=[VMEM] * 5,
        out_specs=VMEM,
        compiler_params=limit,
    )(scaled, force, mass, label, hot)
    n = lax.axis_size("gx")
    if n == 2:
        arrivals = lax.ppermute(record, "gx", [(0, 1), (1, 0)])
    else:
        up = [(i, (i + 1) % n) for i in range(n)]
        down = [(j, i) for i, j in up]
        arrivals = jnp.stack(
            [lax.ppermute(record[0], "gx", up), lax.ppermute(record[1], "gx", down)]
        )
    return (forces.reshape(1, 1, 1, 3, atoms), arrivals[None, None, None])


def solution(mesh):
    cell = ("gx", "gy", "gz")
    placed = (
        P(*cell, None, None),
        P(*cell, None),
        P(*cell, None),
        P(*cell, None),
        P(*cell, None),
        P(*cell, None, None),
        P(*cell, None, None),
        P(*cell, None, None),
    )
    return jax.shard_map(
        per_device,
        mesh=mesh,
        in_specs=placed,
        out_specs=(P(*cell, None, None), P(*cell, None, None, None)),
        check_vma=False,
    )
```

```python
import functools
import itertools
import math

import jax
import jax.numpy as jnp
from jax import lax
from jax.experimental import pallas as pl
from jax.experimental.pallas import tpu as pltpu
from jax.sharding import PartitionSpec as P

SOFT_CORE = 0.01
EPS_COARSE = 2.0
SIGMA_SQ = 0.25
LANES = 128
ROWS = 32
PARTS = 2
F32, BF16 = jnp.float32, jnp.bfloat16
VMEM = pl.BlockSpec(memory_space=pltpu.VMEM)
HBM = pl.BlockSpec(memory_space=pltpu.HBM)
CONTRACT_LANES = (((1,), (1,)), ((), ()))


def split3(v):
    high = v.astype(BF16).astype(F32)
    rest = v - high
    mid = rest.astype(BF16).astype(F32)
    return high, mid, rest - mid


def far_rows(coords, soft):
    parts = [split3(v) for v in coords]
    norm = coords[0] * coords[0] + coords[1] * coords[1] + (coords[2] * coords[2] + soft)
    nh, nm, nl = split3(norm)
    one = jnp.ones_like(norm)
    rows = [p[0] for p in parts] + [p[1] for p in parts] + [nh, nm]
    return rows + [p[2] for p in parts] + [nl, one, one, one, jnp.zeros_like(one)]


def near_rows(coords, scale):
    parts = [[-2.0 * scale * part for part in split3(v)] for v in coords]
    norm = scale * (coords[0] * coords[0] + coords[1] * coords[1] + coords[2] * coords[2])
    one, zero = jnp.full_like(norm, scale), jnp.zeros_like(norm)
    h, m, l = ([p[k] for p in parts] for k in range(3))
    rows = h + h + [one, one] + m + m + [zero, zero] + l + l + [zero, zero]
    return rows + h + [one] + list(split3(norm)) + [zero]


def picked_rows(far, k, stride):
    first = far[pl.ds(k, 8, stride=stride), :]
    last = far[pl.ds(k + 8 * stride, 8, stride=stride), :]
    return jnp.concatenate([first, first, first, last], axis=0).astype(BF16)


def one_hot(label_ref, out_ref, tiles):
    ids = lax.broadcasted_iota(jnp.int32, (LANES, LANES), 0)
    for t in range(tiles):
        at = slice(t * LANES, (t + 1) * LANES)
        low = lax.rem(label_ref[:, at], LANES)
        out_ref[:, at] = jnp.where(ids == low, 1.0, 0.0).astype(BF16)


def high_mask(label, groups, repeat):
    ids = lax.broadcasted_iota(jnp.int32, (groups, label.shape[1]), 0)
    hit = (ids == label // LANES).astype(F32)
    return jnp.concatenate([hit] * repeat, axis=0)


def stacked3(v):
    return jnp.concatenate(list(split3(v)), axis=0).astype(BF16)


def fold3(v):
    n = v.shape[0] // 3
    return v[:n] + v[n : 2 * n] + v[2 * n :]


def gather_rows(table, label, hot, groups):
    features = table.shape[0] // groups
    picked = fold3(jnp.dot(stacked3(table), hot, preferred_element_type=F32))
    picked = picked * high_mask(label, groups, features)
    return [
        jnp.sum(picked[f * groups : (f + 1) * groups], axis=0, keepdims=True)
        for f in range(features)
    ]


def sum_rows(values, label, hot, groups):
    spread = jnp.concatenate([jnp.broadcast_to(v, (groups, v.shape[1])) for v in values], axis=0)
    spread = spread * high_mask(label, groups, len(values))
    return fold3(
        lax.dot_general(stacked3(spread), hot, CONTRACT_LANES, preferred_element_type=F32)
    )


def flat_row(ref, first, tiles):
    return jnp.concatenate([ref[first + t : first + t + 1, :] for t in range(tiles)], axis=1)


def signs_here():
    return [sign_of(axis) for axis in ("gx", "gy", "gz")]


def column_of(step):
    return 9 * (step[0] + 1) + 3 * (step[1] + 1) + (step[2] + 1)


def number_plan(tiles):
    bits = max((tiles - 1).bit_length(), 1)
    return bits, min(31 // bits, 9)


def place_of(step, tiles):
    bits, share = number_plan(tiles)
    order = 3 * (step[0] + 1) + (step[1] + 1)
    return -(-9 // share) * (step[2] + 1) + order // share, bits * (order % share)


def packed_numbers(lists, tiles):
    numbers = lists - tiles * lax.broadcasted_iota(jnp.int32, lists.shape, 1)
    for sign, width in zip(signs_here(), (9, 3, 1)):
        pieces = []
        for start in range(0, 27, 3 * width):
            for k in (2, 1, 0):
                pieces.append(numbers[:, start + k * width : start + (k + 1) * width])
        numbers = jnp.where(sign < 0, jnp.concatenate(pieces, axis=1), numbers)
    words = {}
    for x, y, z in itertools.product((-1, 0, 1), repeat=3):
        word, shift = place_of((x, y, z), tiles)
        column = column_of((x, y, z))
        piece = lax.shift_left(numbers[:, column : column + 1], jnp.int32(shift))
        words[word] = words[word] + piece if word in words else piece
    return jnp.concatenate([words[word] for word in sorted(words)], axis=1)


def as_float(step):
    return float(step) if isinstance(step, int) else step.astype(F32)


def pair_plan(tiles, count):
    held, ahead = (8, 6) if count == 1 else (4, 2) if count == 2 else (2, 1)
    unroll = 8 if count < 6 else 4
    if tiles % unroll:
        held, unroll, ahead = 2, 2, 1
    return held, unroll, ahead


def prepare_kernel(
    label_in, mass_in, pos_in, weight_in, charge_in, lists_in, bead_lists_in, leaving_in,
    rows_out, mass_out, hot, label_ref, mass, lists_out, bead_lists_out, leaving_out,
    pos, weight, charge, sem,
):
    moves = [
        (label_in, label_ref), (mass_in, mass), (pos_in, pos), (weight_in, weight),
        (charge_in, charge), (lists_in, lists_out), (bead_lists_in, bead_lists_out),
        (leaving_in, leaving_out),
    ]
    copies = [pltpu.make_async_copy(a, b, sem.at[i]) for i, (a, b) in enumerate(moves)]
    for copy in copies:
        copy.start()
    beads = weight.shape[1]
    tiles, groups = pos.shape[0] // 3, beads // LANES
    copies[0].wait()
    one_hot(label_ref, hot, tiles)
    label = label_ref[...]
    copies[1].wait()
    copies[2].wait()
    m = mass[...]
    values = [m * flat_row(pos, k * tiles, tiles) for k in range(3)] + [m]
    sums = sum_rows(values, label, hot[...], groups)
    mass_sum = sums[3 * groups :]
    mass_out[...] = mass_sum
    for copy in copies[3:]:
        copy.wait()
    table = jnp.concatenate(
        [weight[:, g * LANES : (g + 1) * LANES] for g in range(groups)], axis=0
    )
    charged = charge[...] * gather_rows(table, label, hot[...], groups)[0]
    rows_out[: 3 * tiles, :] = pos[...]
    for t in range(tiles):
        at = slice(t * LANES, (t + 1) * LANES)
        rows_out[3 * tiles + t : 3 * tiles + t + 1, :] = charged[:, at]
    base = 4 * tiles
    for k in range(3):
        rows_out[base + k * groups : base + (k + 1) * groups, :] = (
            sums[k * groups : (k + 1) * groups] / mass_sum
        )
    rows_out[base + 3 * groups : base + 4 * groups, :] = table


def pair_kernel(tiles, groups, entries, sources, first, last, *refs):
    numbers, own = refs[:2]
    near = None if first else refs[2]
    refs = refs[2 if first else 3 :]
    cells = refs[:sources]
    rest = refs[sources:]
    before = None if first else rest[0]
    rest = rest[0 if first else 1 :]
    if first:
        rest[1][...] = packed_numbers(numbers[...], tiles)
        numbers, near, rest = rest[1], rest[2], rest[:1] + rest[3:]
        coords = [own[k * tiles : (k + 1) * tiles, :] - 0.5 for k in range(3)]
        for r, row in enumerate(near_rows(coords, 1.0)):
            rest[-1][r * tiles : (r + 1) * tiles, :] = row
        for t in range(tiles):
            near[t] = rest[-1][pl.ds(t, ROWS, stride=tiles), :].T.astype(BF16)
    out, far, held = rest[:3]
    total = rest[-1] if last else None
    count = len(entries)
    height = 4 * (tiles + groups)
    signs = signs_here()
    places = []
    for e, (source, cell, steps) in enumerate(entries):
        step = [steps[k] * signs[k] if steps[k] else 0 for k in range(3)]
        places.append(place_of(steps, tiles))
        base = cell * height
        coords = [
            cells[source][base + k * tiles : base + (k + 1) * tiles, :]
            + (as_float(step[k]) - 0.5)
            for k in range(3)
        ]
        charged = cells[source][base + 3 * tiles : base + 4 * tiles, :]
        for r, row in enumerate(far_rows(coords, SOFT_CORE) + coords + [charged]):
            far[e, r * tiles : (r + 1) * tiles, :] = row

    bits = number_plan(tiles)[0]

    used = sorted({word for word, _ in places})

    def words_of(t):
        row = numbers[pl.ds(t, 1), :]
        return tuple(row[0, word] for word in used)

    def numbers_of(words):
        words = dict(zip(used, words))
        return [
            lax.bitwise_and(
                lax.shift_right_logical(words[word], jnp.int32(shift)), jnp.int32((1 << bits) - 1)
            )
            for word, shift in places
        ]

    def distances(t, into, ks, part=None):
        lhs = near[t]
        starts = list(range(0, count, 2))
        if part is not None:
            starts = starts[part::PARTS]
        for e in starts:
            members = range(e, min(e + 2, count))
            rhs = [
                picked_rows(far.at[m], ks[m], tiles) for m in members
            ]
            rhs = jnp.concatenate(rhs, axis=1) if len(rhs) > 1 else rhs[0]
            inv = lax.rsqrt(jnp.dot(lhs, rhs, preferred_element_type=F32))
            charged = [far[m, pl.ds(19 * tiles + ks[m], 1), :] for m in members]
            charged = jnp.concatenate(charged, axis=1) if len(charged) > 1 else charged[0]
            into[:, e * LANES : e * LANES + rhs.shape[1]] = inv * inv * inv * charged

    def strengths(t, dist, ks, part):
        block = LANES // PARTS
        at = slice(part * block, (part + 1) * block)
        if True:
            if before is None:
                acc = [jnp.zeros((block, LANES), F32)] * 4
            else:
                acc = [before[t, d, at, :] for d in range(4)]
            for e in range(count):
                k = ks[e]
                s = dist[at, e * LANES : (e + 1) * LANES]
                acc[3] = acc[3] + s
                for d in range(3):
                    acc[d] = acc[d] + s * far[e, pl.ds((16 + d) * tiles + k, 1), :]
            for d in range(4):
                if last:
                    total[d, at, :] = acc[d]
                else:
                    out[t, d, at, :] = acc[d]
        if not last or part < PARTS - 1:
            return
        sums = [jnp.sum(total[d].T, axis=0, keepdims=True) for d in range(4)]
        scale = own[pl.ds(3 * tiles + t, 1), :]
        for d in range(3):
            here = own[pl.ds(d * tiles + t, 1), :] - 0.5
            out[pl.ds(d * tiles + t, 1), :] = scale * (here * sums[3] - sums[d])

    buffered, unroll, ahead = pair_plan(tiles, count)
    buffers = [held.at[i] for i in range(buffered)]
    words = [words_of(min(i, tiles - 1)) for i in range(unroll + ahead)]
    for i in range(ahead):
        distances(i, buffers[i], numbers_of(words[i]))

    def some_tiles(step, words):
        following = [
            words_of(jnp.minimum(unroll * (step + 1) + ahead + u, tiles - 1)) for u in range(unroll)
        ]
        for u in range(unroll):
            t = unroll * step + u
            later = jnp.minimum(t + ahead, tiles - 1)
            ks, ks_later = numbers_of(words[u]), numbers_of(words[u + ahead])
            for part in range(PARTS):
                distances(later, buffers[(u + ahead) % buffered], ks_later, part)
                strengths(t, buffers[u % buffered], ks, part)
        return tuple(words[unroll:]) + tuple(following)

    lax.fori_loop(0, tiles // unroll, some_tiles, tuple(words))


def weight_rows(weight):
    h, m, l = split3(weight)
    return [h, h, h, m, m, l], [h, m, l, h, m, h]


def force_kernel(tiles, groups, scaled, atomic, mass, label_ref, hot, forces_out):
    spread = gather_rows(scaled[...], label_ref[...], hot[...], groups)
    for d in range(3):
        added = mass[...] * spread[d]
        for t in range(tiles):
            row = slice(d * tiles + t, d * tiles + t + 1)
            forces_out[row, :] = atomic[row, :] + added[:, t * LANES : (t + 1) * LANES]


def record_kernel(tiles, groups, entries, sources, *refs):
    lists_ref, own, mass_sum_ref, atomic, label_ref, leave_ref, hot = refs[:7]
    cells = refs[7 : 7 + sources]
    rest = refs[7 + sources :]
    scaled_out, record_out, leave_hot, raw, far, near, nearest = rest[:7]
    buffers, (total, coarse) = rest[7:9], rest[9:]
    lists, listed = lists_ref[...], lists_ref.shape[1]
    height = 4 * (tiles + groups)
    signs = signs_here()
    every = len(entries) * groups
    for source, cell, steps in entries:
        step = [steps[k] * signs[k] if steps[k] else 0 for k in range(3)]
        column = column_of(step)
        base = cell * height + 4 * tiles
        for k in range(4):
            block = cells[source][base + k * groups : base + (k + 1) * groups, :]
            if k < 3:
                block = block + (as_float(step[k]) - 0.5)
            raw[k, pl.ds(column * groups, groups), :] = block
    scale = math.sqrt(math.log2(math.e) / SIGMA_SQ)
    coords = [raw[k] for k in range(3)]
    one, zero = jnp.ones_like(coords[0]), jnp.zeros_like(coords[0])
    plain = coords + weight_rows(raw[3])[0] + [one, zero]
    for r, row in enumerate(far_rows([scale * v for v in coords], 0.0) + plain):
        far[r * every : (r + 1) * every, :] = row
    base = 4 * tiles
    coords = [own[base + k * groups : base + (k + 1) * groups, :] - 0.5 for k in range(3)]
    own_weight = own[base + 3 * groups : base + 4 * groups, :]
    zero = jnp.zeros_like(own_weight)
    factors = [-EPS_COARSE * row for row in weight_rows(own_weight)[1]]
    factors += [zero + EPS_COARSE, zero] + [zero] * 8
    for r, row in enumerate(near_rows([scale * v for v in coords], -1.0) + factors):
        near[r * groups : (r + 1) * groups, :] = row
    for b in range(groups):
        nearest[b] = near[pl.ds(b, ROWS + 16, stride=groups), :].T.astype(BF16)

    def products(b, into):
        lhs = nearest[b]
        for e in range(0, listed, 2):
            members = [lists[b, m] for m in range(e, min(e + 2, listed))]
            rhs = jnp.concatenate([picked_rows(far, k, every) for k in members], axis=1)
            dist = jnp.dot(lhs[:, :ROWS], rhs, preferred_element_type=F32)
            rhs = [far[pl.ds(k + 19 * every, 8, stride=every), :] for k in members]
            rhs = jnp.concatenate([jnp.concatenate([r, r], axis=0) for r in rhs], axis=1)
            factor = jnp.dot(lhs[:, ROWS:], rhs.astype(BF16), preferred_element_type=F32)
            into[:, e * LANES : (e + len(members)) * LANES] = jnp.exp2(dist) * factor

    def strengths(b, held):
        block = LANES // PARTS
        for part in range(PARTS):
            at = slice(part * block, (part + 1) * block)
            acc = [jnp.zeros((block, LANES), F32)] * 4
            for e in range(listed):
                k = lists[b, e]
                s = held[at, e * LANES : (e + 1) * LANES]
                acc[3] = acc[3] + s
                for d in range(3):
                    acc[d] = acc[d] + s * far[pl.ds((16 + d) * every + k, 1), :]
            for d in range(4):
                total[d, at, :] = acc[d]
        sums = [jnp.sum(total[d].T, axis=0, keepdims=True) for d in range(4)]
        for d in range(3):
            centre = own[base + d * groups + b : base + d * groups + b + 1, :] - 0.5
            coarse[d * groups + b : d * groups + b + 1, :] = centre * sums[3] - sums[d]

    products(0, buffers[0])
    for b in range(groups):
        if b + 1 < groups:
            products(b + 1, buffers[(b + 1) % 2])
        strengths(b, buffers[b % 2])

    mass_sum = mass_sum_ref[...]
    flat = [flat_row(atomic, d * tiles, tiles) for d in range(3)]
    summed = sum_rows(flat, label_ref[...], hot[...], groups)
    scaled_out[...] = coarse[...] / jnp.concatenate([mass_sum] * 3, axis=0)
    molecule = summed + coarse[...]
    table = jnp.concatenate(
        [own[base : base + 3 * groups, :], molecule, own_weight, mass_sum], axis=0
    )
    leavers = leave_ref.shape[1] // 2
    one_hot(leave_ref, leave_hot, leave_ref.shape[1] // LANES)
    picked = gather_rows(table, leave_ref[...], leave_hot[...], groups)
    for side, shift in ((0, -1.0), (1, 1.0)):
        for f in range(8):
            row = picked[f][:, side * leavers : (side + 1) * leavers]
            record_out[side, f : f + 1, :] = row + shift if f == 0 else row


def moves(axis):
    n = lax.axis_size(axis)
    if n <= 2:
        return [([n - 1 - i for i in range(n)], (1, -1))]
    if n % 2 == 0:
        inner = [i ^ 1 for i in range(n)]
        return [([(((i + 1) ^ 1) - 1) % n for i in range(n)], (-1,)), (inner, (1,))]
    return [([(i + 1) % n for i in range(n)], (-1,)), ([(i - 1) % n for i in range(n)], (1,))]


def exchange(x, axis):
    return [
        (lax.ppermute(x, axis, list(enumerate(receivers))), steps)
        for receivers, steps in moves(axis)
    ]


def exchange_plane(x, first, second):
    sizes = lax.axis_size(first), lax.axis_size(second)
    still = [(list(range(n)), (0,)) for n in sizes]
    blocks = []
    for to_b, steps_b in moves(second) + [still[1]]:
        for to_a, steps_a in [still[0]] + moves(first):
            steps = [(p, q) for p in steps_a for q in steps_b]
            if steps == [(0, 0)]:
                continue
            pairs = [
                (a * sizes[1] + b, to_a[a] * sizes[1] + to_b[b])
                for a in range(sizes[0])
                for b in range(sizes[1])
            ]
            blocks.append((lax.ppermute(x, (first, second), pairs), steps))
    return blocks


def sign_of(axis):
    n = lax.axis_size(axis)
    if n > 2 and n % 2 == 0:
        return 1 - 2 * lax.rem(lax.axis_index(axis), 2)
    return jnp.int32(1)


def per_device(positions, charges, masses, weights, mapping, atom_lists, bead_lists, leaving):
    atoms, beads = positions.shape[4], weights.shape[3]
    tiles, groups = atoms // LANES, beads // LANES
    pos = positions.reshape(3 * tiles, LANES)
    charge, mass = charges[0, 0], masses[0, 0]
    weight, label = weights[0, 0], mapping[0, 0]
    leavers = leaving.shape[4]
    height = 4 * (tiles + groups)
    limit = pltpu.CompilerParams(vmem_limit_bytes=48 * 2**20)
    inputs = [
        label, mass, pos, weight, charge,
        atom_lists[0, 0, 0], bead_lists[0, 0, 0], leaving.reshape(1, 2 * leavers),
    ]

    def like(x):
        return jax.ShapeDtypeStruct(x.shape, x.dtype)

    own, mass_sum, hot, label, mass, lists, *small = pl.pallas_call(
        prepare_kernel,
        out_shape=(
            jax.ShapeDtypeStruct((height, LANES), F32),
            jax.ShapeDtypeStruct((groups, LANES), F32),
            jax.ShapeDtypeStruct((LANES, atoms), BF16),
            like(label),
            like(mass),
            *[like(x) for x in inputs[5:]],
        ),
        in_specs=[HBM] * 8,
        out_specs=(VMEM,) * 8,
        scratch_shapes=[
            *[pltpu.VMEM(x.shape, x.dtype) for x in inputs[2:5]],
            pltpu.SemaphoreType.DMA((8,)),
        ],
        compiler_params=pltpu.CompilerParams(vmem_limit_bytes=48 * 2**20),
    )(*[pltpu.with_memory_space_constraint(x, pltpu.HBM) for x in inputs])

    def pairs(lists, near, entries, cells, before, last=False):
        count = len(entries)
        first = before is None
        args = [lists, own, *cells] if first else [lists, own, near, *cells, before]
        place = len(args) - 1
        words = jax.ShapeDtypeStruct((tiles, 3 * -(-9 // number_plan(tiles)[1])), jnp.int32)
        points = jax.ShapeDtypeStruct((tiles, LANES, ROWS), BF16)
        extra = [words, points] if first else []
        shape = (3 * tiles, LANES) if last else (tiles, 4, LANES, LANES)
        work = tiles * count * LANES * LANES
        return pl.pallas_call(
            functools.partial(
                pair_kernel, tiles, groups, entries, len(cells), before is None, last
            ),
            out_shape=(jax.ShapeDtypeStruct(shape, F32), *extra),
            in_specs=[VMEM] * len(args),
            out_specs=(VMEM,) * (1 + len(extra)),
            scratch_shapes=[
                pltpu.VMEM((count, 20 * tiles, LANES), F32),
                pltpu.VMEM((pair_plan(tiles, count)[0], LANES, count * LANES), F32),
            ]
            + ([pltpu.VMEM((4, LANES, LANES), F32)] if last else [])
            + ([pltpu.VMEM((ROWS * tiles, LANES), F32)] if first else []),
            input_output_aliases={} if last or before is None else {place: 0},
            compiler_params=limit,
            cost_estimate=pl.CostEstimate(
                flops=60 * work, bytes_accessed=4 * height * LANES, transcendentals=work
            ),
        )(*args)

    with_x = exchange(own, "gx")
    force, lists, near = pairs(lists, None, [(0, 0, (0, 0, 0))], [own], None)
    column = jnp.concatenate([own] + [block for block, _ in with_x], axis=0)
    column, force = lax.optimization_barrier((column, force))
    cells = [(0, 0)] + [(c + 1, x) for c, (_, steps) in enumerate(with_x) for x in steps]
    with_y = exchange(column, "gy")[::-1]
    entries = [(0, c, (x, 0, 0)) for c, x in cells[1:]]
    force = pairs(lists, near, entries, [column], force)[0]
    near_y, far_y = with_y[:1], with_y[1:]
    if far_y:
        entries = [(0, c, (x, y, 0)) for y in near_y[0][1] for c, x in cells]
        force = pairs(lists, near, entries, [near_y[0][0]], force)[0]
    plane = jnp.concatenate([column] + [block for block, _ in with_y], axis=0)
    plane, force = lax.optimization_barrier((plane, force))
    held = 1 + len(with_x)
    plane_cells = [(c, (x, 0)) for c, x in cells]
    plane_cells += [
        (held * (k + 1) + c, (x, y))
        for k, (_, steps) in enumerate(with_y)
        for y in steps
        for c, x in cells
    ]
    with_z = [(block, z) for block, steps in exchange(plane, "gz") for z in steps][::-1]
    left = far_y[0][1] if far_y else near_y[0][1]
    entries = [(0, c, (x, y, 0)) for c, (x, y) in plane_cells if y in left]
    force = pairs(lists, near, entries, [plane], force)[0]
    for place, (block, z) in enumerate(with_z):
        entries = [(0, c, (x, y, z)) for c, (x, y) in plane_cells]
        force = pairs(lists, near, entries, [block], force, place == 1)[0]

    sources = [plane] + [block for block, _ in with_z]
    z_steps = [0] + [step for _, step in with_z]
    entries = [(s, c, (x, y, z_steps[s])) for s in range(3) for c, (x, y) in plane_cells]
    every, listed = len(entries) * groups, small[0].shape[1]
    scaled, record = pl.pallas_call(
        functools.partial(record_kernel, tiles, groups, entries, len(sources)),
        out_shape=(
            jax.ShapeDtypeStruct((3 * groups, LANES), F32),
            jax.ShapeDtypeStruct((2, 8, leavers), F32),
        ),
        in_specs=[VMEM] * (7 + len(sources)),
        out_specs=(VMEM, VMEM),
        scratch_shapes=[
            pltpu.VMEM((LANES, 2 * leavers), BF16),
            pltpu.VMEM((4, every, LANES), F32),
            pltpu.VMEM((27 * every, LANES), F32),
            pltpu.VMEM(((ROWS + 16) * groups, LANES), F32),
            pltpu.VMEM((groups, LANES, ROWS + 16), BF16),
            *[pltpu.VMEM((LANES, listed * LANES), F32)] * 2,
            pltpu.VMEM((4, LANES, LANES), F32),
            pltpu.VMEM((3 * groups, LANES), F32),
        ],
        compiler_params=limit,
    )(small[0], own, mass_sum, force, label, small[1], hot, *sources)
    forces = pl.pallas_call(
        functools.partial(force_kernel, tiles, groups),
        out_shape=jax.ShapeDtypeStruct((3 * tiles, LANES), F32),
        in_specs=[VMEM] * 5,
        out_specs=VMEM,
        compiler_params=limit,
    )(scaled, force, mass, label, hot)
    n = lax.axis_size("gx")
    if n == 2:
        arrivals = lax.ppermute(record, "gx", [(0, 1), (1, 0)])
    else:
        up = [(i, (i + 1) % n) for i in range(n)]
        down = [(j, i) for i, j in up]
        arrivals = jnp.stack(
            [lax.ppermute(record[0], "gx", up), lax.ppermute(record[1], "gx", down)]
        )
    return (forces.reshape(1, 1, 1, 3, atoms), arrivals[None, None, None])


def solution(mesh):
    cell = ("gx", "gy", "gz")
    placed = (
        P(*cell, None, None),
        P(*cell, None),
        P(*cell, None),
        P(*cell, None),
        P(*cell, None),
        P(*cell, None, None),
        P(*cell, None, None),
        P(*cell, None, None),
    )
    return jax.shard_map(
        per_device,
        mesh=mesh,
        in_specs=placed,
        out_specs=(P(*cell, None, None), P(*cell, None, None, None)),
        check_vma=False,
    )
```
